512 devices in a mesh: ctx: 64 (over y, z), ch: 8 (over x, core).
Axes of the slice: x: 4, y: 8, z: 8, core: 2. Of those that a mesh axis runs over, the one named last changes fastest.
Arguments:
- inputs: bfloat16 [3, 1024, 16384], P(None, 'ch', 'ctx'), may hold values from -6 to 6
- short_weight: float32 [3, 1024, 7], P(None, 'ch'), may hold values from -2 to 2
- skip: float32 [1024], P('ch'), may hold values from -1 to 1
- filters: float32 [64, 16384], P('ch', 'ctx'), may hold values from -6 to 6
- cotangent: float32 [1024, 16384], P('ch', 'ctx'), may hold values from -6 to 6
Outputs:
- output: float32 [1024, 16384], P('ch', 'ctx')
- grad_inputs: float32 [3, 1024, 16384], P(None, 'ch', 'ctx')
- grad_filters: float32 [64, 16384], P('ch', 'ctx')
The draws below stay inside these ranges and needn't reach their ends.
All inputs are finite; a program needn't handle non-finite values.
Results may differ from the reference program's by a relative error of at most 0.00045.
Values may be sent and summed in bfloat16 or wider, within the bound.
No kernel may reach another device: no remote copies, remote signals or barrier semaphores. Data moves between devices by JAX's collectives and lax.ppermute only.
A program may use at most 64 MiB of HBM per device.

```python
import math
import jax
import jax.numpy as jnp
from jax import lax

TAPS = 7
SEQ = 16384
CH = 1024
G = 64


def block_scale(own_key, shape, shards, low, top_value):
    def one(dim, parts):
        heights = jax.random.uniform(jax.random.fold_in(jax.random.fold_in(own_key, 6), dim), (parts,), jnp.float32, low / len(shards), top_value / len(shards))
        return jnp.repeat(jnp.exp(heights), shape[dim] // parts).reshape((-1,) + (1,) * (len(shape) - dim - 1))

    level = one(*shards[0])
    for cut in shards[1:]:
        level = level * one(*cut)
    return level


def centred(stream_key, dims, width, bound, cuts=(), held_as=jnp.bfloat16):
    result = jax.random.normal(stream_key, dims, jnp.float32) * width
    if len(cuts) > 0:
        result = block_scale(stream_key, dims, cuts, -0.22, 0.18) * result
    return jnp.clip(result, min=-bound, max=bound).astype(held_as)


def setup_inputs(seed: int = 0) -> dict:
    arg_keys = jax.random.split(jax.random.key(seed), 6)
    inputs = centred(arg_keys[0], (3, CH, SEQ), 1.0, 6.0, ((1, 8), (2, 64)))
    short_weight = centred(arg_keys[1], (3, CH, TAPS), TAPS ** -0.5, 2.0, ((1, 8),), jnp.float32)
    skip = jnp.clip(jax.random.uniform(arg_keys[2], (CH,), jnp.float32, -1.0, 1.0) * block_scale(arg_keys[2], (CH,), ((0, 8),), -0.4, 0.0), -1.0, 1.0)
    filters = centred(arg_keys[3], (G, SEQ), 1.0, 6.0, ((0, 8), (1, 64)), jnp.float32)
    cotangent = centred(arg_keys[4], (CH, SEQ), 1.0, 6.0, ((0, 8), (1, 64)), jnp.float32)
    return {"inputs": inputs, "short_weight": short_weight, "skip": skip, "filters": filters, "cotangent": cotangent}


def conv_forward(values, weights):
    padded = jnp.pad(values, ((0, 0), (0, 0), (TAPS - 1, 0)))
    summed = jnp.zeros(values.shape, jnp.float32)
    for offset in range(TAPS):
        summed = summed + weights[:, :, offset:offset + 1] * padded[:, :, TAPS - 1 - offset:TAPS - 1 - offset + SEQ]
    return summed

def conv_backward(grads, weights):
    padded = jnp.pad(grads, ((0, 0), (0, 0), (0, TAPS - 1)))
    summed = jnp.zeros(grads.shape, jnp.float32)
    for offset in range(TAPS):
        summed = summed + weights[:, :, offset:offset + 1] * padded[:, :, offset:offset + SEQ]
    return summed

def reference(inputs, short_weight, skip, filters, cotangent):
    values = inputs.astype(jnp.float32)
    featured = conv_forward(values, short_weight)
    query_feat = featured[0]
    key_feat = featured[1]
    value_feat = featured[2]
    product = key_feat * value_feat
    transform_len = 2 * SEQ
    filter_scale = 1.0 / math.sqrt(SEQ)
    filter_spec = jnp.fft.fft(filters * filter_scale, n=transform_len, axis=-1)
    repeats = CH // G

    def block_step(running, pieces):
        prod_block, query_block, cot_block, skip_block = pieces
        spectrum = jnp.fft.fft(prod_block, n=transform_len, axis=-1)
        long_out = jnp.real(jnp.fft.ifft(spectrum * filter_spec, axis=-1))[:, :SEQ]
        mixer = long_out + skip_block[:, None] * prod_block
        out_block = query_block * mixer
        grad_mixer = cot_block * query_block
        grad_query = cot_block * mixer
        grad_spec = jnp.fft.fft(grad_mixer, n=transform_len, axis=-1)
        grad_long = jnp.real(jnp.fft.ifft(jnp.conj(filter_spec) * grad_spec, axis=-1))[:, :SEQ]
        grad_product = grad_long + skip_block[:, None] * grad_mixer
        return (running + jnp.conj(spectrum) * grad_spec, (out_block, grad_query, grad_product))
    pieces = (product.reshape(repeats, G, SEQ), query_feat.reshape(repeats, G, SEQ), cotangent.reshape(repeats, G, SEQ), skip.reshape(repeats, G))
    running, stacked = lax.scan(block_step, jnp.zeros_like(filter_spec), pieces)
    output = stacked[0].reshape(CH, SEQ)
    grad_query = stacked[1].reshape(CH, SEQ)
    grad_product = stacked[2].reshape(CH, SEQ)
    grad_filters = jnp.real(jnp.fft.ifft(running, axis=-1))[:, :SEQ] * filter_scale
    grad_featured = jnp.stack([grad_query, grad_product * value_feat, grad_product * key_feat])
    grad_inputs = conv_backward(grad_featured, short_weight)
    return (output, grad_inputs, grad_filters)
```

```python
import functools
import math

import jax
import jax.numpy as jnp
import ml_dtypes
import numpy as np
from jax import lax
from jax.experimental import pallas as pl
from jax.experimental.pallas import tpu as pltpu
from jax.sharding import PartitionSpec as P

BF16 = jnp.bfloat16
F32 = jnp.float32
LANES = 128
ROWS = 24
IN_COT, IN_COT_REST, IN_FILT, IN_FILT_REST = 12, 16, 20, 22
OUT_LONG, OUT_GRAD, OUT_FILT, OUT_RIM, OUT_REST = 0, 4, 8, 10, 12


def halves(array):
    array = np.asarray(array, np.float32)
    high = array.astype(ml_dtypes.bfloat16)
    low = (array - high.astype(np.float32)).astype(ml_dtypes.bfloat16)
    return high, low


@functools.lru_cache(maxsize=None)
def tables(pieces, length, scale):
    blocks = 2 * pieces
    total = blocks * length
    freq = np.arange(blocks)[:, None]
    angle = 2.0 * np.pi * ((freq * np.arange(pieces)[None, :]) % blocks) / blocks
    cos, sin = np.cos(angle), np.sin(angle)
    outer = np.block([[cos, sin], [-sin, cos]])
    back = np.block([[cos.T, sin.T], [sin.T, -cos.T]]) * (scale / total)
    angle = 2.0 * np.pi * ((freq * np.arange(length)[None, :]) % total) / total
    twiddle = np.stack([np.cos(angle), -np.sin(angle)]).astype(np.float32)
    count = np.arange(length)
    angle = 2.0 * np.pi * ((count[:, None] * count[None, :]) % length) / length
    cos, sin = np.cos(angle), np.sin(angle)
    inner = np.block([[cos, -sin], [sin, cos]])
    return (*halves(outer), *halves(back), twiddle, *halves(inner))


def split(value):
    high = value.astype(BF16)
    return high, (value - high.astype(F32)).astype(BF16)


def product3(left, right):
    def dot(a, b):
        return jnp.dot(a, b, preferred_element_type=F32)

    return dot(left[0], right[0]) + (dot(left[1], right[0]) + dot(left[0], right[1]))


def put(scratch, row, value):
    scratch[pl.ds(row, value.shape[0], stride=ROWS), :] = value


def put_block(scratch, row, value):
    for half in range(value.shape[1] // LANES):
        put(scratch, row + half, value[:, half * LANES : (half + 1) * LANES])


def put_split(scratch, row, rest, value):
    high = value.astype(BF16).astype(F32)
    put_block(scratch, row, high)
    put_block(scratch, rest, value - high)


def pack_kernel(x_ref, cot_ref, filt_ref, out_ref, scratch):
    pieces = filt_ref.shape[0]
    for stream in range(3):
        for side in range(2):
            block = x_ref[stream, side * pieces : (side + 1) * pieces, :].astype(F32)
            put_block(scratch, (stream * 2 + side) * 2, block)
    for side in range(2):
        block = cot_ref[side * pieces : (side + 1) * pieces, :]
        put_split(scratch, IN_COT + 2 * side, IN_COT_REST + 2 * side, block)
    put_split(scratch, IN_FILT, IN_FILT_REST, filt_ref[...])
    out_ref[...] = scratch[...].astype(BF16)


def conv_kernel(
    r_ref,
    w_ref,
    outer_hi,
    outer_lo,
    back_hi,
    back_lo,
    twiddle,
    inner_hi,
    inner_lo,
    out_ref,
    scratch,
):
    pieces = r_ref.shape[0] // ROWS
    taps = 7
    scratch[...] = r_ref[...].astype(F32)

    def row(index):
        return scratch[pl.ds(index, pieces, stride=ROWS), :]

    def block(index):
        return jnp.concatenate([row(index), row(index + 1)], axis=1)

    row_number = lax.broadcasted_iota(jnp.int32, (pieces, LANES), 0)
    lane_number = lax.broadcasted_iota(jnp.int32, (pieces, LANES), 1)
    rim = jnp.zeros((pieces, LANES), F32)
    featured = []
    for stream in range(3):
        for side in range(2):
            place = stream * 2 + side
            signal = block(place * 2)
            before = jnp.where(row_number == 0, 0.0, pltpu.roll(signal[:, LANES:], 1, 0))
            moved = pltpu.roll(before, (16 * place + 6) % LANES, 1)
            inside = (lane_number >= 16 * place) & (lane_number < 16 * place + taps - 1)
            rim = jnp.where(inside, moved, rim)
            extended = jnp.concatenate([before, signal], axis=1)
            total = w_ref[place * taps] * signal
            for offset in range(1, taps):
                shifted = pltpu.roll(extended, offset, 1)[:, LANES:]
                total = total + w_ref[place * taps + offset] * shifted
            featured.append(total)
    query, key, value = featured[0:2], featured[2:4], featured[4:6]
    cot = [block(IN_COT + 2 * side) + block(IN_COT_REST + 2 * side) for side in range(2)]
    prod = [key[side] * value[side] for side in range(2)]
    mixed = [cot[side] * query[side] for side in range(2)]
    filt = block(IN_FILT) + block(IN_FILT_REST)
    length = filt.shape[1]

    outer = (outer_hi[...], outer_lo[...])
    inner = (inner_hi[...], inner_lo[...])
    back = (back_hi[...], back_lo[...])
    turn_re, turn_im = twiddle[0], twiddle[1]
    count = 2 * pieces

    signals = jnp.concatenate(
        [jnp.concatenate(prod, axis=0), jnp.concatenate(mixed, axis=0)], axis=1
    )
    spread = product3(outer, split(signals))
    spread_f = product3((outer[0][:, :pieces], outer[1][:, :pieces]), split(filt))

    def turned(re, im):
        return jnp.concatenate([re * turn_re - im * turn_im, re * turn_im + im * turn_re], axis=1)

    parts = [spread[:, :length], spread[:, length:], spread_f]
    stacked = jnp.concatenate([turned(part[:count], part[count:]) for part in parts], axis=0)
    spectra = product3(split(stacked), inner)
    z_re, z_im = spectra[:count, :length], spectra[:count, length:]
    m_re, m_im = spectra[count : 2 * count, :length], spectra[count : 2 * count, length:]
    f_re, f_im = spectra[2 * count :, :length], spectra[2 * count :, length:]
    long_re, long_im = z_re * f_re - z_im * f_im, -(z_re * f_im + z_im * f_re)
    grad_re, grad_im = m_re * f_re + m_im * f_im, m_re * f_im - m_im * f_re
    tail_re, tail_im = z_re * m_re + z_im * m_im, z_im * m_re - z_re * m_im
    stacked = jnp.concatenate(
        [
            jnp.concatenate([long_re, long_im], axis=1),
            jnp.concatenate([grad_re, grad_im], axis=1),
            jnp.concatenate([tail_re, tail_im], axis=1),
        ],
        axis=0,
    )
    inside = product3(split(stacked), inner)

    def upright(start):
        re, im = inside[start : start + count, :length], inside[start : start + count, length:]
        return jnp.concatenate([re * turn_re - im * turn_im, re * turn_im + im * turn_re], axis=0)

    columns = jnp.concatenate([upright(0), upright(count), upright(2 * count)], axis=1)
    restored = product3(back, split(columns))

    put_split(scratch, OUT_FILT, OUT_FILT + OUT_REST, restored[:pieces, 2 * length :])
    for side in range(2):
        rows = slice(side * pieces, (side + 1) * pieces)
        long_out = restored[rows, :length]
        grad_long = restored[rows, length : 2 * length]
        put_split(scratch, OUT_LONG + 2 * side, OUT_LONG + OUT_REST + 2 * side, long_out)
        put_split(scratch, OUT_GRAD + 2 * side, OUT_GRAD + OUT_REST + 2 * side, grad_long)
        skip = w_ref[6 * taps + side]
        first = slice(0, LANES)
        grad_query = cot[side][:, first] * (long_out[:, first] + skip * prod[side][:, first])
        grad_product = grad_long[:, first] + skip * mixed[side][:, first]
        grads = (
            grad_query,
            grad_product * value[side][:, first],
            grad_product * key[side][:, first],
        )
        for stream in range(3):
            place = stream * 2 + side
            after = pltpu.roll(grads[stream], pieces - 1, 0)
            after = jnp.where(row_number == pieces - 1, 0.0, after)
            moved = pltpu.roll(after, 16 * place + 8, 1)
            inside_rim = (lane_number >= 16 * place + 8) & (lane_number < 16 * place + 8 + taps - 1)
            rim = jnp.where(inside_rim, moved, rim)
    high = rim.astype(BF16).astype(F32)
    put(scratch, OUT_RIM, high)
    put(scratch, OUT_RIM + OUT_REST, rim - high)
    put(scratch, OUT_RIM + 1, jnp.zeros_like(rim))
    put(scratch, OUT_RIM + 1 + OUT_REST, jnp.zeros_like(rim))
    out_ref[...] = scratch[...].astype(BF16)


def local_kernel(r_ref, x_ref, w_ref, skip_ref, cot_ref, out_ref, grad_ref, scratch):
    pieces = r_ref.shape[0] // ROWS
    taps = w_ref.shape[2]
    length = x_ref.shape[2]
    scratch[...] = r_ref[...].astype(F32)

    def row(index):
        first = scratch[pl.ds(index, pieces, stride=ROWS), :]
        return first + scratch[pl.ds(index + OUT_REST, pieces, stride=ROWS), :]

    def block(index):
        return jnp.concatenate([row(index), row(index + 1)], axis=1)

    rim = row(OUT_RIM)
    for side in range(2):
        rows = slice(side * pieces, (side + 1) * pieces)
        weights = [w_ref[stream, rows, :] for stream in range(3)]
        featured = []
        for stream in range(3):
            place = stream * 2 + side
            signal = x_ref[stream, rows, :].astype(F32)
            before = pltpu.roll(rim, LANES - taps + 1 - 16 * place, 1)
            extended = jnp.concatenate([before, signal], axis=1)
            total = weights[stream][:, 0:1] * signal
            for offset in range(1, taps):
                shifted = pltpu.roll(extended, offset, 1)[:, LANES:]
                total = total + weights[stream][:, offset : offset + 1] * shifted
            featured.append(total)
        query, key, value = featured
        cot = cot_ref[rows, :]
        skip = skip_ref[rows, :]
        prod = key * value
        mixer = block(OUT_LONG + 2 * side) + skip * prod
        out_ref[rows, :] = query * mixer
        grad_product = block(OUT_GRAD + 2 * side) + skip * (cot * query)
        grads = (cot * mixer, grad_product * value, grad_product * key)
        for stream in range(3):
            place = stream * 2 + side
            after = pltpu.roll(rim, LANES - 16 * place - 8, 1)
            extended = jnp.concatenate([grads[stream], after], axis=1)
            total = weights[stream][:, 0:1] * grads[stream]
            for offset in range(1, taps):
                shifted = pltpu.roll(extended, length + LANES - offset, 1)[:, :length]
                total = total + weights[stream][:, offset : offset + 1] * shifted
            grad_ref[stream, rows, :] = total


def call(kernel, out_shape, operands, scratch, smem=(), flops=0):
    specs = [
        pl.BlockSpec(memory_space=pltpu.SMEM if place in smem else pltpu.VMEM)
        for place in range(len(operands))
    ]
    outs = jax.tree.map(lambda _: pl.BlockSpec(memory_space=pltpu.VMEM), out_shape)
    return pl.pallas_call(
        kernel,
        out_shape=out_shape,
        in_specs=specs,
        out_specs=outs,
        scratch_shapes=scratch,
        compiler_params=pltpu.CompilerParams(vmem_limit_bytes=24 * 1024 * 1024),
        cost_estimate=pl.CostEstimate(flops=flops, bytes_accessed=1 << 21, transcendentals=0),
    )(*operands)


def shards(inputs, short_weight, skip, filters, cotangent):
    pieces = lax.axis_size("ctx")
    owners = lax.axis_size("ch")
    position = lax.axis_index("ctx")
    _, channels, length = inputs.shape
    taps = short_weight.shape[2]
    owned = filters.shape[0]
    scale = 1.0 / math.sqrt(pieces * length)
    packed = jax.ShapeDtypeStruct((pieces * ROWS, LANES), BF16)
    room = [pltpu.VMEM((pieces * ROWS, LANES), F32)]

    def transposed(array):
        array = lax.all_to_all(array.reshape(pieces, ROWS, LANES), "ctx", 0, 0)
        return array.reshape(pieces * ROWS, LANES)

    copies = jnp.broadcast_to(filters[None], (owners, owned, length))
    every = lax.all_to_all(copies, "ch", 0, 0).reshape(pieces, length)
    sent = call(pack_kernel, packed, (inputs, cotangent, every), room)
    received = transposed(sent)

    own = lax.dynamic_slice_in_dim(short_weight.reshape(3, 2, pieces, taps), position, 1, 2)
    own_skip = lax.dynamic_slice_in_dim(skip.reshape(2, pieces), position, 1, 1)
    scalars = jnp.concatenate([own.reshape(-1), own_skip.reshape(-1)])
    constants = [jnp.asarray(table) for table in tables(pieces, length, scale)]
    sent = call(
        conv_kernel, packed, (received, scalars, *constants), room, smem=(1,), flops=1500000000
    )
    received = transposed(sent)

    lines = received.reshape(pieces, ROWS, LANES)
    rounded = lines[:, OUT_FILT : OUT_FILT + 2].astype(F32)
    rest = lines[:, OUT_FILT + OUT_REST : OUT_FILT + OUT_REST + 2].astype(F32)
    partial = (rounded + rest).reshape(owners, owned, length)
    terms = lax.all_to_all(partial, "ch", 0, 0)
    output, grad_inputs = call(
        local_kernel,
        (
            jax.ShapeDtypeStruct((channels, length), F32),
            jax.ShapeDtypeStruct((3, channels, length), F32),
        ),
        (received, inputs, short_weight, skip[:, None], cotangent),
        room,
    )
    grad_filters = terms.sum(axis=0)
    return (output, grad_inputs, grad_filters)


def solution(mesh):
    in_specs = (P(None, "ch", "ctx"), P(None, "ch", None), P("ch"), P("ch", "ctx"), P("ch", "ctx"))
    out_specs = (P("ch", "ctx"), P(None, "ch", "ctx"), P("ch", "ctx"))
    return jax.shard_map(shards, mesh=mesh, in_specs=in_specs, out_specs=out_specs, check_vma=False)
```

```python
import functools
import math

import jax
import jax.numpy as jnp
import ml_dtypes
import numpy as np
from jax import lax
from jax.experimental import pallas as pl
from jax.experimental.pallas import tpu as pltpu
from jax.sharding import PartitionSpec as P

BF16 = jnp.bfloat16
F32 = jnp.float32
LANES = 128
TAPS = 7
IN_COT, IN_FILT, IN_TOPS, IN_ROWS = 12, 16, 18, 20
CROSS_FILT, CROSS_GRAD, CROSS_TOPS, CROSS_ROWS = 0, 2, 4, 5
OUT_LONG, OUT_GRAD, OUT_FILT, OUT_RIM, OUT_HEAD, OUT_ROWS = 0, 4, 8, 10, 11, 12
RIM = TAPS - 1
TOP_LANE = 12 * RIM
REACH = 125.0


def halves(array):
    array = np.asarray(array, np.float32)
    high = array.astype(ml_dtypes.bfloat16)
    low = (array - high.astype(np.float32)).astype(ml_dtypes.bfloat16)
    return high, low


@functools.lru_cache(maxsize=None)
def tables(pieces, length, scale):
    blocks = 2 * pieces
    total = blocks * length
    freq = np.arange(blocks)[:, None]
    angle = 2.0 * np.pi * ((freq * np.arange(pieces)[None, :]) % blocks) / blocks
    cos, sin = np.cos(angle), np.sin(angle)
    outer = np.block([[cos, sin], [-sin, cos]])
    back = np.block([[cos.T, sin.T], [sin.T, -cos.T]]) * (scale / total)
    angle = 2.0 * np.pi * ((freq * np.arange(length)[None, :]) % total) / total
    twiddle = np.stack([np.cos(angle), -np.sin(angle)]).astype(np.float32)
    count = np.arange(length)
    angle = 2.0 * np.pi * ((count[:, None] * count[None, :]) % length) / length
    cos, sin = np.cos(angle), np.sin(angle)
    inner = np.block([[cos, -sin], [sin, cos]])
    return (*halves(outer), *halves(back), twiddle, *halves(inner))


def split(value):
    high = value.astype(BF16)
    return high, (value - high.astype(F32)).astype(BF16)


def product3(left, right):
    def dot(a, b):
        return jnp.dot(a, b, preferred_element_type=F32)

    return dot(left[0], right[0]) + (dot(left[1], right[0]) + dot(left[0], right[1]))


def encoded(value):
    top = jnp.max(jnp.abs(value), axis=1, keepdims=True)
    top = (jnp.maximum(top, 1e-30) * 1.008).astype(BF16).astype(F32)
    size = jnp.sqrt(jnp.abs(value) * (1.0 / top))
    code = jnp.exp2(size * (2.0 * REACH) - REACH)
    return jnp.where(value < 0.0, -code, code), top


def decoded(code, top):
    size = (jnp.log2(jnp.abs(code)) + REACH) * (0.5 / REACH)
    value = size * size * top
    return jnp.where(code < 0.0, -value, value)


class Lines:
    def __init__(self, ref, rows):
        self.ref, self.rows = ref, rows
        self.count = ref.shape[0] // rows

    def get(self, row):
        return self.ref[pl.ds(row, self.count, stride=self.rows), :]

    def put(self, row, value):
        self.ref[pl.ds(row, self.count, stride=self.rows), :] = value

    def get_block(self, row):
        return jnp.concatenate([self.get(row), self.get(row + 1)], axis=1)

    def put_block(self, row, value):
        self.put(row, value[:, :LANES])
        self.put(row + 1, value[:, LANES:])


def in_lanes(columns, first, like):
    lane = lax.broadcasted_iota(jnp.int32, like.shape, 1)
    for place, column in enumerate(columns):
        like = jnp.where(lane == first + place, column, like)
    return like


def exchanged(value, member, owners):
    size = value.shape[0] // owners
    step = 1
    while step < owners:
        order = [place ^ step for place in range(owners)]
        swapped = jnp.concatenate([value[k * size : (k + 1) * size] for k in order], axis=0)
        value = jnp.where((member & step) != 0, swapped, value)
        step *= 2
    return value


def pack_kernel(
    owners, member_ref, x_hbm, cot_hbm, filt_hbm, out_ref, scratch, x_ref, cot_ref, filt_ref, sems
):
    copies = [pltpu.make_async_copy(x_hbm.at[place], x_ref.at[place], sems.at[place]) for place in range(3)]
    copies.append(pltpu.make_async_copy(cot_hbm, cot_ref, sems.at[3]))
    copies.append(pltpu.make_async_copy(filt_hbm, filt_ref, sems.at[4]))
    for copy in copies:
        copy.start()
    lines = Lines(scratch, IN_ROWS)
    pieces = lines.count
    member = member_ref[0]
    for stream in range(3):
        copies[stream].wait()
        for side in range(2):
            rows = slice(side * pieces, (side + 1) * pieces)
            block = x_ref[stream, rows, :].astype(F32)
            lines.put_block((stream * 2 + side) * 2, exchanged(block, member, owners))
    tops = []
    copies[3].wait()
    for side in range(2):
        block = exchanged(cot_ref[side * pieces : (side + 1) * pieces, :], member, owners)
        code, top = encoded(block)
        tops.append(top)
        lines.put_block(IN_COT + 2 * side, code)
    copies[4].wait()
    code, top = encoded(filt_ref[...])
    lines.put_block(IN_FILT, jnp.concatenate([code] * owners, axis=0))
    tops.append(jnp.concatenate([top] * owners, axis=0))
    blank = jnp.zeros((pieces, LANES), F32)
    lines.put(IN_TOPS, in_lanes(tops, 0, blank))
    lines.put(IN_TOPS + 1, blank)
    out_ref[...] = scratch[...].astype(BF16)


def turned(re, im, twiddle):
    turn_re, turn_im = twiddle[0], twiddle[1]
    return re * turn_re - im * turn_im, re * turn_im + im * turn_re


def upright(spectra, inner, twiddle, count):
    length = spectra.shape[1] // 2
    inside = product3(split(spectra), inner)
    columns = []
    for start in range(0, spectra.shape[0], count):
        rows = slice(start, start + count)
        pair = turned(inside[rows, :length], inside[rows, length:], twiddle)
        columns.append(jnp.concatenate(pair, axis=0))
    return jnp.concatenate(columns, axis=1)


def rim_lanes(value, place, rim):
    lane = lax.broadcasted_iota(jnp.int32, rim.shape, 1)
    high = value.astype(BF16).astype(F32)
    both = jnp.where(lane < RIM, high, pltpu.roll(value - high, RIM, 1))
    start = 2 * RIM * place
    moved = pltpu.roll(both, start, 1) if start else both
    return jnp.where((lane >= start) & (lane < start + 2 * RIM), moved, rim)


def forward_kernel(
    r_ref,
    w_ref,
    outer_hi,
    outer_lo,
    back_hi,
    back_lo,
    twiddle,
    inner_hi,
    inner_lo,
    cross_ref,
    spec_ref,
    kept_ref,
    scratch,
    cross_scratch,
):
    scratch[...] = r_ref[...].astype(F32)
    lines = Lines(scratch, IN_ROWS)
    cross = Lines(cross_scratch, CROSS_ROWS)
    pieces = lines.count
    count = 2 * pieces
    length = 2 * LANES
    tops = lines.get(IN_TOPS)
    row_number = lax.broadcasted_iota(jnp.int32, (pieces, LANES), 0)
    head = jnp.zeros((pieces, LANES), F32)
    featured = []
    for stream in range(3):
        for side in range(2):
            place = stream * 2 + side
            signal = lines.get_block(place * 2)
            before = jnp.where(row_number == 0, 0.0, pltpu.roll(signal[:, LANES:], 1, 0))
            extended = jnp.concatenate([before, signal], axis=1)
            total = w_ref[place * TAPS] * signal
            for offset in range(1, TAPS):
                shifted = pltpu.roll(extended, offset, 1)[:, LANES:]
                total = total + w_ref[place * TAPS + offset] * shifted
            featured.append(total)
            head = rim_lanes(total[:, :LANES], place, head)
    query, key, value = featured[0:2], featured[2:4], featured[4:6]
    cot = [
        decoded(lines.get_block(IN_COT + 2 * side), tops[:, side : side + 1]) for side in range(2)
    ]
    prod = [key[side] * value[side] for side in range(2)]
    mixed = [cot[side] * query[side] for side in range(2)]
    for side in range(2):
        for place, array in enumerate((prod, mixed, key, value, cot)):
            kept_ref[side * 5 + place] = array[side][:, :LANES]
    kept_ref[10] = head

    signals = jnp.concatenate(
        [jnp.concatenate(prod, axis=0), jnp.concatenate(mixed, axis=0)], axis=1
    )
    spread = product3((outer_hi[...], outer_lo[...]), split(signals))
    parts = []
    for start in (0, length):
        part = spread[:, start : start + length]
        parts.append(jnp.concatenate(turned(part[:count], part[count:], twiddle), axis=1))
    inner = (inner_hi[...], inner_lo[...])
    spectra = product3(split(jnp.concatenate(parts, axis=0)), inner)
    spec_ref[...] = spectra
    z_re, z_im = spectra[:count, :length], spectra[:count, length:]
    m_re, m_im = spectra[count:, :length], spectra[count:, length:]
    tail = jnp.concatenate([z_re * m_re + z_im * m_im, z_im * m_re - z_re * m_im], axis=1)
    columns = upright(tail, inner, twiddle, count)
    partial = product3((back_hi[:pieces, :], back_lo[:pieces, :]), split(columns))
    code, top = encoded(partial)
    cross.put_block(CROSS_GRAD, code)
    cross.put_block(CROSS_FILT, lines.get_block(IN_FILT))
    blank = jnp.zeros((pieces, LANES), F32)
    cross.put(CROSS_TOPS, in_lanes([tops[:, 2:3], top], 0, blank))
    cross_ref[...] = cross_scratch[...].astype(BF16)


def inverse_kernel(
    cross_ref,
    spec_ref,
    kept_ref,
    w_ref,
    outer_hi,
    outer_lo,
    back_hi,
    back_lo,
    twiddle,
    inner_hi,
    inner_lo,
    out_ref,
    cross_scratch,
    scratch,
):
    cross_scratch[...] = cross_ref[...].astype(F32)
    cross = Lines(cross_scratch, CROSS_ROWS)
    lines = Lines(scratch, OUT_ROWS)
    pieces = lines.count
    count = 2 * pieces
    length = 2 * LANES
    tops = cross.get(CROSS_TOPS)
    filt = decoded(cross.get_block(CROSS_FILT), tops[:, 0:1])
    inner = (inner_hi[...], inner_lo[...])
    spread = product3((outer_hi[:, :pieces], outer_lo[:, :pieces]), split(filt))
    stacked = jnp.concatenate(turned(spread[:count], spread[count:], twiddle), axis=1)
    spectra = product3(split(stacked), inner)
    f_re, f_im = spectra[:, :length], spectra[:, length:]
    z_re, z_im = spec_ref[:count, :length], spec_ref[:count, length:]
    m_re, m_im = spec_ref[count:, :length], spec_ref[count:, length:]
    long_pair = jnp.concatenate(
        [z_re * f_re - z_im * f_im, -(z_re * f_im + z_im * f_re)], axis=1
    )
    grad_pair = jnp.concatenate([m_re * f_re + m_im * f_im, m_re * f_im - m_im * f_re], axis=1)
    columns = upright(jnp.concatenate([long_pair, grad_pair], axis=0), inner, twiddle, count)
    restored = product3((back_hi[...], back_lo[...]), split(columns))
    row_number = lax.broadcasted_iota(jnp.int32, (pieces, LANES), 0)
    rim = jnp.zeros((pieces, LANES), F32)
    long_tops, grad_tops = [], []
    for side in range(2):
        rows = slice(side * pieces, (side + 1) * pieces)
        long_out = restored[rows, :length]
        grad_long = restored[rows, length:]
        code, top = encoded(long_out)
        lines.put_block(OUT_LONG + 2 * side, code)
        long_tops.append(top)
        code, top = encoded(grad_long)
        lines.put_block(OUT_GRAD + 2 * side, code)
        grad_tops.append(top)
        skip = w_ref[6 * TAPS + side]
        prod, mixed, key, value, cot = [kept_ref[side * 5 + place] for place in range(5)]
        grad_product = grad_long[:, :LANES] + skip * mixed
        grad_query = cot * (long_out[:, :LANES] + skip * prod)
        for stream, grad in enumerate((grad_query, grad_product * value, grad_product * key)):
            after = jnp.where(row_number == pieces - 1, 0.0, pltpu.roll(grad, pieces - 1, 0))
            rim = rim_lanes(after, stream * 2 + side, rim)
    lines.put_block(OUT_FILT, cross.get_block(CROSS_GRAD))
    lines.put(OUT_RIM, in_lanes([*long_tops, *grad_tops, tops[:, 1:2]], TOP_LANE, rim))
    lines.put(OUT_HEAD, kept_ref[10])
    out_ref[...] = scratch[...].astype(BF16)


def feature_kernel(x_ref, w_ref, out_ref):
    pieces = x_ref.shape[1] // 2
    for stream in range(3):
        for side in range(2):
            rows = slice(side * pieces, (side + 1) * pieces)
            weights = w_ref[stream, rows, :]
            signal = x_ref[stream, rows, :].astype(F32)
            total = weights[:, 0:1] * signal
            for offset in range(1, TAPS):
                total = total + weights[:, offset : offset + 1] * pltpu.roll(signal, offset, 1)
            out_ref[stream, rows, :] = total


def local_kernel(
    owners,
    r_ref,
    member_ref,
    feat_ref,
    w_ref,
    skip_ref,
    cot_ref,
    out_ref,
    grad_ref,
    tail_ref,
    scratch,
    out_room,
    grad_room,
    tail_room,
    sems,
):
    member = member_ref[0]
    length = cot_ref.shape[1]
    scratch[...] = r_ref[...].astype(F32)
    lines = Lines(scratch, OUT_ROWS)
    pieces = lines.count
    copies = []

    def send(source, target):
        copy = pltpu.make_async_copy(source, target, sems.at[len(copies)])
        copy.start()
        copies.append(copy)

    def block(row, top_place):
        return decoded(lines.get_block(row), tops[:, TOP_LANE + top_place : TOP_LANE + top_place + 1])

    tops = lines.get(OUT_RIM)
    rim = exchanged(tops, member, owners)
    rim = rim + pltpu.roll(rim, LANES - RIM, 1)
    head = exchanged(lines.get(OUT_HEAD), member, owners)
    head = head + pltpu.roll(head, LANES - RIM, 1)
    lane = lax.broadcasted_iota(jnp.int32, (pieces, LANES), 1)

    def first_lanes(array, place):
        start = 2 * RIM * place
        return pltpu.roll(array, LANES - start, 1) if start else array

    for side in range(2):
        rows = slice(side * pieces, (side + 1) * pieces)
        featured = []
        for stream in range(3):
            inside = feat_ref[stream, rows, :]
            left = first_lanes(head, stream * 2 + side)
            left = jnp.where(lane < RIM, left, inside[:, :LANES])
            featured.append(jnp.concatenate([left, inside[:, LANES:]], axis=1))
        query, key, value = featured
        cot = cot_ref[rows, :]
        skip = skip_ref[rows, :]
        long_out = exchanged(block(OUT_LONG + 2 * side, side), member, owners)
        mixer = long_out + skip * (key * value)
        out_room[rows, :] = query * mixer
        send(out_room.at[rows, :], out_ref.at[rows, :])
        grad_long = exchanged(block(OUT_GRAD + 2 * side, 2 + side), member, owners)
        grad_product = grad_long + skip * (cot * query)
        for stream, grad in enumerate((cot * mixer, grad_product * value, grad_product * key)):
            weights = w_ref[stream, rows, :]
            after = first_lanes(rim, stream * 2 + side)
            extended = jnp.concatenate([grad, after], axis=1)
            total = weights[:, 0:1] * grad
            for offset in range(1, TAPS):
                shifted = pltpu.roll(extended, length + LANES - offset, 1)[:, :length]
                total = total + weights[:, offset : offset + 1] * shifted
            grad_room[stream, rows, :] = total
            send(grad_room.at[stream, rows, :], grad_ref.at[stream, rows, :])
    partial = block(OUT_FILT, 4)
    owned = pieces // owners
    total = partial[:owned]
    for place in range(1, owners):
        total = total + partial[place * owned : (place + 1) * owned]
    tail_room[...] = total
    send(tail_room, tail_ref)
    for copy in copies:
        copy.wait()


VMEM_SPEC = pl.BlockSpec(memory_space=pltpu.VMEM)
SMEM_SPEC = pl.BlockSpec(memory_space=pltpu.SMEM)
ANY_SPEC = pl.BlockSpec(memory_space=pl.ANY)


def call(kernel, out_shape, operands, scratch=(), specs=None, flops=0, out_spec=VMEM_SPEC):
    specs = specs or {}
    return pl.pallas_call(
        kernel,
        out_shape=out_shape,
        in_specs=[specs.get(place, VMEM_SPEC) for place in range(len(operands))],
        out_specs=jax.tree.map(lambda _: out_spec, out_shape),
        scratch_shapes=list(scratch),
        compiler_params=pltpu.CompilerParams(vmem_limit_bytes=24 * 1024 * 1024),
        cost_estimate=pl.CostEstimate(flops=flops, bytes_accessed=1 << 20, transcendentals=0),
    )(*operands)


def shards(inputs, short_weight, skip, filters, cotangent):
    pieces = lax.axis_size("ctx")
    owners = lax.axis_size("ch")
    position = lax.axis_index("ctx")
    member = lax.axis_index("ch")
    _, channels, length = inputs.shape
    owned = filters.shape[0]
    count = 2 * pieces
    scale = 1.0 / math.sqrt(pieces * length)
    member_word = member.astype(jnp.int32).reshape(1)

    def shape(*dims, dtype=F32):
        return jax.ShapeDtypeStruct(dims, dtype)

    def room(rows):
        return pltpu.VMEM((pieces * rows, LANES), F32)

    def transposed(array):
        rows = array.shape[0] // pieces
        array = lax.all_to_all(array.reshape(pieces, rows // 2, 2, LANES), "ctx", 0, 0)
        return array.reshape(pieces * rows, LANES)

    sent = call(
        functools.partial(pack_kernel, owners),
        shape(pieces * IN_ROWS, LANES, dtype=BF16),
        (member_word, inputs, cotangent, filters),
        [
            room(IN_ROWS),
            pltpu.VMEM(inputs.shape, BF16),
            pltpu.VMEM(cotangent.shape, F32),
            pltpu.VMEM(filters.shape, F32),
            pltpu.SemaphoreType.DMA((5,)),
        ],
        specs={0: SMEM_SPEC, 1: ANY_SPEC, 2: ANY_SPEC, 3: ANY_SPEC},
    )
    received = transposed(sent)

    group = ((position // owned) ^ member) * owned + position % owned
    own = lax.dynamic_slice_in_dim(short_weight.reshape(3, 2, pieces, TAPS), group, 1, 2)
    own_skip = lax.dynamic_slice_in_dim(skip.reshape(2, pieces), group, 1, 1)
    scalars = jnp.concatenate([own.reshape(-1), own_skip.reshape(-1)])
    constants = [jnp.asarray(table) for table in tables(pieces, length, scale)]
    featured = call(feature_kernel, shape(3, channels, length), (inputs, short_weight))
    skip_column = skip[:, None]
    received, featured, skip_column, short_rows = lax.optimization_barrier(
        (received, featured, skip_column, short_weight)
    )

    cross, spectra, kept = call(
        forward_kernel,
        (
            shape(pieces * CROSS_ROWS, LANES, dtype=BF16),
            shape(2 * count, 2 * length),
            shape(11, pieces, LANES),
        ),
        (received, scalars, *constants),
        [room(IN_ROWS), room(CROSS_ROWS)],
        specs={1: SMEM_SPEC},
        flops=800000000,
    )
    partners = [
        (place * owners + shard, place * owners + (shard ^ (place // owned)))
        for place in range(pieces)
        for shard in range(owners)
    ]
    cross = lax.ppermute(cross, ("ctx", "ch"), partners)
    sent = call(
        inverse_kernel,
        shape(pieces * OUT_ROWS, LANES, dtype=BF16),
        (cross, spectra, kept, scalars, *constants),
        [room(CROSS_ROWS), room(OUT_ROWS)],
        specs={3: SMEM_SPEC},
        flops=800000000,
    )
    received = transposed(sent)

    return call(
        functools.partial(local_kernel, owners),
        (shape(channels, length), shape(3, channels, length), shape(owned, length)),
        (received, member_word, featured, short_rows, skip_column, cotangent),
        [
            room(OUT_ROWS),
            pltpu.VMEM((channels, length), F32),
            pltpu.VMEM((3, channels, length), F32),
            pltpu.VMEM((owned, length), F32),
            pltpu.SemaphoreType.DMA((9,)),
        ],
        specs={1: SMEM_SPEC},
        out_spec=ANY_SPEC,
    )


def solution(mesh):
    in_specs = (P(None, "ch", "ctx"), P(None, "ch", None), P("ch"), P("ch", "ctx"), P("ch", "ctx"))
    out_specs = (P("ch", "ctx"), P(None, "ch", "ctx"), P("ch", "ctx"))
    return jax.shard_map(shards, mesh=mesh, in_specs=in_specs, out_specs=out_specs, check_vma=False)
```

```python
import functools
import math

import jax
import jax.numpy as jnp
import ml_dtypes
import numpy as np
from jax import lax
from jax.experimental import pallas as pl
from jax.experimental.pallas import tpu as pltpu
from jax.sharding import PartitionSpec as P

BF16 = jnp.bfloat16
F32 = jnp.float32
LANES = 128
TAPS = 7
IN_PROD, IN_MIXED, IN_FILT, IN_RIM, IN_ROWS = 0, 4, 8, 10, 12
CROSS_FILT, CROSS_GRAD, CROSS_TOPS, CROSS_ROWS = 0, 2, 4, 5
OUT_LONG, OUT_GRAD, OUT_FILT, OUT_RIM, OUT_HEAD, OUT_ROWS = 0, 4, 8, 10, 11, 12
RIM = TAPS - 1
COT_LANE = 12 * RIM
IN_TOP_LANE = 16 * RIM
TOP_LANE = 12 * RIM
REACH = 125.0
TABLES = 7


def halves(array):
    array = np.asarray(array, np.float32)
    high = array.astype(ml_dtypes.bfloat16)
    low = (array - high.astype(np.float32)).astype(ml_dtypes.bfloat16)
    return high, low


@functools.lru_cache(maxsize=None)
def tables(pieces, length, scale):
    blocks = 2 * pieces
    total = blocks * length
    freq = np.arange(blocks)[:, None]
    angle = 2.0 * np.pi * ((freq * np.arange(pieces)[None, :]) % blocks) / blocks
    cos, sin = np.cos(angle), np.sin(angle)
    outer = np.block([[cos, sin], [-sin, cos]])
    back = np.block([[cos.T, sin.T], [sin.T, -cos.T]]) * (scale / total)
    angle = 2.0 * np.pi * ((freq * np.arange(length)[None, :]) % total) / total
    twiddle = np.stack([np.cos(angle), -np.sin(angle)]).astype(np.float32)
    angle = 2.0 * np.pi * np.arange(length // 2) / length
    middle = np.zeros((2, 8, length), np.float32)
    middle[:, 0, : length // 2] = np.stack([np.cos(angle), -np.sin(angle)])
    twiddle = np.concatenate([twiddle, middle], axis=1)
    count = np.arange(length // 2)
    angle = 2.0 * np.pi * ((count[:, None] * count[None, :]) % (length // 2)) / (length // 2)
    cos, sin = np.cos(angle), np.sin(angle)
    inner = np.block([[cos, -sin], [sin, cos]])
    return (*halves(outer), *halves(back), twiddle, *halves(inner))


def split(value):
    high = value.astype(BF16)
    return high, (value - high.astype(F32)).astype(BF16)


def product3(left, right):
    left = jnp.concatenate([left[0], left[1], left[0]], axis=1)
    right = jnp.concatenate([right[0], right[0], right[1]], axis=0)
    return jnp.dot(left, right, preferred_element_type=F32)


def encoded(value):
    top = jnp.max(jnp.abs(value), axis=1, keepdims=True)
    top = (jnp.maximum(top, 1e-30) * 1.008).astype(BF16).astype(F32)
    square = jnp.abs(value) * (1.0 / top)
    size = square * lax.rsqrt(jnp.maximum(square, 1e-30))
    code = jnp.exp2(size * (2.0 * REACH) - REACH)
    return jnp.where(value < 0.0, -code, code), top


def decoded(code, top):
    size = (jnp.log2(jnp.abs(code)) + REACH) * (0.5 / REACH)
    value = size * size * top
    return jnp.where(code < 0.0, -value, value)


class Lines:
    def __init__(self, ref, rows):
        self.ref, self.rows = ref, rows
        self.count = ref.shape[0] // rows

    def get(self, row):
        return self.ref[pl.ds(row, self.count, stride=self.rows), :]

    def put(self, row, value):
        self.ref[pl.ds(row, self.count, stride=self.rows), :] = value

    def get_block(self, row):
        return jnp.concatenate([self.get(row), self.get(row + 1)], axis=1)

    def put_block(self, row, value):
        self.put(row, value[:, :LANES])
        self.put(row + 1, value[:, LANES:])


def in_lanes(columns, first, like):
    lane = lax.broadcasted_iota(jnp.int32, like.shape, 1)
    for place, column in enumerate(columns):
        like = jnp.where(lane == first + place, column, like)
    return like


def exchanged(value, member, owners):
    size = value.shape[0] // owners
    step = 1
    while step < owners:
        order = [place ^ step for place in range(owners)]
        swapped = jnp.concatenate([value[k * size : (k + 1) * size] for k in order], axis=0)
        value = jnp.where((member & step) != 0, swapped, value)
        step *= 2
    return value


def rolled(value, lanes):
    lanes %= value.shape[1]
    return pltpu.roll(value, lanes, 1) if lanes else value


def lane_numbers(like):
    return lax.broadcasted_iota(jnp.int32, like.shape, 1)


def put_lanes(target, first, count, value, start=0):
    lane = lane_numbers(target)
    inside = (lane >= first) & (lane < first + count)
    return jnp.where(inside, rolled(value, first - start), target)


def eight_rows(taps):
    return jnp.concatenate([taps, jnp.zeros((8 - TAPS, taps.shape[1]), F32)], axis=0)


def spread_taps(taps):
    columns = jnp.transpose(eight_rows(taps))
    shape = (columns.shape[0], LANES)
    return jnp.concatenate(
        [jnp.broadcast_to(columns[:, tap : tap + 1], shape) for tap in range(TAPS)], axis=1
    )


def inner_featured(signal, spread):
    halves_total = [0.0, 0.0]
    for offset in range(TAPS):
        shifted = pltpu.roll(signal, offset, 1) if offset else signal
        weight = spread[:, offset * LANES : (offset + 1) * LANES]
        for half in range(2):
            part = weight * shifted[:, half * LANES : (half + 1) * LANES]
            halves_total[half] = halves_total[half] + part if offset else part
    return jnp.concatenate(halves_total, axis=1)


def own_lanes(taps_ref, skip, group):
    lane = lax.broadcasted_iota(jnp.int32, (8, LANES), 1)
    row = lax.broadcasted_iota(jnp.int32, (8, LANES), 0)
    pieces = LANES // 2
    own = jnp.zeros((8, LANES), F32)
    skips = jnp.broadcast_to(skip, (8, LANES))
    for side in range(2):
        here = lane == group + side * pieces
        value = jnp.sum(jnp.where(here, skips, 0.0), axis=1, keepdims=True)
        first = 2 * RIM * side
        own = jnp.where((row == TAPS) & (lane >= first) & (lane < first + RIM), value, own)
        for stream in range(3):
            value = jnp.sum(
                jnp.where(here, eight_rows(taps_ref[stream]), 0.0), axis=1, keepdims=True
            )
            first = 2 * RIM * (stream * 2 + side)
            own = jnp.where((row < TAPS) & (lane >= first) & (lane < first + RIM), value, own)
    return own


def pack_kernel(
    owners,
    place_ref,
    x_hbm,
    cot_hbm,
    filt_hbm,
    w_hbm,
    skip_hbm,
    out_ref,
    own_ref,
    scratch,
    x_ref,
    cot_ref,
    filt_ref,
    w_ref,
    skip_ref,
    spread_ref,
    sems,
):
    copies = [
        pltpu.make_async_copy(source, target, sems.at[place])
        for place, (source, target) in enumerate(
            [
                (w_hbm, w_ref),
                (x_hbm.at[1], x_ref.at[1]),
                (x_hbm.at[2], x_ref.at[2]),
                (x_hbm.at[0], x_ref.at[0]),
                (cot_hbm, cot_ref),
                (filt_hbm, filt_ref),
                (skip_hbm, skip_ref),
            ]
        )
    ]
    for copy in copies:
        copy.start()
    lines = Lines(scratch, IN_ROWS)
    pieces = lines.count
    member = place_ref[0]
    blank = jnp.zeros((pieces, LANES), F32)
    lane = lane_numbers(blank)
    rims = [blank, blank]
    featured = {}

    def inner_part(value):
        return jnp.concatenate(
            [jnp.where(lane < RIM, 0.0, value[:, :LANES]), value[:, LANES:]], axis=1
        )

    copies[0].wait()
    for stream in range(3):
        spread_ref[stream] = spread_taps(w_ref[stream])
    for place, stream in ((1, 1), (2, 2), (3, 0)):
        copies[place].wait()
        for side in range(2):
            rows = slice(side * pieces, (side + 1) * pieces)
            signal = x_ref[stream, rows, :].astype(F32)
            featured[stream, side] = inner_featured(signal, spread_ref[stream, rows, :])
            first = 2 * RIM * (stream * 2 + side)
            rims[side] = put_lanes(rims[side], first, RIM, signal[:, LANES:], LANES - RIM)
            rims[side] = put_lanes(rims[side], first + RIM, RIM, signal[:, :LANES])
    products, mixed = [], []
    for side in range(2):
        products.append(inner_part(featured[1, side] * featured[2, side]))
    copies[4].wait()
    for side in range(2):
        cot = cot_ref[side * pieces : (side + 1) * pieces, :]
        mixed.append(inner_part(featured[0, side] * cot))
        high = cot[:, :LANES].astype(BF16).astype(F32)
        first = COT_LANE + 2 * RIM * side
        rims[side] = put_lanes(rims[side], first, RIM, high)
        rims[side] = put_lanes(rims[side], first + RIM, RIM, cot[:, :LANES] - high)
    tops = []
    for row, values in ((IN_PROD, products), (IN_MIXED, mixed)):
        for side in range(2):
            code, top = encoded(exchanged(values[side], member, owners))
            lines.put_block(row + 2 * side, code)
            tops.append(top)
    copies[5].wait()
    code, top = encoded(filt_ref[...])
    lines.put_block(IN_FILT, jnp.concatenate([code] * owners, axis=0))
    tops.append(jnp.concatenate([top] * owners, axis=0))
    rim = exchanged(rims[0] + rims[1], member, owners)
    lines.put(IN_RIM, in_lanes(tops, IN_TOP_LANE, rim))
    lines.put(IN_RIM + 1, blank)
    out_ref[...] = scratch[...].astype(BF16)
    copies[6].wait()
    own_ref[...] = own_lanes(w_ref, skip_ref[...], place_ref[1])


def turned(re, im, twiddle):
    turn_re, turn_im = twiddle
    return re * turn_re - im * turn_im, re * turn_im + im * turn_re


def parted(re, im, middle):
    half = re.shape[1] // 2
    even = jnp.concatenate([re[:, :half] + re[:, half:], im[:, :half] + im[:, half:]], axis=1)
    odd = turned(re[:, :half] - re[:, half:], im[:, :half] - im[:, half:], middle)
    return jnp.concatenate([even, jnp.concatenate(odd, axis=1)], axis=0)


def joined(pair, middle):
    count, half = pair.shape[0] // 2, pair.shape[1] // 2
    re, im = pair[:count, :half], pair[:count, half:]
    turn_re, turn_im = turned(pair[count:, :half], pair[count:, half:], middle)
    whole_re = jnp.concatenate([re + turn_re, re - turn_re], axis=1)
    return whole_re, jnp.concatenate([im + turn_im, im - turn_im], axis=1)


def spectrum(columns, twiddle, middle, count):
    re, im = turned(columns[:count], columns[count:], twiddle)
    return parted(re, im, middle)


def upright(spectra, inner, twiddle, middle, count):
    inside = product3(split(spectra), inner)
    columns = []
    for start in range(0, spectra.shape[0], 2 * count):
        re, im = joined(inside[start : start + 2 * count], middle)
        columns.append(jnp.concatenate(turned(re, im, twiddle), axis=0))
    return jnp.concatenate(columns, axis=1)


def halved_lanes(value):
    high = value.astype(BF16).astype(F32)
    lane = lane_numbers(value)
    both = jnp.where(lane % (2 * RIM) < RIM, high, rolled(value - high, RIM))
    return jnp.where(lane < 12 * RIM, both, 0.0)


def forward_kernel(
    r_ref,
    w_ref,
    outer_hi,
    outer_lo,
    back_hi,
    back_lo,
    twiddle_ref,
    inner_hi,
    inner_lo,
    cross_ref,
    spec_ref,
    kept_ref,
    scratch,
    cross_scratch,
):
    scratch[...] = r_ref[...].astype(F32)
    lines = Lines(scratch, IN_ROWS)
    cross = Lines(cross_scratch, CROSS_ROWS)
    pieces = lines.count
    count = 2 * pieces
    length = 2 * LANES
    rim = lines.get(IN_RIM)
    tops = [rim[:, IN_TOP_LANE + place : IN_TOP_LANE + place + 1] for place in range(5)]
    lane = lane_numbers(rim)
    row_number = lax.broadcasted_iota(jnp.int32, rim.shape, 0)
    before = jnp.where(row_number == 0, 0.0, pltpu.roll(rim, 1, 0))
    ends = jnp.where(lane % (2 * RIM) < RIM, before, rim)
    head = jnp.zeros_like(rim)
    for offset in range(TAPS):
        head = head + w_ref[offset : offset + 1, :] * rolled(ends, offset - RIM)
    side_lanes = 2 * RIM
    head_key, head_value = rolled(head, -2 * side_lanes), rolled(head, -4 * side_lanes)
    head_cot = rolled(rim + rolled(rim, -RIM), -COT_LANE)
    head_prod, head_mixed = head_key * head_value, head_cot * head
    for place, array in enumerate((head, head_prod, head_mixed, head_key, head_value, head_cot)):
        kept_ref[place] = array

    def whole(row, top, first):
        value = decoded(lines.get_block(row), top)
        return jnp.concatenate([jnp.where(lane < RIM, first, value[:, :LANES]), value[:, LANES:]], axis=1)

    prod, mixed = [], []
    for side in range(2):
        shift = -side_lanes * side
        prod.append(whole(IN_PROD + 2 * side, tops[side], rolled(head_prod, shift)))
        mixed.append(whole(IN_MIXED + 2 * side, tops[2 + side], rolled(head_mixed, shift)))

    signals = jnp.concatenate(
        [jnp.concatenate(prod, axis=0), jnp.concatenate(mixed, axis=0)], axis=1
    )
    twiddle = (twiddle_ref[0, :count], twiddle_ref[1, :count])
    middle = tuple(twiddle_ref[place, count : count + 1, :LANES] for place in range(2))
    spread = product3((outer_hi[...], outer_lo[...]), split(signals))
    parts = [
        spectrum(spread[:, start : start + length], twiddle, middle, count) for start in (0, length)
    ]
    inner = (inner_hi[...], inner_lo[...])
    spectra = product3(split(jnp.concatenate(parts, axis=0)), inner)
    spec_ref[...] = spectra
    z_re, z_im = spectra[:length, :LANES], spectra[:length, LANES:]
    m_re, m_im = spectra[length:, :LANES], spectra[length:, LANES:]
    tail = jnp.concatenate([z_re * m_re + z_im * m_im, z_im * m_re - z_re * m_im], axis=1)
    columns = upright(tail, inner, twiddle, middle, count)
    partial = product3((back_hi[:pieces, :], back_lo[:pieces, :]), split(columns))
    code, top = encoded(partial)
    cross.put_block(CROSS_GRAD, code)
    cross.put_block(CROSS_FILT, lines.get_block(IN_FILT))
    blank = jnp.zeros((pieces, LANES), F32)
    cross.put(CROSS_TOPS, in_lanes([tops[4], top], 0, blank))
    cross_ref[...] = cross_scratch[...].astype(BF16)


def inverse_kernel(
    cross_ref,
    spec_ref,
    kept_ref,
    w_ref,
    outer_hi,
    outer_lo,
    back_hi,
    back_lo,
    twiddle_ref,
    inner_hi,
    inner_lo,
    out_ref,
    cross_scratch,
    scratch,
):
    cross_scratch[...] = cross_ref[...].astype(F32)
    cross = Lines(cross_scratch, CROSS_ROWS)
    lines = Lines(scratch, OUT_ROWS)
    pieces = lines.count
    count = 2 * pieces
    length = 2 * LANES
    tops = cross.get(CROSS_TOPS)
    filt = decoded(cross.get_block(CROSS_FILT), tops[:, 0:1])
    inner = (inner_hi[...], inner_lo[...])
    twiddle = (twiddle_ref[0, :count], twiddle_ref[1, :count])
    middle = tuple(twiddle_ref[place, count : count + 1, :LANES] for place in range(2))
    spread = product3((outer_hi[:, :pieces], outer_lo[:, :pieces]), split(filt))
    spectra = product3(split(spectrum(spread, twiddle, middle, count)), inner)
    f_re, f_im = spectra[:, :LANES], spectra[:, LANES:]
    z_re, z_im = spec_ref[:length, :LANES], spec_ref[:length, LANES:]
    m_re, m_im = spec_ref[length:, :LANES], spec_ref[length:, LANES:]
    long_pair = jnp.concatenate(
        [z_re * f_re - z_im * f_im, -(z_re * f_im + z_im * f_re)], axis=1
    )
    grad_pair = jnp.concatenate([m_re * f_re + m_im * f_im, m_re * f_im - m_im * f_re], axis=1)
    columns = upright(
        jnp.concatenate([long_pair, grad_pair], axis=0), inner, twiddle, middle, count
    )
    restored = product3((back_hi[...], back_lo[...]), split(columns))
    side_lanes = 2 * RIM
    blank = jnp.zeros((pieces, LANES), F32)
    heads = {OUT_LONG: blank, OUT_GRAD: blank}
    out_tops = []
    for row, columns in ((OUT_LONG, slice(0, length)), (OUT_GRAD, slice(length, 2 * length))):
        for side in range(2):
            value = restored[side * pieces : (side + 1) * pieces, columns]
            code, top = encoded(value)
            lines.put_block(row + 2 * side, code)
            out_tops.append(top)
            heads[row] = put_lanes(heads[row], side_lanes * side, RIM, value[:, :LANES])
    head, prod, mixed, key, value, cot = [kept_ref[place] for place in range(6)]
    skip = w_ref[TAPS : TAPS + 1, :]
    grad_query = cot * (heads[OUT_LONG] + skip * prod)
    grad_product = heads[OUT_GRAD] + skip * mixed
    rim = put_lanes(blank, 0, 2 * side_lanes, grad_query)
    rim = put_lanes(rim, 2 * side_lanes, 2 * side_lanes, grad_product * value)
    rim = put_lanes(rim, 4 * side_lanes, 2 * side_lanes, grad_product * key)
    row_number = lax.broadcasted_iota(jnp.int32, rim.shape, 0)
    rim = jnp.where(row_number == pieces - 1, 0.0, pltpu.roll(rim, pieces - 1, 0))
    lines.put_block(OUT_FILT, cross.get_block(CROSS_GRAD))
    lines.put(OUT_RIM, in_lanes([*out_tops, tops[:, 1:2]], TOP_LANE, halved_lanes(rim)))
    lines.put(OUT_HEAD, halved_lanes(head))
    out_ref[...] = scratch[...].astype(BF16)


def feature_kernel(*refs):
    x_hbm, w_hbm, skip_hbm = refs[:3]
    out_ref, spread_ref, wide_ref = refs[3 + TABLES : 6 + TABLES]
    x_ref, w_ref, skip_ref, sems = refs[6 + 2 * TABLES :]
    pairs = [(w_hbm, w_ref), (x_hbm, x_ref), (skip_hbm, skip_ref)]
    pairs += list(zip(refs[3 : 3 + TABLES], refs[6 + TABLES : 6 + 2 * TABLES]))
    copies = [
        pltpu.make_async_copy(source, target, sems.at[place])
        for place, (source, target) in enumerate(pairs)
    ]
    for copy in copies:
        copy.start()
    copies[0].wait()
    for stream in range(3):
        spread_ref[stream] = spread_taps(w_ref[stream])
    copies[1].wait()
    for stream in range(3):
        out_ref[stream] = inner_featured(x_ref[stream].astype(F32), spread_ref[stream])
    copies[2].wait()
    column = jnp.transpose(jnp.broadcast_to(skip_ref[...], (8, LANES)))[:, 0:1]
    wide_ref[...] = jnp.broadcast_to(column, wide_ref.shape)
    for copy in copies[3:]:
        copy.wait()


def local_kernel(
    owners,
    r_ref,
    place_ref,
    feat_ref,
    w_ref,
    skip_ref,
    cot_ref,
    out_ref,
    grad_ref,
    tail_ref,
    scratch,
    out_room,
    grad_room,
    tail_room,
    sems,
):
    member = place_ref[0]
    scratch[...] = r_ref[...].astype(F32)
    lines = Lines(scratch, OUT_ROWS)
    pieces = lines.count
    copies = []

    def send(source, target):
        copy = pltpu.make_async_copy(source, target, sems.at[len(copies)])
        copy.start()
        copies.append(copy)

    def block(row, top_place):
        return decoded(lines.get_block(row), tops[:, TOP_LANE + top_place : TOP_LANE + top_place + 1])

    tops = lines.get(OUT_RIM)
    rim = exchanged(tops, member, owners)
    rim = rim + pltpu.roll(rim, LANES - RIM, 1)
    head = exchanged(lines.get(OUT_HEAD), member, owners)
    head = head + pltpu.roll(head, LANES - RIM, 1)
    lane = lax.broadcasted_iota(jnp.int32, (pieces, LANES), 1)

    def first_lanes(array, place):
        return rolled(array, -2 * RIM * place)

    for side in range(2):
        rows = slice(side * pieces, (side + 1) * pieces)
        featured = []
        for stream in range(3):
            inside = feat_ref[stream, rows, :]
            left = first_lanes(head, stream * 2 + side)
            left = jnp.where(lane < RIM, left, inside[:, :LANES])
            featured.append(jnp.concatenate([left, inside[:, LANES:]], axis=1))
        query, key, value = featured
        cot = cot_ref[rows, :]
        skip = jnp.concatenate([skip_ref[rows, :]] * 2, axis=1)
        long_out = exchanged(block(OUT_LONG + 2 * side, side), member, owners)
        mixer = long_out + skip * (key * value)
        out_room[rows, :] = query * mixer
        send(out_room.at[rows, :], out_ref.at[rows, :])
        grad_long = exchanged(block(OUT_GRAD + 2 * side, 2 + side), member, owners)
        grad_product = grad_long + skip * (cot * query)
        for stream, grad in enumerate((cot * mixer, grad_product * value, grad_product * key)):
            after = first_lanes(rim, stream * 2 + side)
            near, far = grad[:, :LANES], grad[:, LANES:]
            weight = w_ref[stream, rows, :LANES]
            total_near, total_far = weight * near, weight * far
            for offset in range(1, TAPS):
                weight = w_ref[stream, rows, offset * LANES : (offset + 1) * LANES]
                wrapped = lane < offset
                total_near = total_near + weight * rolled(jnp.where(wrapped, far, near), -offset)
                total_far = total_far + weight * rolled(jnp.where(wrapped, after, far), -offset)
            grad_room[stream, rows, :LANES] = total_near
            grad_room[stream, rows, LANES:] = total_far
            send(grad_room.at[stream, rows, :], grad_ref.at[stream, rows, :])
    partial = block(OUT_FILT, 4)
    owned = pieces // owners
    total = partial[:owned]
    for place in range(1, owners):
        total = total + partial[place * owned : (place + 1) * owned]
    tail_room[...] = total
    send(tail_room, tail_ref)
    for copy in copies:
        copy.wait()


VMEM_SPEC = pl.BlockSpec(memory_space=pltpu.VMEM)
SMEM_SPEC = pl.BlockSpec(memory_space=pltpu.SMEM)
ANY_SPEC = pl.BlockSpec(memory_space=pl.ANY)
HBM_SPEC = pl.BlockSpec(memory_space=pltpu.HBM)


def call(
    kernel, out_shape, operands, scratch=(), specs=None, flops=0, out_spec=VMEM_SPEC, room_mib=24
):
    specs = specs or {}
    return pl.pallas_call(
        kernel,
        out_shape=out_shape,
        in_specs=[specs.get(place, VMEM_SPEC) for place in range(len(operands))],
        out_specs=jax.tree.map(lambda _: out_spec, out_shape),
        scratch_shapes=list(scratch),
        compiler_params=pltpu.CompilerParams(vmem_limit_bytes=room_mib << 20),
        cost_estimate=pl.CostEstimate(flops=flops, bytes_accessed=1 << 20, transcendentals=0),
    )(*operands)


def shards(inputs, short_weight, skip, filters, cotangent):
    pieces = lax.axis_size("ctx")
    owners = lax.axis_size("ch")
    position = lax.axis_index("ctx")
    member = lax.axis_index("ch")
    _, channels, length = inputs.shape
    owned = filters.shape[0]
    count = 2 * pieces
    scale = 1.0 / math.sqrt(pieces * length)

    def shape(*dims, dtype=F32):
        return jax.ShapeDtypeStruct(dims, dtype)

    def pinned(array):
        return pltpu.with_memory_space_constraint(array, pltpu.HBM)

    def room(rows):
        return pltpu.VMEM((pieces * rows, LANES), F32)

    def transposed(array):
        rows = array.shape[0] // pieces
        array = lax.all_to_all(array.reshape(pieces, rows // 2, 2, LANES), "ctx", 0, 0)
        return array.reshape(pieces * rows, LANES)

    group = ((position // owned) ^ member) * owned + position % owned
    place = jnp.stack([member, group]).astype(jnp.int32)
    taps = jnp.transpose(short_weight, (0, 2, 1))
    skip_row = skip[None]
    sent, own = call(
        functools.partial(pack_kernel, owners),
        (shape(pieces * IN_ROWS, LANES, dtype=BF16), shape(8, LANES)),
        (place, *(pinned(array) for array in (inputs, cotangent, filters, taps, skip_row))),
        [
            room(IN_ROWS),
            pltpu.VMEM(inputs.shape, BF16),
            pltpu.VMEM(cotangent.shape, F32),
            pltpu.VMEM(filters.shape, F32),
            pltpu.VMEM(taps.shape, F32),
            pltpu.VMEM(skip_row.shape, F32),
            pltpu.VMEM((3, channels, TAPS * LANES), F32),
            pltpu.SemaphoreType.DMA((7,)),
        ],
        specs={0: SMEM_SPEC, **{operand: HBM_SPEC for operand in range(1, 6)}},
    )
    received = transposed(sent)
    constants = [jnp.asarray(table) for table in tables(pieces, length, scale)]
    beside = call(
        feature_kernel,
        (
            shape(3, channels, length),
            shape(3, channels, TAPS * LANES),
            shape(channels, LANES),
            *(shape(*table.shape, dtype=table.dtype) for table in constants),
        ),
        [pinned(array) for array in (inputs, taps, skip_row, *constants)],
        [
            *(pltpu.VMEM(array.shape, array.dtype) for array in (inputs, taps, skip_row)),
            pltpu.SemaphoreType.DMA((3 + TABLES,)),
        ],
        specs={operand: HBM_SPEC for operand in range(3 + TABLES)},
        flops=10000000,
    )
    received, beside = lax.optimization_barrier((received, beside))
    beside, constants = beside[:3], beside[3:]
    cross, spectra, kept = call(
        forward_kernel,
        (
            shape(pieces * CROSS_ROWS, LANES, dtype=BF16),
            shape(2 * length, length),
            shape(6, pieces, LANES),
        ),
        (received, own, *constants),
        [room(IN_ROWS), room(CROSS_ROWS)],
        flops=800000000,
    )
    partners = [
        (place * owners + shard, place * owners + (shard ^ (place // owned)))
        for place in range(pieces)
        for shard in range(owners)
    ]
    cross = lax.ppermute(cross, ("ctx", "ch"), partners)
    sent = call(
        inverse_kernel,
        shape(pieces * OUT_ROWS, LANES, dtype=BF16),
        (cross, spectra, kept, own, *constants),
        [room(CROSS_ROWS), room(OUT_ROWS)],
        flops=800000000,
    )
    received = transposed(sent)

    return call(
        functools.partial(local_kernel, owners),
        (shape(channels, length), shape(3, channels, length), shape(owned, length)),
        (received, place, *beside, cotangent),
        [
            room(OUT_ROWS),
            pltpu.VMEM((channels, length), F32),
            pltpu.VMEM((3, channels, length), F32),
            pltpu.VMEM((owned, length), F32),
            pltpu.SemaphoreType.DMA((9,)),
        ],
        specs={1: SMEM_SPEC},
        out_spec=ANY_SPEC,
    )


def solution(mesh):
    in_specs = (P(None, "ch", "ctx"), P(None, "ch", None), P("ch"), P("ch", "ctx"), P("ch", "ctx"))
    out_specs = (P("ch", "ctx"), P(None, "ch", "ctx"), P("ch", "ctx"))
    return jax.shard_map(shards, mesh=mesh, in_specs=in_specs, out_specs=out_specs, check_vma=False)
```

```python
import functools
import math

import jax
import jax.numpy as jnp
import ml_dtypes
import numpy as np
from jax import lax
from jax.experimental import pallas as pl
from jax.experimental.pallas import tpu as pltpu
from jax.sharding import PartitionSpec as P

BF16 = jnp.bfloat16
F32 = jnp.float32
LANES = 128
TAPS = 7
IN_PROD, IN_MIXED, IN_FILT, IN_RIM, IN_ROWS = 0, 4, 8, 10, 12
CROSS_FILT, CROSS_GRAD, CROSS_TOPS, CROSS_ROWS = 0, 2, 4, 5
OUT_LONG, OUT_GRAD, OUT_FILT, OUT_RIM, OUT_HEAD, OUT_ROWS = 0, 4, 8, 10, 11, 12
RIM = TAPS - 1
COT_LANE = 12 * RIM
IN_TOP_LANE = 16 * RIM
TOP_LANE = 12 * RIM
REACH = 125.0
TABLES = 7
CHUNK = 16


def halves(array):
    array = np.asarray(array, np.float32)
    high = array.astype(ml_dtypes.bfloat16)
    low = (array - high.astype(np.float32)).astype(ml_dtypes.bfloat16)
    return high, low


@functools.lru_cache(maxsize=None)
def tables(pieces, length, scale):
    blocks = 2 * pieces
    total = blocks * length
    freq = np.arange(blocks)[:, None]
    angle = 2.0 * np.pi * ((freq * np.arange(pieces)[None, :]) % blocks) / blocks
    cos, sin = np.cos(angle), np.sin(angle)
    outer = np.block([[cos, sin], [-sin, cos]])
    back = np.block([[cos.T, sin.T], [sin.T, -cos.T]]) * (scale / total)
    angle = 2.0 * np.pi * ((freq * np.arange(length)[None, :]) % total) / total
    twiddle = np.stack([np.cos(angle), -np.sin(angle)]).astype(np.float32)
    angle = 2.0 * np.pi * np.arange(length // 2) / length
    middle = np.zeros((2, 8, length), np.float32)
    middle[:, 0, : length // 2] = np.stack([np.cos(angle), -np.sin(angle)])
    twiddle = np.concatenate([twiddle, middle], axis=1)
    count = np.arange(length // 2)
    angle = 2.0 * np.pi * ((count[:, None] * count[None, :]) % (length // 2)) / (length // 2)
    cos, sin = np.cos(angle), np.sin(angle)
    inner = np.block([[cos, -sin], [sin, cos]])
    return (*halves(outer), *halves(back), twiddle, *halves(inner))


def split(value):
    high = value.astype(BF16)
    return high, (value - high.astype(F32)).astype(BF16)


def product3(left, right):
    left = jnp.concatenate([left[0], left[1], left[0]], axis=1)
    right = jnp.concatenate([right[0], right[0], right[1]], axis=0)
    parts = [
        jnp.dot(left[start : start + LANES], right, preferred_element_type=F32)
        for start in range(0, left.shape[0], LANES)
    ]
    return jnp.concatenate(parts, axis=0)


def encoded(value):
    top = jnp.max(jnp.abs(value), axis=1, keepdims=True)
    top = (jnp.maximum(top, 1e-30) * 1.008).astype(BF16).astype(F32)
    square = jnp.abs(value) * (1.0 / top)
    size = square * lax.rsqrt(jnp.maximum(square, 1e-30))
    code = jnp.exp2(size * (2.0 * REACH) - REACH)
    return jnp.where(value < 0.0, -code, code), top


def decoded(code, top):
    size = (jnp.log2(jnp.abs(code)) + REACH) * (0.5 / REACH)
    value = size * size * top
    return jnp.where(code < 0.0, -value, value)


class Lines:
    def __init__(self, ref, rows):
        self.ref, self.rows = ref, rows
        self.count = ref.shape[0] // rows

    def get(self, row):
        return self.ref[pl.ds(row, self.count, stride=self.rows), :]

    def put(self, row, value):
        self.ref[pl.ds(row, self.count, stride=self.rows), :] = value

    def get_block(self, row):
        return jnp.concatenate([self.get(row), self.get(row + 1)], axis=1)

    def put_block(self, row, value):
        self.put(row, value[:, :LANES])
        self.put(row + 1, value[:, LANES:])


def in_lanes(columns, first, like):
    lane = lax.broadcasted_iota(jnp.int32, like.shape, 1)
    for place, column in enumerate(columns):
        like = jnp.where(lane == first + place, column, like)
    return like


def exchanged(value, member, owners):
    size = value.shape[0] // owners
    step = 1
    while step < owners:
        order = [place ^ step for place in range(owners)]
        swapped = jnp.concatenate([value[k * size : (k + 1) * size] for k in order], axis=0)
        value = jnp.where((member & step) != 0, swapped, value)
        step *= 2
    return value


def rolled(value, lanes):
    lanes %= value.shape[1]
    return pltpu.roll(value, lanes, 1) if lanes else value


def lane_numbers(like):
    return lax.broadcasted_iota(jnp.int32, like.shape, 1)


def put_lanes(target, first, count, value, start=0):
    lane = lane_numbers(target)
    inside = (lane >= first) & (lane < first + count)
    return jnp.where(inside, rolled(value, first - start), target)


def eight_rows(taps):
    return jnp.concatenate([taps, jnp.zeros((8 - TAPS, taps.shape[1]), F32)], axis=0)


def spread_taps(taps):
    rest = eight_rows(taps)
    parts = []
    for _ in range(3):
        parts.append(rest.astype(BF16).astype(F32))
        rest = rest - parts[-1]
    columns = jnp.transpose(jnp.concatenate(parts, axis=0)).astype(BF16)
    shape = (24, TAPS * LANES)
    first = lax.broadcasted_iota(jnp.int32, shape, 0) % 8 * LANES
    lane = lax.broadcasted_iota(jnp.int32, shape, 1)
    chosen = jnp.where((lane >= first) & (lane < first + LANES), 1.0, 0.0).astype(BF16)
    return jnp.dot(columns, chosen, preferred_element_type=F32)


def inner_featured(signal, spread):
    near, far = signal[:, :LANES], signal[:, LANES:]
    lane = lane_numbers(near)
    weight = spread[:, :LANES]
    total_near, total_far = weight * near, weight * far
    for offset in range(1, TAPS):
        weight = spread[:, offset * LANES : (offset + 1) * LANES]
        wrapped = jnp.where(lane >= LANES - offset, near, far)
        total_near = total_near + weight * rolled(near, offset)
        total_far = total_far + weight * rolled(wrapped, offset)
    return jnp.concatenate([total_near, total_far], axis=1)


def own_lanes(taps_ref, skip, group):
    lane = lax.broadcasted_iota(jnp.int32, (8, LANES), 1)
    row = lax.broadcasted_iota(jnp.int32, (8, LANES), 0)
    pieces = LANES // 2
    own = jnp.zeros((8, LANES), F32)
    skips = jnp.broadcast_to(skip, (8, LANES))
    for side in range(2):
        here = lane == group + side * pieces
        value = jnp.sum(jnp.where(here, skips, 0.0), axis=1, keepdims=True)
        first = 2 * RIM * side
        own = jnp.where((row == TAPS) & (lane >= first) & (lane < first + RIM), value, own)
        for stream in range(3):
            value = jnp.sum(
                jnp.where(here, eight_rows(taps_ref[stream]), 0.0), axis=1, keepdims=True
            )
            first = 2 * RIM * (stream * 2 + side)
            own = jnp.where((row < TAPS) & (lane >= first) & (lane < first + RIM), value, own)
    return own


def pack_kernel(owners, place_ref, *refs):
    sources = refs[: 5 + TABLES]
    out_ref, own_ref, feat_ref, spread_ref, wide_ref, cot_ref = refs[5 + TABLES : 11 + TABLES]
    tables_here = refs[11 + TABLES : 11 + 2 * TABLES]
    scratch, x_ref, filt_ref, w_ref, skip_ref, sems = refs[11 + 2 * TABLES :]
    x_hbm, cot_hbm, filt_hbm, w_hbm, skip_hbm = sources[:5]
    pairs = [(w_hbm, w_ref)]
    pairs += [(x_hbm.at[stream], x_ref.at[stream]) for stream in (1, 2, 0)]
    pairs += [(cot_hbm, cot_ref), (filt_hbm, filt_ref), (skip_hbm, skip_ref)]
    pairs += list(zip(sources[5:], tables_here))
    copies = [
        pltpu.make_async_copy(source, target, sems.at[number])
        for number, (source, target) in enumerate(pairs)
    ]
    for copy in copies:
        copy.start()
    lines = Lines(scratch, IN_ROWS)
    pieces = lines.count
    member = place_ref[0]
    blank = jnp.zeros((pieces, LANES), F32)
    lane = lane_numbers(blank)
    rims = [blank, blank]

    def inner_part(value):
        return jnp.concatenate(
            [jnp.where(lane < RIM, 0.0, value[:, :LANES]), value[:, LANES:]], axis=1
        )

    copies[0].wait()
    for stream in range(3):
        spread_ref[stream] = spread_taps(w_ref[stream])
    for number, stream in ((1, 1), (2, 2), (3, 0)):
        copies[number].wait()
        for start in range(0, 2 * pieces, CHUNK):
            rows = slice(start, start + CHUNK)
            signal = x_ref[stream, rows, :].astype(F32)
            feat_ref[stream, rows, :] = inner_featured(signal, spread_ref[stream, rows, :])
        for side in range(2):
            signal = x_ref[stream, side * pieces : (side + 1) * pieces, :].astype(F32)
            ends = jnp.where(lane < RIM, signal[:, :LANES], signal[:, LANES:])
            first = 2 * RIM * (stream * 2 + side)
            rims[side] = put_lanes(rims[side], first, 2 * RIM, ends, LANES - RIM)
    tops = []
    for side in range(2):
        rows = slice(side * pieces, (side + 1) * pieces)
        product = inner_part(feat_ref[1, rows, :] * feat_ref[2, rows, :])
        code, top = encoded(exchanged(product, member, owners))
        lines.put_block(IN_PROD + 2 * side, code)
        tops.append(top)
    copies[4].wait()
    for side in range(2):
        rows = slice(side * pieces, (side + 1) * pieces)
        cot = cot_ref[rows, :]
        code, top = encoded(exchanged(inner_part(feat_ref[0, rows, :] * cot), member, owners))
        lines.put_block(IN_MIXED + 2 * side, code)
        tops.append(top)
        high = cot[:, :LANES].astype(BF16).astype(F32)
        both = jnp.where(lane < RIM, high, rolled(cot[:, :LANES] - high, RIM))
        rims[side] = put_lanes(rims[side], COT_LANE + 2 * RIM * side, 2 * RIM, both)
    copies[5].wait()
    code, top = encoded(filt_ref[...])
    lines.put_block(IN_FILT, jnp.concatenate([code] * owners, axis=0))
    tops.append(jnp.concatenate([top] * owners, axis=0))
    rim = exchanged(rims[0] + rims[1], member, owners)
    lines.put(IN_RIM, in_lanes(tops, IN_TOP_LANE, rim))
    lines.put(IN_RIM + 1, blank)
    out_ref[...] = scratch[...].astype(BF16)
    copies[6].wait()
    own_ref[...] = own_lanes(w_ref, skip_ref[...], place_ref[1])
    column = jnp.transpose(jnp.broadcast_to(skip_ref[...], (8, LANES)))[:, 0:1]
    wide_ref[...] = jnp.broadcast_to(column, wide_ref.shape)
    for copy in copies[7:]:
        copy.wait()


def turned(re, im, twiddle):
    turn_re, turn_im = twiddle
    return re * turn_re - im * turn_im, re * turn_im + im * turn_re


def parted(re, im, middle):
    half = re.shape[1] // 2
    even = jnp.concatenate([re[:, :half] + re[:, half:], im[:, :half] + im[:, half:]], axis=1)
    odd = turned(re[:, :half] - re[:, half:], im[:, :half] - im[:, half:], middle)
    return jnp.concatenate([even, jnp.concatenate(odd, axis=1)], axis=0)


def joined(pair, middle):
    count, half = pair.shape[0] // 2, pair.shape[1] // 2
    re, im = pair[:count, :half], pair[:count, half:]
    turn_re, turn_im = turned(pair[count:, :half], pair[count:, half:], middle)
    whole_re = jnp.concatenate([re + turn_re, re - turn_re], axis=1)
    return whole_re, jnp.concatenate([im + turn_im, im - turn_im], axis=1)


def spectrum(columns, twiddle, middle, count):
    re, im = turned(columns[:count], columns[count:], twiddle)
    return parted(re, im, middle)


def upright(spectra, inner, twiddle, middle, count):
    inside = product3(split(spectra), inner)
    columns = []
    for start in range(0, spectra.shape[0], 2 * count):
        re, im = joined(inside[start : start + 2 * count], middle)
        columns.append(jnp.concatenate(turned(re, im, twiddle), axis=0))
    return jnp.concatenate(columns, axis=1)


def halved_lanes(value):
    high = value.astype(BF16).astype(F32)
    lane = lane_numbers(value)
    both = jnp.where(lane % (2 * RIM) < RIM, high, rolled(value - high, RIM))
    return jnp.where(lane < 12 * RIM, both, 0.0)


def forward_kernel(
    r_ref,
    w_ref,
    outer_hi,
    outer_lo,
    back_hi,
    back_lo,
    twiddle_ref,
    inner_hi,
    inner_lo,
    cross_ref,
    spec_ref,
    kept_ref,
    scratch,
    cross_scratch,
):
    scratch[...] = r_ref[...].astype(F32)
    lines = Lines(scratch, IN_ROWS)
    cross = Lines(cross_scratch, CROSS_ROWS)
    pieces = lines.count
    count = 2 * pieces
    length = 2 * LANES
    rim = lines.get(IN_RIM)
    tops = [rim[:, IN_TOP_LANE + place : IN_TOP_LANE + place + 1] for place in range(5)]
    lane = lane_numbers(rim)
    row_number = lax.broadcasted_iota(jnp.int32, rim.shape, 0)
    before = jnp.where(row_number == 0, 0.0, pltpu.roll(rim, 1, 0))
    ends = jnp.where(lane % (2 * RIM) < RIM, before, rim)
    head = jnp.zeros_like(rim)
    for offset in range(TAPS):
        head = head + w_ref[offset : offset + 1, :] * rolled(ends, offset - RIM)
    side_lanes = 2 * RIM
    head_key, head_value = rolled(head, -2 * side_lanes), rolled(head, -4 * side_lanes)
    head_cot = rolled(rim + rolled(rim, -RIM), -COT_LANE)
    head_prod, head_mixed = head_key * head_value, head_cot * head
    for place, array in enumerate((head, head_prod, head_mixed, head_key, head_value, head_cot)):
        kept_ref[place] = array

    def whole(row, top, first):
        value = decoded(lines.get_block(row), top)
        return jnp.concatenate([jnp.where(lane < RIM, first, value[:, :LANES]), value[:, LANES:]], axis=1)

    prod, mixed = [], []
    for side in range(2):
        shift = -side_lanes * side
        prod.append(whole(IN_PROD + 2 * side, tops[side], rolled(head_prod, shift)))
        mixed.append(whole(IN_MIXED + 2 * side, tops[2 + side], rolled(head_mixed, shift)))

    signals = jnp.concatenate(
        [jnp.concatenate(prod, axis=0), jnp.concatenate(mixed, axis=0)], axis=1
    )
    twiddle = (twiddle_ref[0, :count], twiddle_ref[1, :count])
    middle = tuple(twiddle_ref[place, count : count + 1, :LANES] for place in range(2))
    spread = product3((outer_hi[...], outer_lo[...]), split(signals))
    parts = [
        spectrum(spread[:, start : start + length], twiddle, middle, count) for start in (0, length)
    ]
    inner = (inner_hi[...], inner_lo[...])
    spectra = product3(split(jnp.concatenate(parts, axis=0)), inner)
    spec_ref[...] = spectra
    z_re, z_im = spectra[:length, :LANES], spectra[:length, LANES:]
    m_re, m_im = spectra[length:, :LANES], spectra[length:, LANES:]
    tail = jnp.concatenate([z_re * m_re + z_im * m_im, z_im * m_re - z_re * m_im], axis=1)
    columns = upright(tail, inner, twiddle, middle, count)
    partial = product3((back_hi[:pieces, :], back_lo[:pieces, :]), split(columns))
    code, top = encoded(partial)
    cross.put_block(CROSS_GRAD, code)
    cross.put_block(CROSS_FILT, lines.get_block(IN_FILT))
    blank = jnp.zeros((pieces, LANES), F32)
    cross.put(CROSS_TOPS, in_lanes([tops[4], top], 0, blank))
    cross_ref[...] = cross_scratch[...].astype(BF16)


def inverse_kernel(
    cross_ref,
    spec_ref,
    kept_ref,
    w_ref,
    outer_hi,
    outer_lo,
    back_hi,
    back_lo,
    twiddle_ref,
    inner_hi,
    inner_lo,
    out_ref,
    cross_scratch,
    scratch,
):
    cross_scratch[...] = cross_ref[...].astype(F32)
    cross = Lines(cross_scratch, CROSS_ROWS)
    lines = Lines(scratch, OUT_ROWS)
    pieces = lines.count
    count = 2 * pieces
    length = 2 * LANES
    tops = cross.get(CROSS_TOPS)
    filt = decoded(cross.get_block(CROSS_FILT), tops[:, 0:1])
    inner = (inner_hi[...], inner_lo[...])
    twiddle = (twiddle_ref[0, :count], twiddle_ref[1, :count])
    middle = tuple(twiddle_ref[place, count : count + 1, :LANES] for place in range(2))
    spread = product3((outer_hi[:, :pieces], outer_lo[:, :pieces]), split(filt))
    spectra = product3(split(spectrum(spread, twiddle, middle, count)), inner)
    f_re, f_im = spectra[:, :LANES], spectra[:, LANES:]
    z_re, z_im = spec_ref[:length, :LANES], spec_ref[:length, LANES:]
    m_re, m_im = spec_ref[length:, :LANES], spec_ref[length:, LANES:]
    long_pair = jnp.concatenate(
        [z_re * f_re - z_im * f_im, -(z_re * f_im + z_im * f_re)], axis=1
    )
    grad_pair = jnp.concatenate([m_re * f_re + m_im * f_im, m_re * f_im - m_im * f_re], axis=1)
    columns = upright(
        jnp.concatenate([long_pair, grad_pair], axis=0), inner, twiddle, middle, count
    )
    restored = product3((back_hi[...], back_lo[...]), split(columns))
    side_lanes = 2 * RIM
    blank = jnp.zeros((pieces, LANES), F32)
    heads = {OUT_LONG: blank, OUT_GRAD: blank}
    out_tops = []
    for row, columns in ((OUT_LONG, slice(0, length)), (OUT_GRAD, slice(length, 2 * length))):
        for side in range(2):
            value = restored[side * pieces : (side + 1) * pieces, columns]
            code, top = encoded(value)
            lines.put_block(row + 2 * side, code)
            out_tops.append(top)
            heads[row] = put_lanes(heads[row], side_lanes * side, RIM, value[:, :LANES])
    head, prod, mixed, key, value, cot = [kept_ref[place] for place in range(6)]
    skip = w_ref[TAPS : TAPS + 1, :]
    grad_query = cot * (heads[OUT_LONG] + skip * prod)
    grad_product = heads[OUT_GRAD] + skip * mixed
    rim = put_lanes(blank, 0, 2 * side_lanes, grad_query)
    rim = put_lanes(rim, 2 * side_lanes, 2 * side_lanes, grad_product * value)
    rim = put_lanes(rim, 4 * side_lanes, 2 * side_lanes, grad_product * key)
    row_number = lax.broadcasted_iota(jnp.int32, rim.shape, 0)
    rim = jnp.where(row_number == pieces - 1, 0.0, pltpu.roll(rim, pieces - 1, 0))
    lines.put_block(OUT_FILT, cross.get_block(CROSS_GRAD))
    lines.put(OUT_RIM, in_lanes([*out_tops, tops[:, 1:2]], TOP_LANE, halved_lanes(rim)))
    lines.put(OUT_HEAD, halved_lanes(head))
    out_ref[...] = scratch[...].astype(BF16)


def local_kernel(
    owners,
    r_ref,
    place_ref,
    feat_ref,
    w_ref,
    skip_ref,
    cot_ref,
    out_ref,
    grad_ref,
    tail_ref,
    scratch,
    out_room,
    grad_room,
    tail_room,
    sems,
):
    member = place_ref[0]
    scratch[...] = r_ref[...].astype(F32)
    lines = Lines(scratch, OUT_ROWS)
    pieces = lines.count
    copies = []

    def send(source, target):
        copy = pltpu.make_async_copy(source, target, sems.at[len(copies)])
        copy.start()
        copies.append(copy)

    def block(row, top_place):
        return decoded(lines.get_block(row), tops[:, TOP_LANE + top_place : TOP_LANE + top_place + 1])

    tops = lines.get(OUT_RIM)
    rim = exchanged(tops, member, owners)
    rim = rim + pltpu.roll(rim, LANES - RIM, 1)
    head = exchanged(lines.get(OUT_HEAD), member, owners)
    head = head + pltpu.roll(head, LANES - RIM, 1)
    lane = lax.broadcasted_iota(jnp.int32, (pieces, LANES), 1)

    def first_lanes(array, place):
        return rolled(array, -2 * RIM * place)

    partial = block(OUT_FILT, 4)
    owned = pieces // owners
    total = partial[:owned]
    for place in range(1, owners):
        total = total + partial[place * owned : (place + 1) * owned]
    tail_room[...] = total
    send(tail_room, tail_ref)
    lane = lane[:CHUNK]
    for side in range(2):
        long_out = exchanged(block(OUT_LONG + 2 * side, side), member, owners)
        grad_long = exchanged(block(OUT_GRAD + 2 * side, 2 + side), member, owners)
        lefts = [first_lanes(head, stream * 2 + side) for stream in range(3)]
        afters = [first_lanes(rim, stream * 2 + side) for stream in range(3)]
        for start in range(0, pieces, CHUNK):
            part = slice(start, start + CHUNK)
            rows = slice(side * pieces + start, side * pieces + start + CHUNK)
            featured = []
            for stream in range(3):
                inside = feat_ref[stream, rows, :]
                left = jnp.where(lane < RIM, lefts[stream][part], inside[:, :LANES])
                featured.append(jnp.concatenate([left, inside[:, LANES:]], axis=1))
            query, key, value = featured
            cot = cot_ref[rows, :]
            skip = jnp.concatenate([skip_ref[rows, :]] * 2, axis=1)
            mixer = long_out[part] + skip * (key * value)
            out_room[rows, :] = query * mixer
            grad_product = grad_long[part] + skip * (cot * query)
            for stream, grad in enumerate((cot * mixer, grad_product * value, grad_product * key)):
                after = afters[stream][part]
                near, far = grad[:, :LANES], grad[:, LANES:]
                weight = w_ref[stream, rows, :LANES]
                total_near, total_far = weight * near, weight * far
                for offset in range(1, TAPS):
                    weight = w_ref[stream, rows, offset * LANES : (offset + 1) * LANES]
                    wrapped = lane < offset
                    moved = rolled(jnp.where(wrapped, far, near), -offset)
                    total_near = total_near + weight * moved
                    moved = rolled(jnp.where(wrapped, after, far), -offset)
                    total_far = total_far + weight * moved
                grad_room[stream, rows, :LANES] = total_near
                grad_room[stream, rows, LANES:] = total_far
        rows = slice(side * pieces, (side + 1) * pieces)
        send(out_room.at[rows, :], out_ref.at[rows, :])
        for stream in range(3):
            send(grad_room.at[stream, rows, :], grad_ref.at[stream, rows, :])
    for copy in copies:
        copy.wait()


VMEM_SPEC = pl.BlockSpec(memory_space=pltpu.VMEM)
SMEM_SPEC = pl.BlockSpec(memory_space=pltpu.SMEM)
ANY_SPEC = pl.BlockSpec(memory_space=pl.ANY)
HBM_SPEC = pl.BlockSpec(memory_space=pltpu.HBM)


def call(
    kernel, out_shape, operands, scratch=(), specs=None, flops=0, out_spec=VMEM_SPEC, room_mib=24
):
    specs = specs or {}
    return pl.pallas_call(
        kernel,
        out_shape=out_shape,
        in_specs=[specs.get(place, VMEM_SPEC) for place in range(len(operands))],
        out_specs=jax.tree.map(lambda _: out_spec, out_shape),
        scratch_shapes=list(scratch),
        compiler_params=pltpu.CompilerParams(vmem_limit_bytes=room_mib << 20),
        cost_estimate=pl.CostEstimate(flops=flops, bytes_accessed=1 << 20, transcendentals=0),
    )(*operands)


def shards(inputs, short_weight, skip, filters, cotangent):
    pieces = lax.axis_size("ctx")
    owners = lax.axis_size("ch")
    position = lax.axis_index("ctx")
    member = lax.axis_index("ch")
    _, channels, length = inputs.shape
    owned = filters.shape[0]
    count = 2 * pieces
    scale = 1.0 / math.sqrt(pieces * length)

    def shape(*dims, dtype=F32):
        return jax.ShapeDtypeStruct(dims, dtype)

    def room(rows):
        return pltpu.VMEM((pieces * rows, LANES), F32)

    def transposed(array):
        rows = array.shape[0] // pieces
        array = lax.all_to_all(array.reshape(pieces, rows // 2, 2, LANES), "ctx", 0, 0)
        return array.reshape(pieces * rows, LANES)

    group = ((position // owned) ^ member) * owned + position % owned
    place = jnp.stack([member, group]).astype(jnp.int32)
    taps = jnp.transpose(short_weight, (0, 2, 1))
    skip_row = skip[None]
    constants = [jnp.asarray(table) for table in tables(pieces, length, scale)]
    arguments = (inputs, cotangent, filters, taps, skip_row, *constants)
    sent, own, featured, spread, skip_wide, cot, *constants = call(
        functools.partial(pack_kernel, owners),
        (
            shape(pieces * IN_ROWS, LANES, dtype=BF16),
            shape(8, LANES),
            shape(3, channels, length),
            shape(3, channels, TAPS * LANES),
            shape(channels, LANES),
            shape(channels, length),
            *(shape(*table.shape, dtype=table.dtype) for table in constants),
        ),
        (place, *(pltpu.with_memory_space_constraint(array, pltpu.HBM) for array in arguments)),
        [
            room(IN_ROWS),
            pltpu.VMEM(inputs.shape, BF16),
            pltpu.VMEM(filters.shape, F32),
            pltpu.VMEM(taps.shape, F32),
            pltpu.VMEM(skip_row.shape, F32),
            pltpu.SemaphoreType.DMA((7 + TABLES,)),
        ],
        specs={0: SMEM_SPEC, **{operand: HBM_SPEC for operand in range(1, 6 + TABLES)}},
    )
    received = transposed(sent)
    cross, spectra, kept = call(
        forward_kernel,
        (
            shape(pieces * CROSS_ROWS, LANES, dtype=BF16),
            shape(2 * length, length),
            shape(6, pieces, LANES),
        ),
        (received, own, *constants),
        [room(IN_ROWS), room(CROSS_ROWS)],
        flops=800000000,
    )
    partners = [
        (place * owners + shard, place * owners + (shard ^ (place // owned)))
        for place in range(pieces)
        for shard in range(owners)
    ]
    cross = lax.ppermute(cross, ("ctx", "ch"), partners)
    sent = call(
        inverse_kernel,
        shape(pieces * OUT_ROWS, LANES, dtype=BF16),
        (cross, spectra, kept, own, *constants),
        [room(CROSS_ROWS), room(OUT_ROWS)],
        flops=800000000,
    )
    received = transposed(sent)

    return call(
        functools.partial(local_kernel, owners),
        (shape(channels, length), shape(3, channels, length), shape(owned, length)),
        (received, place, featured, spread, skip_wide, cot),
        [
            room(OUT_ROWS),
            pltpu.VMEM((channels, length), F32),
            pltpu.VMEM((3, channels, length), F32),
            pltpu.VMEM((owned, length), F32),
            pltpu.SemaphoreType.DMA((9,)),
        ],
        specs={1: SMEM_SPEC},
        out_spec=ANY_SPEC,
    )


def solution(mesh):
    in_specs = (P(None, "ch", "ctx"), P(None, "ch", None), P("ch"), P("ch", "ctx"), P("ch", "ctx"))
    out_specs = (P("ch", "ctx"), P(None, "ch", "ctx"), P("ch", "ctx"))
    return jax.shard_map(shards, mesh=mesh, in_specs=in_specs, out_specs=out_specs, check_vma=False)
```

```python
import functools
import math

import jax
import jax.numpy as jnp
import ml_dtypes
import numpy as np
from jax import lax
from jax.experimental import pallas as pl
from jax.experimental.pallas import tpu as pltpu
from jax.sharding import PartitionSpec as P

BF16 = jnp.bfloat16
F32 = jnp.float32
LANES = 128
TAPS = 7
IN_PROD, IN_MIXED, IN_FILT, IN_RIM, IN_ROWS = 0, 4, 8, 10, 12
CROSS_FILT, CROSS_GRAD, CROSS_TOPS, CROSS_ROWS = 0, 2, 4, 5
OUT_LONG, OUT_GRAD, OUT_FILT, OUT_RIM, OUT_HEAD, OUT_ROWS = 0, 4, 8, 10, 11, 12
RIM = TAPS - 1
COT_LANE = 12 * RIM
IN_TOP_LANE = 16 * RIM
TOP_LANE = 12 * RIM
REACH = 125.0
TABLES = 7
CHUNK = 16


def halves(array):
    array = np.asarray(array, np.float32)
    high = array.astype(ml_dtypes.bfloat16)
    low = (array - high.astype(np.float32)).astype(ml_dtypes.bfloat16)
    return high, low


@functools.lru_cache(maxsize=None)
def tables(pieces, length, scale):
    blocks = 2 * pieces
    total = blocks * length
    freq = np.arange(blocks)[:, None]
    angle = 2.0 * np.pi * ((freq * np.arange(pieces)[None, :]) % blocks) / blocks
    cos, sin = np.cos(angle), np.sin(angle)
    outer = np.block([[cos, sin], [-sin, cos]])
    back = np.block([[cos.T, sin.T], [sin.T, -cos.T]]) * (scale / total)
    angle = 2.0 * np.pi * ((freq * np.arange(length)[None, :]) % total) / total
    twiddle = np.stack([np.cos(angle), -np.sin(angle)]).astype(np.float32)
    angle = 2.0 * np.pi * np.arange(length // 2) / length
    middle = np.zeros((2, 8, length), np.float32)
    middle[:, 0, : length // 2] = np.stack([np.cos(angle), -np.sin(angle)])
    twiddle = np.concatenate([twiddle, middle], axis=1)
    count = np.arange(length // 2)
    angle = 2.0 * np.pi * ((count[:, None] * count[None, :]) % (length // 2)) / (length // 2)
    cos, sin = np.cos(angle), np.sin(angle)
    inner = np.block([[cos, -sin], [sin, cos]])
    return (*halves(outer), *halves(back), twiddle, *halves(inner))


def split(value):
    high = value.astype(BF16)
    return high, (value - high.astype(F32)).astype(BF16)


def product3(left, right):
    left = jnp.concatenate([left[0], left[1], left[0]], axis=1)
    right = jnp.concatenate([right[0], right[0], right[1]], axis=0)
    parts = [
        jnp.dot(left[start : start + LANES], right, preferred_element_type=F32)
        for start in range(0, left.shape[0], LANES)
    ]
    return jnp.concatenate(parts, axis=0)


def encoded(value):
    top = jnp.max(jnp.abs(value), axis=1, keepdims=True)
    top = (jnp.maximum(top, 1e-30) * 1.008).astype(BF16).astype(F32)
    square = jnp.abs(value) * (1.0 / top)
    size = square * lax.rsqrt(jnp.maximum(square, 1e-30))
    code = jnp.exp2(size * (2.0 * REACH) - REACH)
    return jnp.where(value < 0.0, -code, code), top


def decoded(code, top):
    size = (jnp.log2(jnp.abs(code)) + REACH) * (0.5 / REACH)
    value = size * size * top
    return jnp.where(code < 0.0, -value, value)


class Lines:
    def __init__(self, ref, rows):
        self.ref, self.rows = ref, rows
        self.count = ref.shape[0] // rows

    def get(self, row):
        return self.ref[pl.ds(row, self.count, stride=self.rows), :]

    def put(self, row, value):
        self.ref[pl.ds(row, self.count, stride=self.rows), :] = value

    def get_block(self, row):
        return jnp.concatenate([self.get(row), self.get(row + 1)], axis=1)

    def put_block(self, row, value):
        self.put(row, value[:, :LANES])
        self.put(row + 1, value[:, LANES:])


def in_lanes(columns, first, like):
    lane = lax.broadcasted_iota(jnp.int32, like.shape, 1)
    for place, column in enumerate(columns):
        like = jnp.where(lane == first + place, column, like)
    return like


def exchanged(value, member, owners):
    size = value.shape[0] // owners
    step = 1
    while step < owners:
        order = [place ^ step for place in range(owners)]
        swapped = jnp.concatenate([value[k * size : (k + 1) * size] for k in order], axis=0)
        value = jnp.where((member & step) != 0, swapped, value)
        step *= 2
    return value


def rolled(value, lanes):
    lanes %= value.shape[1]
    return pltpu.roll(value, lanes, 1) if lanes else value


def lane_numbers(like):
    return lax.broadcasted_iota(jnp.int32, like.shape, 1)


def put_lanes(target, first, count, value, start=0):
    lane = lane_numbers(target)
    inside = (lane >= first) & (lane < first + count)
    return jnp.where(inside, rolled(value, first - start), target)


def eight_rows(taps):
    return jnp.concatenate([taps, jnp.zeros((8 - TAPS, taps.shape[1]), F32)], axis=0)


def spread_taps(taps):
    rest = eight_rows(taps)
    parts = []
    for _ in range(3):
        parts.append(rest.astype(BF16).astype(F32))
        rest = rest - parts[-1]
    columns = jnp.transpose(jnp.concatenate(parts, axis=0)).astype(BF16)
    shape = (24, TAPS * LANES)
    first = lax.broadcasted_iota(jnp.int32, shape, 0) % 8 * LANES
    lane = lax.broadcasted_iota(jnp.int32, shape, 1)
    chosen = jnp.where((lane >= first) & (lane < first + LANES), 1.0, 0.0).astype(BF16)
    return jnp.dot(columns, chosen, preferred_element_type=F32)


def inner_featured(signal, spread):
    near, far = signal[:, :LANES], signal[:, LANES:]
    lane = lane_numbers(near)
    weight = spread[:, :LANES]
    total_near, total_far = weight * near, weight * far
    for offset in range(1, TAPS):
        weight = spread[:, offset * LANES : (offset + 1) * LANES]
        wrapped = jnp.where(lane >= LANES - offset, near, far)
        total_near = total_near + weight * rolled(near, offset)
        total_far = total_far + weight * rolled(wrapped, offset)
    return jnp.concatenate([total_near, total_far], axis=1)


def own_lanes(taps_ref, skip, group):
    lane = lax.broadcasted_iota(jnp.int32, (8, LANES), 1)
    row = lax.broadcasted_iota(jnp.int32, (8, LANES), 0)
    pieces = LANES // 2
    own = jnp.zeros((8, LANES), F32)
    skips = jnp.broadcast_to(skip, (8, LANES))
    for side in range(2):
        here = lane == group + side * pieces
        value = jnp.sum(jnp.where(here, skips, 0.0), axis=1, keepdims=True)
        first = 2 * RIM * side
        own = jnp.where((row == TAPS) & (lane >= first) & (lane < first + RIM), value, own)
        for stream in range(3):
            value = jnp.sum(
                jnp.where(here, eight_rows(taps_ref[stream]), 0.0), axis=1, keepdims=True
            )
            first = 2 * RIM * (stream * 2 + side)
            own = jnp.where((row < TAPS) & (lane >= first) & (lane < first + RIM), value, own)
    return own


def pack_kernel(owners, *refs):
    sources = refs[: 5 + TABLES]
    out_ref, own_ref, feat_ref, spread_ref, wide_ref, cot_ref = refs[5 + TABLES : 11 + TABLES]
    tables_here = refs[11 + TABLES : 11 + 2 * TABLES]
    scratch, x_ref, filt_ref, w_ref, skip_ref, sems = refs[11 + 2 * TABLES :]
    x_hbm, cot_hbm, filt_hbm, w_hbm, skip_hbm = sources[:5]
    pairs = [(w_hbm, w_ref)]
    pairs += [(x_hbm.at[stream], x_ref.at[stream]) for stream in (1, 2, 0)]
    pairs += [(cot_hbm, cot_ref), (filt_hbm, filt_ref), (skip_hbm, skip_ref)]
    pairs += list(zip(sources[5:], tables_here))
    copies = [
        pltpu.make_async_copy(source, target, sems.at[number])
        for number, (source, target) in enumerate(pairs)
    ]
    for copy in copies:
        copy.start()
    lines = Lines(scratch, IN_ROWS)
    pieces = lines.count
    member = lax.axis_index("ch")
    position = lax.axis_index("ctx")
    owned = pieces // owners
    group = ((position // owned) ^ member) * owned + position % owned
    blank = jnp.zeros((pieces, LANES), F32)
    lane = lane_numbers(blank)
    rims = [blank, blank]

    def inner_part(value):
        return jnp.concatenate(
            [jnp.where(lane < RIM, 0.0, value[:, :LANES]), value[:, LANES:]], axis=1
        )

    copies[0].wait()
    for stream in range(3):
        spread_ref[stream] = spread_taps(w_ref[stream])
    for number, stream in ((1, 1), (2, 2), (3, 0)):
        copies[number].wait()
        for start in range(0, 2 * pieces, CHUNK):
            rows = slice(start, start + CHUNK)
            signal = x_ref[stream, rows, :].astype(F32)
            feat_ref[stream, rows, :] = inner_featured(signal, spread_ref[stream, rows, :])
        for side in range(2):
            signal = x_ref[stream, side * pieces : (side + 1) * pieces, :].astype(F32)
            ends = jnp.where(lane < RIM, signal[:, :LANES], signal[:, LANES:])
            first = 2 * RIM * (stream * 2 + side)
            rims[side] = put_lanes(rims[side], first, 2 * RIM, ends, LANES - RIM)
    tops = []
    for side in range(2):
        rows = slice(side * pieces, (side + 1) * pieces)
        product = inner_part(feat_ref[1, rows, :] * feat_ref[2, rows, :])
        code, top = encoded(exchanged(product, member, owners))
        lines.put_block(IN_PROD + 2 * side, code)
        tops.append(top)
    copies[4].wait()
    for side in range(2):
        rows = slice(side * pieces, (side + 1) * pieces)
        cot = cot_ref[rows, :]
        code, top = encoded(exchanged(inner_part(feat_ref[0, rows, :] * cot), member, owners))
        lines.put_block(IN_MIXED + 2 * side, code)
        tops.append(top)
        high = cot[:, :LANES].astype(BF16).astype(F32)
        both = jnp.where(lane < RIM, high, rolled(cot[:, :LANES] - high, RIM))
        rims[side] = put_lanes(rims[side], COT_LANE + 2 * RIM * side, 2 * RIM, both)
    copies[5].wait()
    code, top = encoded(filt_ref[...])
    lines.put_block(IN_FILT, jnp.concatenate([code] * owners, axis=0))
    tops.append(jnp.concatenate([top] * owners, axis=0))
    rim = exchanged(rims[0] + rims[1], member, owners)
    lines.put(IN_RIM, in_lanes(tops, IN_TOP_LANE, rim))
    lines.put(IN_RIM + 1, blank)
    out_ref[...] = scratch[...].astype(BF16)
    copies[6].wait()
    own_ref[...] = own_lanes(w_ref, skip_ref[...], group)
    column = jnp.transpose(jnp.broadcast_to(skip_ref[...], (8, LANES)))[:, 0:1]
    wide_ref[...] = jnp.broadcast_to(column, wide_ref.shape)
    for copy in copies[7:]:
        copy.wait()


def turned(re, im, twiddle):
    turn_re, turn_im = twiddle
    return re * turn_re - im * turn_im, re * turn_im + im * turn_re


def parted(re, im, middle):
    half = re.shape[1] // 2
    even = jnp.concatenate([re[:, :half] + re[:, half:], im[:, :half] + im[:, half:]], axis=1)
    odd = turned(re[:, :half] - re[:, half:], im[:, :half] - im[:, half:], middle)
    return jnp.concatenate([even, jnp.concatenate(odd, axis=1)], axis=0)


def joined(pair, middle):
    count, half = pair.shape[0] // 2, pair.shape[1] // 2
    re, im = pair[:count, :half], pair[:count, half:]
    turn_re, turn_im = turned(pair[count:, :half], pair[count:, half:], middle)
    whole_re = jnp.concatenate([re + turn_re, re - turn_re], axis=1)
    return whole_re, jnp.concatenate([im + turn_im, im - turn_im], axis=1)


def spectrum(columns, twiddle, middle, count):
    re, im = turned(columns[:count], columns[count:], twiddle)
    return parted(re, im, middle)


def upright(spectra, inner, twiddle, middle, count):
    inside = product3(split(spectra), inner)
    columns = []
    for start in range(0, spectra.shape[0], 2 * count):
        re, im = joined(inside[start : start + 2 * count], middle)
        columns.append(jnp.concatenate(turned(re, im, twiddle), axis=0))
    return jnp.concatenate(columns, axis=1)


def halved_lanes(value):
    high = value.astype(BF16).astype(F32)
    lane = lane_numbers(value)
    both = jnp.where(lane % (2 * RIM) < RIM, high, rolled(value - high, RIM))
    return jnp.where(lane < 12 * RIM, both, 0.0)


def forward_kernel(
    r_ref,
    w_ref,
    outer_hi,
    outer_lo,
    back_hi,
    back_lo,
    twiddle_ref,
    inner_hi,
    inner_lo,
    cross_ref,
    spec_ref,
    kept_ref,
    scratch,
    cross_scratch,
):
    scratch[...] = r_ref[...].astype(F32)
    lines = Lines(scratch, IN_ROWS)
    cross = Lines(cross_scratch, CROSS_ROWS)
    pieces = lines.count
    count = 2 * pieces
    length = 2 * LANES
    rim = lines.get(IN_RIM)
    tops = [rim[:, IN_TOP_LANE + place : IN_TOP_LANE + place + 1] for place in range(5)]
    lane = lane_numbers(rim)
    row_number = lax.broadcasted_iota(jnp.int32, rim.shape, 0)
    before = jnp.where(row_number == 0, 0.0, pltpu.roll(rim, 1, 0))
    ends = jnp.where(lane % (2 * RIM) < RIM, before, rim)
    head = jnp.zeros_like(rim)
    for offset in range(TAPS):
        head = head + w_ref[offset : offset + 1, :] * rolled(ends, offset - RIM)
    side_lanes = 2 * RIM
    head_key, head_value = rolled(head, -2 * side_lanes), rolled(head, -4 * side_lanes)
    head_cot = rolled(rim + rolled(rim, -RIM), -COT_LANE)
    head_prod, head_mixed = head_key * head_value, head_cot * head
    for place, array in enumerate((head, head_prod, head_mixed, head_key, head_value, head_cot)):
        kept_ref[place] = array

    def whole(row, top, first):
        value = decoded(lines.get_block(row), top)
        return jnp.concatenate([jnp.where(lane < RIM, first, value[:, :LANES]), value[:, LANES:]], axis=1)

    prod, mixed = [], []
    for side in range(2):
        shift = -side_lanes * side
        prod.append(whole(IN_PROD + 2 * side, tops[side], rolled(head_prod, shift)))
        mixed.append(whole(IN_MIXED + 2 * side, tops[2 + side], rolled(head_mixed, shift)))

    signals = jnp.concatenate(
        [jnp.concatenate(prod, axis=0), jnp.concatenate(mixed, axis=0)], axis=1
    )
    twiddle = (twiddle_ref[0, :count], twiddle_ref[1, :count])
    middle = tuple(twiddle_ref[place, count : count + 1, :LANES] for place in range(2))
    spread = product3((outer_hi[...], outer_lo[...]), split(signals))
    parts = [
        spectrum(spread[:, start : start + length], twiddle, middle, count) for start in (0, length)
    ]
    inner = (inner_hi[...], inner_lo[...])
    spectra = product3(split(jnp.concatenate(parts, axis=0)), inner)
    spec_ref[...] = spectra
    z_re, z_im = spectra[:length, :LANES], spectra[:length, LANES:]
    m_re, m_im = spectra[length:, :LANES], spectra[length:, LANES:]
    tail = jnp.concatenate([z_re * m_re + z_im * m_im, z_im * m_re - z_re * m_im], axis=1)
    columns = upright(tail, inner, twiddle, middle, count)
    partial = product3((back_hi[:pieces, :], back_lo[:pieces, :]), split(columns))
    code, top = encoded(partial)
    cross.put_block(CROSS_GRAD, code)
    cross.put_block(CROSS_FILT, lines.get_block(IN_FILT))
    blank = jnp.zeros((pieces, LANES), F32)
    cross.put(CROSS_TOPS, in_lanes([tops[4], top], 0, blank))
    cross_ref[...] = cross_scratch[...].astype(BF16)


def inverse_kernel(
    cross_ref,
    spec_ref,
    kept_ref,
    w_ref,
    outer_hi,
    outer_lo,
    back_hi,
    back_lo,
    twiddle_ref,
    inner_hi,
    inner_lo,
    out_ref,
    cross_scratch,
    scratch,
):
    cross_scratch[...] = cross_ref[...].astype(F32)
    cross = Lines(cross_scratch, CROSS_ROWS)
    lines = Lines(scratch, OUT_ROWS)
    pieces = lines.count
    count = 2 * pieces
    length = 2 * LANES
    tops = cross.get(CROSS_TOPS)
    filt = decoded(cross.get_block(CROSS_FILT), tops[:, 0:1])
    inner = (inner_hi[...], inner_lo[...])
    twiddle = (twiddle_ref[0, :count], twiddle_ref[1, :count])
    middle = tuple(twiddle_ref[place, count : count + 1, :LANES] for place in range(2))
    spread = product3((outer_hi[:, :pieces], outer_lo[:, :pieces]), split(filt))
    spectra = product3(split(spectrum(spread, twiddle, middle, count)), inner)
    f_re, f_im = spectra[:, :LANES], spectra[:, LANES:]
    z_re, z_im = spec_ref[:length, :LANES], spec_ref[:length, LANES:]
    m_re, m_im = spec_ref[length:, :LANES], spec_ref[length:, LANES:]
    long_pair = jnp.concatenate(
        [z_re * f_re - z_im * f_im, -(z_re * f_im + z_im * f_re)], axis=1
    )
    grad_pair = jnp.concatenate([m_re * f_re + m_im * f_im, m_re * f_im - m_im * f_re], axis=1)
    columns = upright(
        jnp.concatenate([long_pair, grad_pair], axis=0), inner, twiddle, middle, count
    )
    restored = product3((back_hi[...], back_lo[...]), split(columns))
    side_lanes = 2 * RIM
    blank = jnp.zeros((pieces, LANES), F32)
    heads = {OUT_LONG: blank, OUT_GRAD: blank}
    out_tops = []
    for row, columns in ((OUT_LONG, slice(0, length)), (OUT_GRAD, slice(length, 2 * length))):
        for side in range(2):
            value = restored[side * pieces : (side + 1) * pieces, columns]
            code, top = encoded(value)
            lines.put_block(row + 2 * side, code)
            out_tops.append(top)
            heads[row] = put_lanes(heads[row], side_lanes * side, RIM, value[:, :LANES])
    head, prod, mixed, key, value, cot = [kept_ref[place] for place in range(6)]
    skip = w_ref[TAPS : TAPS + 1, :]
    grad_query = cot * (heads[OUT_LONG] + skip * prod)
    grad_product = heads[OUT_GRAD] + skip * mixed
    rim = put_lanes(blank, 0, 2 * side_lanes, grad_query)
    rim = put_lanes(rim, 2 * side_lanes, 2 * side_lanes, grad_product * value)
    rim = put_lanes(rim, 4 * side_lanes, 2 * side_lanes, grad_product * key)
    row_number = lax.broadcasted_iota(jnp.int32, rim.shape, 0)
    rim = jnp.where(row_number == pieces - 1, 0.0, pltpu.roll(rim, pieces - 1, 0))
    lines.put_block(OUT_FILT, cross.get_block(CROSS_GRAD))
    lines.put(OUT_RIM, in_lanes([*out_tops, tops[:, 1:2]], TOP_LANE, halved_lanes(rim)))
    lines.put(OUT_HEAD, halved_lanes(head))
    out_ref[...] = scratch[...].astype(BF16)


def local_kernel(
    owners,
    r_ref,
    feat_ref,
    w_ref,
    skip_ref,
    cot_ref,
    out_ref,
    grad_ref,
    tail_ref,
    scratch,
    out_room,
    grad_room,
    tail_room,
    sems,
):
    member = lax.axis_index("ch")
    scratch[...] = r_ref[...].astype(F32)
    lines = Lines(scratch, OUT_ROWS)
    pieces = lines.count
    copies = []

    def send(source, target):
        copy = pltpu.make_async_copy(source, target, sems.at[len(copies)])
        copy.start()
        copies.append(copy)

    def block(row, top_place):
        return decoded(lines.get_block(row), tops[:, TOP_LANE + top_place : TOP_LANE + top_place + 1])

    tops = lines.get(OUT_RIM)
    rim = exchanged(tops, member, owners)
    rim = rim + pltpu.roll(rim, LANES - RIM, 1)
    head = exchanged(lines.get(OUT_HEAD), member, owners)
    head = head + pltpu.roll(head, LANES - RIM, 1)
    lane = lax.broadcasted_iota(jnp.int32, (pieces, LANES), 1)

    def first_lanes(array, place):
        return rolled(array, -2 * RIM * place)

    partial = block(OUT_FILT, 4)
    owned = pieces // owners
    total = partial[:owned]
    for place in range(1, owners):
        total = total + partial[place * owned : (place + 1) * owned]
    tail_room[...] = total
    send(tail_room, tail_ref)
    lane = lane[:CHUNK]
    for side in range(2):
        long_out = exchanged(block(OUT_LONG + 2 * side, side), member, owners)
        grad_long = exchanged(block(OUT_GRAD + 2 * side, 2 + side), member, owners)
        lefts = [first_lanes(head, stream * 2 + side) for stream in range(3)]
        afters = [first_lanes(rim, stream * 2 + side) for stream in range(3)]
        for start in range(0, pieces, CHUNK):
            part = slice(start, start + CHUNK)
            rows = slice(side * pieces + start, side * pieces + start + CHUNK)
            featured = []
            for stream in range(3):
                inside = feat_ref[stream, rows, :]
                left = jnp.where(lane < RIM, lefts[stream][part], inside[:, :LANES])
                featured.append(jnp.concatenate([left, inside[:, LANES:]], axis=1))
            query, key, value = featured
            cot = cot_ref[rows, :]
            skip = jnp.concatenate([skip_ref[rows, :]] * 2, axis=1)
            mixer = long_out[part] + skip * (key * value)
            out_room[rows, :] = query * mixer
            grad_product = grad_long[part] + skip * (cot * query)
            for stream, grad in enumerate((cot * mixer, grad_product * value, grad_product * key)):
                after = afters[stream][part]
                near, far = grad[:, :LANES], grad[:, LANES:]
                weight = w_ref[stream, rows, :LANES]
                total_near, total_far = weight * near, weight * far
                for offset in range(1, TAPS):
                    weight = w_ref[stream, rows, offset * LANES : (offset + 1) * LANES]
                    wrapped = lane < offset
                    moved = rolled(jnp.where(wrapped, far, near), -offset)
                    total_near = total_near + weight * moved
                    moved = rolled(jnp.where(wrapped, after, far), -offset)
                    total_far = total_far + weight * moved
                grad_room[stream, rows, :LANES] = total_near
                grad_room[stream, rows, LANES:] = total_far
        rows = slice(side * pieces, (side + 1) * pieces)
        send(out_room.at[rows, :], out_ref.at[rows, :])
        for stream in range(3):
            send(grad_room.at[stream, rows, :], grad_ref.at[stream, rows, :])
    for copy in copies:
        copy.wait()


VMEM_SPEC = pl.BlockSpec(memory_space=pltpu.VMEM)
ANY_SPEC = pl.BlockSpec(memory_space=pl.ANY)
HBM_SPEC = pl.BlockSpec(memory_space=pltpu.HBM)


def call(
    kernel, out_shape, operands, scratch=(), specs=None, flops=0, out_spec=VMEM_SPEC, room_mib=24
):
    specs = specs or {}
    return pl.pallas_call(
        kernel,
        out_shape=out_shape,
        in_specs=[specs.get(place, VMEM_SPEC) for place in range(len(operands))],
        out_specs=jax.tree.map(lambda _: out_spec, out_shape),
        scratch_shapes=list(scratch),
        compiler_params=pltpu.CompilerParams(vmem_limit_bytes=room_mib << 20),
        cost_estimate=pl.CostEstimate(flops=flops, bytes_accessed=1 << 20, transcendentals=0),
    )(*operands)


def shards(inputs, short_weight, skip, filters, cotangent):
    pieces = lax.axis_size("ctx")
    owners = lax.axis_size("ch")
    _, channels, length = inputs.shape
    owned = filters.shape[0]
    count = 2 * pieces
    scale = 1.0 / math.sqrt(pieces * length)

    def shape(*dims, dtype=F32):
        return jax.ShapeDtypeStruct(dims, dtype)

    def room(rows):
        return pltpu.VMEM((pieces * rows, LANES), F32)

    def transposed(array):
        rows = array.shape[0] // pieces
        array = lax.all_to_all(array.reshape(pieces, rows // 2, 2, LANES), "ctx", 0, 0)
        return array.reshape(pieces * rows, LANES)

    taps = jnp.transpose(short_weight, (0, 2, 1))
    skip_row = skip[None]
    constants = [jnp.asarray(table) for table in tables(pieces, length, scale)]
    arguments = (inputs, cotangent, filters, taps, skip_row, *constants)
    sent, own, featured, spread, skip_wide, cot, *constants = call(
        functools.partial(pack_kernel, owners),
        (
            shape(pieces * IN_ROWS, LANES, dtype=BF16),
            shape(8, LANES),
            shape(3, channels, length),
            shape(3, channels, TAPS * LANES),
            shape(channels, LANES),
            shape(channels, length),
            *(shape(*table.shape, dtype=table.dtype) for table in constants),
        ),
        [pltpu.with_memory_space_constraint(array, pltpu.HBM) for array in arguments],
        [
            room(IN_ROWS),
            pltpu.VMEM(inputs.shape, BF16),
            pltpu.VMEM(filters.shape, F32),
            pltpu.VMEM(taps.shape, F32),
            pltpu.VMEM(skip_row.shape, F32),
            pltpu.SemaphoreType.DMA((7 + TABLES,)),
        ],
        specs={operand: HBM_SPEC for operand in range(5 + TABLES)},
    )
    received = transposed(sent)
    cross, spectra, kept = call(
        forward_kernel,
        (
            shape(pieces * CROSS_ROWS, LANES, dtype=BF16),
            shape(2 * length, length),
            shape(6, pieces, LANES),
        ),
        (received, own, *constants),
        [room(IN_ROWS), room(CROSS_ROWS)],
        flops=800000000,
    )
    partners = [
        (place * owners + shard, place * owners + (shard ^ (place // owned)))
        for place in range(pieces)
        for shard in range(owners)
    ]
    cross = lax.ppermute(cross, ("ctx", "ch"), partners)
    sent = call(
        inverse_kernel,
        shape(pieces * OUT_ROWS, LANES, dtype=BF16),
        (cross, spectra, kept, own, *constants),
        [room(CROSS_ROWS), room(OUT_ROWS)],
        flops=800000000,
    )
    received = transposed(sent)

    return call(
        functools.partial(local_kernel, owners),
        (shape(channels, length), shape(3, channels, length), shape(owned, length)),
        (received, featured, spread, skip_wide, cot),
        [
            room(OUT_ROWS),
            pltpu.VMEM((channels, length), F32),
            pltpu.VMEM((3, channels, length), F32),
            pltpu.VMEM((owned, length), F32),
            pltpu.SemaphoreType.DMA((9,)),
        ],
        out_spec=ANY_SPEC,
    )


def solution(mesh):
    in_specs = (P(None, "ch", "ctx"), P(None, "ch", None), P("ch"), P("ch", "ctx"), P("ch", "ctx"))
    out_specs = (P("ch", "ctx"), P(None, "ch", "ctx"), P("ch", "ctx"))
    return jax.shard_map(shards, mesh=mesh, in_specs=in_specs, out_specs=out_specs, check_vma=False)
```

```python
import functools
import math

import jax
import jax.numpy as jnp
import ml_dtypes
import numpy as np
from jax import lax
from jax.experimental import pallas as pl
from jax.experimental.pallas import tpu as pltpu
from jax.sharding import PartitionSpec as P

BF16 = jnp.bfloat16
F32 = jnp.float32
LANES = 128
TAPS = 7
IN_PROD, IN_MIXED, IN_FILT, IN_RIM, IN_ROWS = 0, 4, 8, 10, 12
CROSS_FILT, CROSS_GRAD, CROSS_TOPS, CROSS_ROWS = 0, 2, 4, 5
OUT_LONG, OUT_GRAD, OUT_FILT, OUT_RIM, OUT_HEAD, OUT_ROWS = 0, 4, 8, 10, 11, 12
RIM = TAPS - 1
COT_LANE = 12 * RIM
IN_TOP_LANE = 16 * RIM
TOP_LANE = 12 * RIM
REACH = 125.0
TABLES = 7
CHUNK = 16


def halves(array):
    array = np.asarray(array, np.float32)
    high = array.astype(ml_dtypes.bfloat16)
    low = (array - high.astype(np.float32)).astype(ml_dtypes.bfloat16)
    return high, low


@functools.lru_cache(maxsize=None)
def tables(pieces, length, scale):
    blocks = 2 * pieces
    total = blocks * length
    freq = np.arange(blocks)[:, None]
    angle = 2.0 * np.pi * ((freq * np.arange(pieces)[None, :]) % blocks) / blocks
    cos, sin = np.cos(angle), np.sin(angle)
    outer = np.block([[cos, sin], [-sin, cos]])
    back = np.block([[cos.T, sin.T], [sin.T, -cos.T]]) * (scale / total)
    angle = 2.0 * np.pi * ((freq * np.arange(length)[None, :]) % total) / total
    twiddle = np.stack([np.cos(angle), -np.sin(angle)]).astype(np.float32)
    angle = 2.0 * np.pi * np.arange(length // 2) / length
    middle = np.zeros((2, 8, length), np.float32)
    middle[:, 0, : length // 2] = np.stack([np.cos(angle), -np.sin(angle)])
    twiddle = np.concatenate([twiddle, middle], axis=1)
    count = np.arange(length // 2)
    angle = 2.0 * np.pi * ((count[:, None] * count[None, :]) % (length // 2)) / (length // 2)
    cos, sin = np.cos(angle), np.sin(angle)
    inner = np.block([[cos, -sin], [sin, cos]])
    return (*halves(outer), *halves(back), twiddle, *halves(inner))


def split(value):
    high = value.astype(BF16)
    return high, (value - high.astype(F32)).astype(BF16)


def product3(left, right):
    left = jnp.concatenate([left[0], left[1], left[0]], axis=1)
    right = jnp.concatenate([right[0], right[0], right[1]], axis=0)
    parts = [
        jnp.dot(left[start : start + LANES], right, preferred_element_type=F32)
        for start in range(0, left.shape[0], LANES)
    ]
    return jnp.concatenate(parts, axis=0)


def encoded(value):
    top = jnp.max(jnp.abs(value), axis=1, keepdims=True)
    top = (jnp.maximum(top, 1e-30) * 1.008).astype(BF16).astype(F32)
    square = jnp.abs(value) * (1.0 / top)
    size = square * lax.rsqrt(jnp.maximum(square, 1e-30))
    code = jnp.exp2(size * (2.0 * REACH) - REACH)
    return jnp.where(value < 0.0, -code, code), top


def decoded(code, top):
    size = (jnp.log2(jnp.abs(code)) + REACH) * (0.5 / REACH)
    value = size * size * top
    return jnp.where(code < 0.0, -value, value)


class Lines:
    def __init__(self, ref, rows):
        self.ref, self.rows = ref, rows
        self.count = ref.shape[0] // rows

    def get(self, row):
        return self.ref[pl.ds(row, self.count, stride=self.rows), :]

    def put(self, row, value):
        self.ref[pl.ds(row, self.count, stride=self.rows), :] = value

    def get_block(self, row):
        return jnp.concatenate([self.get(row), self.get(row + 1)], axis=1)

    def put_block(self, row, value):
        self.put(row, value[:, :LANES])
        self.put(row + 1, value[:, LANES:])


def in_lanes(columns, first, like):
    lane = lax.broadcasted_iota(jnp.int32, like.shape, 1)
    for place, column in enumerate(columns):
        like = jnp.where(lane == first + place, column, like)
    return like


def exchanged(value, member, owners):
    size = value.shape[0] // owners
    step = 1
    while step < owners:
        order = [place ^ step for place in range(owners)]
        swapped = jnp.concatenate([value[k * size : (k + 1) * size] for k in order], axis=0)
        value = jnp.where((member & step) != 0, swapped, value)
        step *= 2
    return value


def rolled(value, lanes):
    lanes %= value.shape[1]
    return pltpu.roll(value, lanes, 1) if lanes else value


def lane_numbers(like):
    return lax.broadcasted_iota(jnp.int32, like.shape, 1)


def put_lanes(target, first, count, value, start=0):
    lane = lane_numbers(target)
    inside = (lane >= first) & (lane < first + count)
    return jnp.where(inside, rolled(value, first - start), target)


def eight_rows(taps):
    return jnp.concatenate([taps, jnp.zeros((8 - TAPS, taps.shape[1]), F32)], axis=0)


def spread_taps(taps):
    rest = eight_rows(taps)
    parts = []
    for _ in range(3):
        parts.append(rest.astype(BF16).astype(F32))
        rest = rest - parts[-1]
    columns = jnp.transpose(jnp.concatenate(parts, axis=0)).astype(BF16)
    shape = (24, TAPS * LANES)
    first = lax.broadcasted_iota(jnp.int32, shape, 0) % 8 * LANES
    lane = lax.broadcasted_iota(jnp.int32, shape, 1)
    chosen = jnp.where((lane >= first) & (lane < first + LANES), 1.0, 0.0).astype(BF16)
    return jnp.dot(columns, chosen, preferred_element_type=F32)


def inner_featured(signal, spread):
    near, far = signal[:, :LANES], signal[:, LANES:]
    lane = lane_numbers(near)
    weight = spread[:, :LANES]
    total_near, total_far = weight * near, weight * far
    for offset in range(1, TAPS):
        weight = spread[:, offset * LANES : (offset + 1) * LANES]
        wrapped = jnp.where(lane >= LANES - offset, near, far)
        total_near = total_near + weight * rolled(near, offset)
        total_far = total_far + weight * rolled(wrapped, offset)
    return jnp.concatenate([total_near, total_far], axis=1)


def own_lanes(taps_ref, skip, group):
    lane = lax.broadcasted_iota(jnp.int32, (8, LANES), 1)
    row = lax.broadcasted_iota(jnp.int32, (8, LANES), 0)
    pieces = LANES // 2
    own = jnp.zeros((8, LANES), F32)
    skips = jnp.broadcast_to(skip, (8, LANES))
    for side in range(2):
        here = lane == group + side * pieces
        value = jnp.sum(jnp.where(here, skips, 0.0), axis=1, keepdims=True)
        first = 2 * RIM * side
        own = jnp.where((row == TAPS) & (lane >= first) & (lane < first + RIM), value, own)
        for stream in range(3):
            value = jnp.sum(
                jnp.where(here, eight_rows(taps_ref[stream]), 0.0), axis=1, keepdims=True
            )
            first = 2 * RIM * (stream * 2 + side)
            own = jnp.where((row < TAPS) & (lane >= first) & (lane < first + RIM), value, own)
    return own


def pack_kernel(owners, *refs):
    sources = refs[: 5 + TABLES]
    out_ref, own_ref, feat_ref, spread_ref, wide_ref, cot_ref = refs[5 + TABLES : 11 + TABLES]
    tables_here = refs[11 + TABLES : 11 + 2 * TABLES]
    scratch, x_ref, filt_ref, w_ref, skip_ref, sems = refs[11 + 2 * TABLES :]
    x_hbm, cot_hbm, filt_hbm, w_hbm, skip_hbm = sources[:5]
    pairs = [(w_hbm, w_ref), (filt_hbm, filt_ref), (skip_hbm, skip_ref)]
    pairs += [(x_hbm.at[stream], x_ref.at[stream]) for stream in (1, 2, 0)]
    pairs += [(cot_hbm, cot_ref)]
    pairs += list(zip(sources[5:], tables_here))
    copies = [
        pltpu.make_async_copy(source, target, sems.at[number])
        for number, (source, target) in enumerate(pairs)
    ]
    for copy in copies:
        copy.start()
    lines = Lines(scratch, IN_ROWS)
    pieces = lines.count
    member = lax.axis_index("ch")
    position = lax.axis_index("ctx")
    owned = pieces // owners
    group = ((position // owned) ^ member) * owned + position % owned
    blank = jnp.zeros((pieces, LANES), F32)
    lane = lane_numbers(blank)
    rims = [blank, blank]

    def inner_part(value):
        return jnp.concatenate(
            [jnp.where(lane < RIM, 0.0, value[:, :LANES]), value[:, LANES:]], axis=1
        )

    copies[0].wait()
    for stream in range(3):
        spread_ref[stream] = spread_taps(w_ref[stream])
    for copy in copies[1:7]:
        copy.wait()
    code, filt_top = encoded(filt_ref[...])
    lines.put_block(IN_FILT, jnp.concatenate([code] * owners, axis=0))
    lines.put(IN_RIM + 1, blank)
    own_ref[...] = own_lanes(w_ref, skip_ref[...], group)
    column = jnp.transpose(jnp.broadcast_to(skip_ref[...], (8, LANES)))[:, 0:1]
    wide_ref[...] = jnp.broadcast_to(column, wide_ref.shape)
    for stream in (1, 2, 0):
        for start in range(0, 2 * pieces, CHUNK):
            rows = slice(start, start + CHUNK)
            signal = x_ref[stream, rows, :].astype(F32)
            feat_ref[stream, rows, :] = inner_featured(signal, spread_ref[stream, rows, :])
        for side in range(2):
            signal = x_ref[stream, side * pieces : (side + 1) * pieces, :].astype(F32)
            ends = jnp.where(lane < RIM, signal[:, :LANES], signal[:, LANES:])
            first = 2 * RIM * (stream * 2 + side)
            rims[side] = put_lanes(rims[side], first, 2 * RIM, ends, LANES - RIM)
    tops = []
    for side in range(2):
        rows = slice(side * pieces, (side + 1) * pieces)
        product = inner_part(feat_ref[1, rows, :] * feat_ref[2, rows, :])
        code, top = encoded(exchanged(product, member, owners))
        lines.put_block(IN_PROD + 2 * side, code)
        tops.append(top)
    for side in range(2):
        rows = slice(side * pieces, (side + 1) * pieces)
        cot = cot_ref[rows, :]
        code, top = encoded(exchanged(inner_part(feat_ref[0, rows, :] * cot), member, owners))
        lines.put_block(IN_MIXED + 2 * side, code)
        tops.append(top)
        high = cot[:, :LANES].astype(BF16).astype(F32)
        both = jnp.where(lane < RIM, high, rolled(cot[:, :LANES] - high, RIM))
        rims[side] = put_lanes(rims[side], COT_LANE + 2 * RIM * side, 2 * RIM, both)
    tops.append(jnp.concatenate([filt_top] * owners, axis=0))
    rim = exchanged(rims[0] + rims[1], member, owners)
    lines.put(IN_RIM, in_lanes(tops, IN_TOP_LANE, rim))
    out_ref[...] = scratch[...].astype(BF16)
    for copy in copies[7:]:
        copy.wait()


def turned(re, im, twiddle):
    turn_re, turn_im = twiddle
    return re * turn_re - im * turn_im, re * turn_im + im * turn_re


def parted(re, im, middle):
    half = re.shape[1] // 2
    even = jnp.concatenate([re[:, :half] + re[:, half:], im[:, :half] + im[:, half:]], axis=1)
    odd = turned(re[:, :half] - re[:, half:], im[:, :half] - im[:, half:], middle)
    return jnp.concatenate([even, jnp.concatenate(odd, axis=1)], axis=0)


def joined(pair, middle):
    count, half = pair.shape[0] // 2, pair.shape[1] // 2
    re, im = pair[:count, :half], pair[:count, half:]
    turn_re, turn_im = turned(pair[count:, :half], pair[count:, half:], middle)
    whole_re = jnp.concatenate([re + turn_re, re - turn_re], axis=1)
    return whole_re, jnp.concatenate([im + turn_im, im - turn_im], axis=1)


def spectrum(columns, twiddle, middle, count):
    re, im = turned(columns[:count], columns[count:], twiddle)
    return parted(re, im, middle)


def upright(spectra, inner, twiddle, middle, count):
    inside = product3(split(spectra), inner)
    columns = []
    for start in range(0, spectra.shape[0], 2 * count):
        re, im = joined(inside[start : start + 2 * count], middle)
        columns.append(jnp.concatenate(turned(re, im, twiddle), axis=0))
    return jnp.concatenate(columns, axis=1)


def halved_lanes(value):
    high = value.astype(BF16).astype(F32)
    lane = lane_numbers(value)
    both = jnp.where(lane % (2 * RIM) < RIM, high, rolled(value - high, RIM))
    return jnp.where(lane < 12 * RIM, both, 0.0)


def forward_kernel(
    r_ref,
    w_ref,
    outer_hi,
    outer_lo,
    back_hi,
    back_lo,
    twiddle_ref,
    inner_hi,
    inner_lo,
    cross_ref,
    spec_ref,
    kept_ref,
    scratch,
    cross_scratch,
):
    scratch[...] = r_ref[...].astype(F32)
    lines = Lines(scratch, IN_ROWS)
    cross = Lines(cross_scratch, CROSS_ROWS)
    pieces = lines.count
    count = 2 * pieces
    length = 2 * LANES
    rim = lines.get(IN_RIM)
    tops = [rim[:, IN_TOP_LANE + place : IN_TOP_LANE + place + 1] for place in range(5)]
    lane = lane_numbers(rim)
    row_number = lax.broadcasted_iota(jnp.int32, rim.shape, 0)
    before = jnp.where(row_number == 0, 0.0, pltpu.roll(rim, 1, 0))
    ends = jnp.where(lane % (2 * RIM) < RIM, before, rim)
    head = jnp.zeros_like(rim)
    for offset in range(TAPS):
        head = head + w_ref[offset : offset + 1, :] * rolled(ends, offset - RIM)
    side_lanes = 2 * RIM
    head_key, head_value = rolled(head, -2 * side_lanes), rolled(head, -4 * side_lanes)
    head_cot = rolled(rim + rolled(rim, -RIM), -COT_LANE)
    head_prod, head_mixed = head_key * head_value, head_cot * head
    for place, array in enumerate((head, head_prod, head_mixed, head_key, head_value, head_cot)):
        kept_ref[place] = array

    def whole(row, top, first):
        value = decoded(lines.get_block(row), top)
        return jnp.concatenate([jnp.where(lane < RIM, first, value[:, :LANES]), value[:, LANES:]], axis=1)

    prod, mixed = [], []
    for side in range(2):
        shift = -side_lanes * side
        prod.append(whole(IN_PROD + 2 * side, tops[side], rolled(head_prod, shift)))
        mixed.append(whole(IN_MIXED + 2 * side, tops[2 + side], rolled(head_mixed, shift)))

    signals = jnp.concatenate(
        [jnp.concatenate(prod, axis=0), jnp.concatenate(mixed, axis=0)], axis=1
    )
    twiddle = (twiddle_ref[0, :count], twiddle_ref[1, :count])
    middle = tuple(twiddle_ref[place, count : count + 1, :LANES] for place in range(2))
    spread = product3((outer_hi[...], outer_lo[...]), split(signals))
    parts = [
        spectrum(spread[:, start : start + length], twiddle, middle, count) for start in (0, length)
    ]
    inner = (inner_hi[...], inner_lo[...])
    spectra = product3(split(jnp.concatenate(parts, axis=0)), inner)
    spec_ref[...] = spectra
    z_re, z_im = spectra[:length, :LANES], spectra[:length, LANES:]
    m_re, m_im = spectra[length:, :LANES], spectra[length:, LANES:]
    tail = jnp.concatenate([z_re * m_re + z_im * m_im, z_im * m_re - z_re * m_im], axis=1)
    columns = upright(tail, inner, twiddle, middle, count)
    partial = product3((back_hi[:pieces, :], back_lo[:pieces, :]), split(columns))
    code, top = encoded(partial)
    cross.put_block(CROSS_GRAD, code)
    cross.put_block(CROSS_FILT, lines.get_block(IN_FILT))
    blank = jnp.zeros((pieces, LANES), F32)
    cross.put(CROSS_TOPS, in_lanes([tops[4], top], 0, blank))
    cross_ref[...] = cross_scratch[...].astype(BF16)


def inverse_kernel(
    cross_ref,
    spec_ref,
    kept_ref,
    w_ref,
    outer_hi,
    outer_lo,
    back_hi,
    back_lo,
    twiddle_ref,
    inner_hi,
    inner_lo,
    out_ref,
    cross_scratch,
    scratch,
):
    cross_scratch[...] = cross_ref[...].astype(F32)
    cross = Lines(cross_scratch, CROSS_ROWS)
    lines = Lines(scratch, OUT_ROWS)
    pieces = lines.count
    count = 2 * pieces
    length = 2 * LANES
    tops = cross.get(CROSS_TOPS)
    filt = decoded(cross.get_block(CROSS_FILT), tops[:, 0:1])
    inner = (inner_hi[...], inner_lo[...])
    twiddle = (twiddle_ref[0, :count], twiddle_ref[1, :count])
    middle = tuple(twiddle_ref[place, count : count + 1, :LANES] for place in range(2))
    spread = product3((outer_hi[:, :pieces], outer_lo[:, :pieces]), split(filt))
    spectra = product3(split(spectrum(spread, twiddle, middle, count)), inner)
    f_re, f_im = spectra[:, :LANES], spectra[:, LANES:]
    z_re, z_im = spec_ref[:length, :LANES], spec_ref[:length, LANES:]
    m_re, m_im = spec_ref[length:, :LANES], spec_ref[length:, LANES:]
    long_pair = jnp.concatenate(
        [z_re * f_re - z_im * f_im, -(z_re * f_im + z_im * f_re)], axis=1
    )
    grad_pair = jnp.concatenate([m_re * f_re + m_im * f_im, m_re * f_im - m_im * f_re], axis=1)
    columns = upright(
        jnp.concatenate([long_pair, grad_pair], axis=0), inner, twiddle, middle, count
    )
    restored = product3((back_hi[...], back_lo[...]), split(columns))
    side_lanes = 2 * RIM
    blank = jnp.zeros((pieces, LANES), F32)
    heads = {OUT_LONG: blank, OUT_GRAD: blank}
    out_tops = []
    for row, columns in ((OUT_LONG, slice(0, length)), (OUT_GRAD, slice(length, 2 * length))):
        for side in range(2):
            value = restored[side * pieces : (side + 1) * pieces, columns]
            code, top = encoded(value)
            lines.put_block(row + 2 * side, code)
            out_tops.append(top)
            heads[row] = put_lanes(heads[row], side_lanes * side, RIM, value[:, :LANES])
    head, prod, mixed, key, value, cot = [kept_ref[place] for place in range(6)]
    skip = w_ref[TAPS : TAPS + 1, :]
    grad_query = cot * (heads[OUT_LONG] + skip * prod)
    grad_product = heads[OUT_GRAD] + skip * mixed
    rim = put_lanes(blank, 0, 2 * side_lanes, grad_query)
    rim = put_lanes(rim, 2 * side_lanes, 2 * side_lanes, grad_product * value)
    rim = put_lanes(rim, 4 * side_lanes, 2 * side_lanes, grad_product * key)
    row_number = lax.broadcasted_iota(jnp.int32, rim.shape, 0)
    rim = jnp.where(row_number == pieces - 1, 0.0, pltpu.roll(rim, pieces - 1, 0))
    lines.put_block(OUT_FILT, cross.get_block(CROSS_GRAD))
    lines.put(OUT_RIM, in_lanes([*out_tops, tops[:, 1:2]], TOP_LANE, halved_lanes(rim)))
    lines.put(OUT_HEAD, halved_lanes(head))
    out_ref[...] = scratch[...].astype(BF16)


def local_kernel(
    owners,
    r_ref,
    feat_ref,
    w_ref,
    skip_ref,
    cot_ref,
    out_ref,
    grad_ref,
    tail_ref,
    scratch,
    out_room,
    grad_room,
    tail_room,
    sems,
):
    member = lax.axis_index("ch")
    scratch[...] = r_ref[...].astype(F32)
    lines = Lines(scratch, OUT_ROWS)
    pieces = lines.count
    copies = []

    def send(source, target):
        copy = pltpu.make_async_copy(source, target, sems.at[len(copies)])
        copy.start()
        copies.append(copy)

    def block(row, top_place):
        return decoded(lines.get_block(row), tops[:, TOP_LANE + top_place : TOP_LANE + top_place + 1])

    tops = lines.get(OUT_RIM)
    rim = exchanged(tops, member, owners)
    rim = rim + pltpu.roll(rim, LANES - RIM, 1)
    head = exchanged(lines.get(OUT_HEAD), member, owners)
    head = head + pltpu.roll(head, LANES - RIM, 1)
    lane = lax.broadcasted_iota(jnp.int32, (pieces, LANES), 1)

    def first_lanes(array, place):
        return rolled(array, -2 * RIM * place)

    partial = block(OUT_FILT, 4)
    owned = pieces // owners
    total = partial[:owned]
    for place in range(1, owners):
        total = total + partial[place * owned : (place + 1) * owned]
    tail_room[...] = total
    send(tail_room, tail_ref)
    lane = lane[:CHUNK]
    for side in range(2):
        long_out = exchanged(block(OUT_LONG + 2 * side, side), member, owners)
        grad_long = exchanged(block(OUT_GRAD + 2 * side, 2 + side), member, owners)
        lefts = [first_lanes(head, stream * 2 + side) for stream in range(3)]
        afters = [first_lanes(rim, stream * 2 + side) for stream in range(3)]
        for start in range(0, pieces, CHUNK):
            part = slice(start, start + CHUNK)
            rows = slice(side * pieces + start, side * pieces + start + CHUNK)
            featured = []
            for stream in range(3):
                inside = feat_ref[stream, rows, :]
                left = jnp.where(lane < RIM, lefts[stream][part], inside[:, :LANES])
                featured.append(jnp.concatenate([left, inside[:, LANES:]], axis=1))
            query, key, value = featured
            cot = cot_ref[rows, :]
            skip = jnp.concatenate([skip_ref[rows, :]] * 2, axis=1)
            mixer = long_out[part] + skip * (key * value)
            out_room[rows, :] = query * mixer
            grad_product = grad_long[part] + skip * (cot * query)
            for stream, grad in enumerate((cot * mixer, grad_product * value, grad_product * key)):
                after = afters[stream][part]
                near, far = grad[:, :LANES], grad[:, LANES:]
                weight = w_ref[stream, rows, :LANES]
                total_near, total_far = weight * near, weight * far
                for offset in range(1, TAPS):
                    weight = w_ref[stream, rows, offset * LANES : (offset + 1) * LANES]
                    wrapped = lane < offset
                    moved = rolled(jnp.where(wrapped, far, near), -offset)
                    total_near = total_near + weight * moved
                    moved = rolled(jnp.where(wrapped, after, far), -offset)
                    total_far = total_far + weight * moved
                grad_room[stream, rows, :LANES] = total_near
                grad_room[stream, rows, LANES:] = total_far
        rows = slice(side * pieces, (side + 1) * pieces)
        send(out_room.at[rows, :], out_ref.at[rows, :])
        for stream in range(3):
            send(grad_room.at[stream, rows, :], grad_ref.at[stream, rows, :])
    for copy in copies:
        copy.wait()


VMEM_SPEC = pl.BlockSpec(memory_space=pltpu.VMEM)
ANY_SPEC = pl.BlockSpec(memory_space=pl.ANY)
HBM_SPEC = pl.BlockSpec(memory_space=pltpu.HBM)


def call(
    kernel, out_shape, operands, scratch=(), specs=None, flops=0, out_spec=VMEM_SPEC, room_mib=24
):
    specs = specs or {}
    return pl.pallas_call(
        kernel,
        out_shape=out_shape,
        in_specs=[specs.get(place, VMEM_SPEC) for place in range(len(operands))],
        out_specs=jax.tree.map(lambda _: out_spec, out_shape),
        scratch_shapes=list(scratch),
        compiler_params=pltpu.CompilerParams(vmem_limit_bytes=room_mib << 20),
        cost_estimate=pl.CostEstimate(flops=flops, bytes_accessed=1 << 20, transcendentals=0),
    )(*operands)


def shards(inputs, short_weight, skip, filters, cotangent):
    pieces = lax.axis_size("ctx")
    owners = lax.axis_size("ch")
    _, channels, length = inputs.shape
    owned = filters.shape[0]
    count = 2 * pieces
    scale = 1.0 / math.sqrt(pieces * length)

    def shape(*dims, dtype=F32):
        return jax.ShapeDtypeStruct(dims, dtype)

    def room(rows):
        return pltpu.VMEM((pieces * rows, LANES), F32)

    def transposed(array):
        rows = array.shape[0] // pieces
        array = lax.all_to_all(array.reshape(pieces, rows // 2, 2, LANES), "ctx", 0, 0)
        return array.reshape(pieces * rows, LANES)

    taps = jnp.transpose(short_weight, (0, 2, 1))
    skip_row = skip[None]
    constants = [jnp.asarray(table) for table in tables(pieces, length, scale)]
    arguments = (inputs, cotangent, filters, taps, skip_row, *constants)
    sent, own, featured, spread, skip_wide, cot, *constants = call(
        functools.partial(pack_kernel, owners),
        (
            shape(pieces * IN_ROWS, LANES, dtype=BF16),
            shape(8, LANES),
            shape(3, channels, length),
            shape(3, channels, TAPS * LANES),
            shape(channels, LANES),
            shape(channels, length),
            *(shape(*table.shape, dtype=table.dtype) for table in constants),
        ),
        [pltpu.with_memory_space_constraint(array, pltpu.HBM) for array in arguments],
        [
            room(IN_ROWS),
            pltpu.VMEM(inputs.shape, BF16),
            pltpu.VMEM(filters.shape, F32),
            pltpu.VMEM(taps.shape, F32),
            pltpu.VMEM(skip_row.shape, F32),
            pltpu.SemaphoreType.DMA((7 + TABLES,)),
        ],
        specs={operand: HBM_SPEC for operand in range(5 + TABLES)},
    )
    received = transposed(sent)
    cross, spectra, kept = call(
        forward_kernel,
        (
            shape(pieces * CROSS_ROWS, LANES, dtype=BF16),
            shape(2 * length, length),
            shape(6, pieces, LANES),
        ),
        (received, own, *constants),
        [room(IN_ROWS), room(CROSS_ROWS)],
        flops=800000000,
    )
    partners = [
        (place * owners + shard, place * owners + (shard ^ (place // owned)))
        for place in range(pieces)
        for shard in range(owners)
    ]
    cross = lax.ppermute(cross, ("ctx", "ch"), partners)
    sent = call(
        inverse_kernel,
        shape(pieces * OUT_ROWS, LANES, dtype=BF16),
        (cross, spectra, kept, own, *constants),
        [room(CROSS_ROWS), room(OUT_ROWS)],
        flops=800000000,
    )
    received = transposed(sent)

    return call(
        functools.partial(local_kernel, owners),
        (shape(channels, length), shape(3, channels, length), shape(owned, length)),
        (received, featured, spread, skip_wide, cot),
        [
            room(OUT_ROWS),
            pltpu.VMEM((channels, length), F32),
            pltpu.VMEM((3, channels, length), F32),
            pltpu.VMEM((owned, length), F32),
            pltpu.SemaphoreType.DMA((9,)),
        ],
        out_spec=ANY_SPEC,
    )


def solution(mesh):
    in_specs = (P(None, "ch", "ctx"), P(None, "ch", None), P("ch"), P("ch", "ctx"), P("ch", "ctx"))
    out_specs = (P("ch", "ctx"), P(None, "ch", "ctx"), P("ch", "ctx"))
    return jax.shard_map(shards, mesh=mesh, in_specs=in_specs, out_specs=out_specs, check_vma=False)
```

```python
import functools
import math

import jax
import jax.numpy as jnp
import ml_dtypes
import numpy as np
from jax import lax
from jax.experimental import pallas as pl
from jax.experimental.pallas import tpu as pltpu
from jax.sharding import PartitionSpec as P

BF16 = jnp.bfloat16
F32 = jnp.float32
LANES = 128
TAPS = 7
IN_PROD, IN_MIXED, IN_FILT, IN_RIM, IN_ROWS = 0, 4, 8, 10, 12
CROSS_FILT, CROSS_GRAD, CROSS_TOPS, CROSS_ROWS = 0, 2, 4, 5
OUT_LONG, OUT_GRAD, OUT_FILT, OUT_RIM, OUT_HEAD, OUT_ROWS = 0, 4, 8, 10, 11, 12
RIM = TAPS - 1
COT_LANE = 12 * RIM
IN_TOP_LANE = 16 * RIM
TOP_LANE = 12 * RIM
REACH = 125.0
IN_FIRST, OUT_FIRST = 36, 36
TABLES = 7
CHUNK = 16


def halves(array):
    array = np.asarray(array, np.float32)
    high = array.astype(ml_dtypes.bfloat16)
    low = (array - high.astype(np.float32)).astype(ml_dtypes.bfloat16)
    return high, low


@functools.lru_cache(maxsize=None)
def tables(pieces, length, scale):
    blocks = 2 * pieces
    total = blocks * length
    freq = np.arange(blocks)[:, None]
    angle = 2.0 * np.pi * ((freq * np.arange(pieces)[None, :]) % blocks) / blocks
    cos, sin = np.cos(angle), np.sin(angle)
    outer = np.block([[cos, sin], [-sin, cos]])
    back = np.block([[cos.T, sin.T], [sin.T, -cos.T]]) * (scale / total)
    angle = 2.0 * np.pi * ((freq * np.arange(length)[None, :]) % total) / total
    twiddle = np.stack([np.cos(angle), -np.sin(angle)]).astype(np.float32)
    angle = 2.0 * np.pi * np.arange(length // 2) / length
    middle = np.zeros((2, 8, length), np.float32)
    middle[:, 0, : length // 2] = np.stack([np.cos(angle), -np.sin(angle)])
    twiddle = np.concatenate([twiddle, middle], axis=1)
    count = np.arange(length // 2)
    angle = 2.0 * np.pi * ((count[:, None] * count[None, :]) % (length // 2)) / (length // 2)
    cos, sin = np.cos(angle), np.sin(angle)
    inner = np.block([[cos, -sin], [sin, cos]])
    return (*halves(outer), *halves(back), twiddle, *halves(inner))


def split(value):
    high = value.astype(BF16)
    return high, (value - high.astype(F32)).astype(BF16)


def product3(left, right):
    left = jnp.concatenate([left[0], left[1], left[0]], axis=1)
    right = jnp.concatenate([right[0], right[0], right[1]], axis=0)
    parts = [
        jnp.dot(left[start : start + LANES], right, preferred_element_type=F32)
        for start in range(0, left.shape[0], LANES)
    ]
    return jnp.concatenate(parts, axis=0)


def encoded(value):
    top = jnp.max(jnp.abs(value), axis=1, keepdims=True)
    top = (jnp.maximum(top, 1e-30) * 1.008).astype(BF16).astype(F32)
    square = jnp.abs(value) * (1.0 / top)
    size = square * lax.rsqrt(jnp.maximum(square, 1e-30))
    code = jnp.exp2(size * (2.0 * REACH) - REACH)
    return jnp.where(value < 0.0, -code, code), top


def decoded(code, top):
    size = (jnp.log2(jnp.abs(code)) + REACH) * (0.5 / REACH)
    value = size * size * top
    return jnp.where(code < 0.0, -value, value)


def turned_rows(value, first):
    first %= value.shape[0]
    return jnp.concatenate([value[first:], value[:first]], axis=0) if first else value


class Lines:
    def __init__(self, ref, rows, first=0):
        self.ref, self.rows = ref, rows
        self.count = ref.shape[0] // rows
        self.first = first % self.count

    def get(self, row):
        value = self.ref[pl.ds(row, self.count, stride=self.rows), :]
        return turned_rows(value, self.count - self.first)

    def put(self, row, value):
        self.ref[pl.ds(row, self.count, stride=self.rows), :] = turned_rows(value, self.first)

    def get_block(self, row):
        return jnp.concatenate([self.get(row), self.get(row + 1)], axis=1)

    def put_block(self, row, value):
        self.put(row, value[:, :LANES])
        self.put(row + 1, value[:, LANES:])


def in_lanes(columns, first, like):
    lane = lax.broadcasted_iota(jnp.int32, like.shape, 1)
    for place, column in enumerate(columns):
        like = jnp.where(lane == first + place, column, like)
    return like


def exchanged(value, member, owners):
    size = value.shape[0] // owners
    step = 1
    while step < owners:
        order = [place ^ step for place in range(owners)]
        swapped = jnp.concatenate([value[k * size : (k + 1) * size] for k in order], axis=0)
        value = jnp.where((member & step) != 0, swapped, value)
        step *= 2
    return value


def rolled(value, lanes):
    lanes %= value.shape[1]
    return pltpu.roll(value, lanes, 1) if lanes else value


def lane_numbers(like):
    return lax.broadcasted_iota(jnp.int32, like.shape, 1)


def put_lanes(target, first, count, value, start=0):
    lane = lane_numbers(target)
    inside = (lane >= first) & (lane < first + count)
    return jnp.where(inside, rolled(value, first - start), target)


def eight_rows(taps):
    return jnp.concatenate([taps, jnp.zeros((8 - TAPS, taps.shape[1]), F32)], axis=0)


def spread_taps(taps):
    rest = eight_rows(taps)
    parts = []
    for _ in range(3):
        parts.append(rest.astype(BF16).astype(F32))
        rest = rest - parts[-1]
    columns = jnp.transpose(jnp.concatenate(parts, axis=0)).astype(BF16)
    shape = (24, TAPS * LANES)
    first = lax.broadcasted_iota(jnp.int32, shape, 0) % 8 * LANES
    lane = lax.broadcasted_iota(jnp.int32, shape, 1)
    chosen = jnp.where((lane >= first) & (lane < first + LANES), 1.0, 0.0).astype(BF16)
    return jnp.dot(columns, chosen, preferred_element_type=F32)


def inner_featured(signal, spread):
    near, far = signal[:, :LANES], signal[:, LANES:]
    lane = lane_numbers(near)
    weight = spread[:, :LANES]
    total_near, total_far = weight * near, weight * far
    for offset in range(1, TAPS):
        weight = spread[:, offset * LANES : (offset + 1) * LANES]
        wrapped = jnp.where(lane >= LANES - offset, near, far)
        total_near = total_near + weight * rolled(near, offset)
        total_far = total_far + weight * rolled(wrapped, offset)
    return jnp.concatenate([total_near, total_far], axis=1)


def own_lanes(taps_ref, skip, group):
    lane = lax.broadcasted_iota(jnp.int32, (8, LANES), 1)
    row = lax.broadcasted_iota(jnp.int32, (8, LANES), 0)
    pieces = LANES // 2
    own = jnp.zeros((8, LANES), F32)
    skips = jnp.broadcast_to(skip, (8, LANES))
    for side in range(2):
        here = lane == group + side * pieces
        value = jnp.sum(jnp.where(here, skips, 0.0), axis=1, keepdims=True)
        first = 2 * RIM * side
        own = jnp.where((row == TAPS) & (lane >= first) & (lane < first + RIM), value, own)
        for stream in range(3):
            value = jnp.sum(
                jnp.where(here, eight_rows(taps_ref[stream]), 0.0), axis=1, keepdims=True
            )
            first = 2 * RIM * (stream * 2 + side)
            own = jnp.where((row < TAPS) & (lane >= first) & (lane < first + RIM), value, own)
    return own


def pack_kernel(owners, *refs):
    sources = refs[: 5 + TABLES]
    out_ref, own_ref, feat_ref, spread_ref, wide_ref, cot_ref = refs[5 + TABLES : 11 + TABLES]
    tables_here = refs[11 + TABLES : 11 + 2 * TABLES]
    scratch, x_ref, filt_ref, w_ref, skip_ref, sems = refs[11 + 2 * TABLES :]
    x_hbm, cot_hbm, filt_hbm, w_hbm, skip_hbm = sources[:5]
    pairs = [(w_hbm, w_ref), (filt_hbm, filt_ref), (skip_hbm, skip_ref)]
    pairs += [(x_hbm.at[stream], x_ref.at[stream]) for stream in (1, 2, 0)]
    pairs += [(cot_hbm, cot_ref)]
    pairs += list(zip(sources[5:], tables_here))
    copies = [
        pltpu.make_async_copy(source, target, sems.at[number])
        for number, (source, target) in enumerate(pairs)
    ]
    for copy in copies:
        copy.start()
    lines = Lines(scratch, IN_ROWS, IN_FIRST)
    pieces = lines.count
    member = lax.axis_index("ch")
    position = lax.axis_index("ctx")
    owned = pieces // owners
    group = ((position // owned) ^ member) * owned + position % owned
    blank = jnp.zeros((pieces, LANES), F32)
    lane = lane_numbers(blank)
    rims = [blank, blank]

    def inner_part(value):
        return jnp.concatenate(
            [jnp.where(lane < RIM, 0.0, value[:, :LANES]), value[:, LANES:]], axis=1
        )

    copies[0].wait()
    for stream in range(3):
        spread_ref[stream] = spread_taps(w_ref[stream])
    for copy in copies[1:7]:
        copy.wait()
    code, filt_top = encoded(filt_ref[...])
    lines.put_block(IN_FILT, jnp.concatenate([code] * owners, axis=0))
    lines.put(IN_RIM + 1, blank)
    own_ref[...] = own_lanes(w_ref, skip_ref[...], group)
    column = jnp.transpose(jnp.broadcast_to(skip_ref[...], (8, LANES)))[:, 0:1]
    wide_ref[...] = jnp.broadcast_to(column, wide_ref.shape)
    for stream in (1, 2, 0):
        for start in range(0, 2 * pieces, CHUNK):
            rows = slice(start, start + CHUNK)
            signal = x_ref[stream, rows, :].astype(F32)
            feat_ref[stream, rows, :] = inner_featured(signal, spread_ref[stream, rows, :])
        for side in range(2):
            signal = x_ref[stream, side * pieces : (side + 1) * pieces, :].astype(F32)
            ends = jnp.where(lane < RIM, signal[:, :LANES], signal[:, LANES:])
            first = 2 * RIM * (stream * 2 + side)
            rims[side] = put_lanes(rims[side], first, 2 * RIM, ends, LANES - RIM)
    tops = []
    for side in range(2):
        rows = slice(side * pieces, (side + 1) * pieces)
        product = inner_part(feat_ref[1, rows, :] * feat_ref[2, rows, :])
        code, top = encoded(exchanged(product, member, owners))
        lines.put_block(IN_PROD + 2 * side, code)
        tops.append(top)
    for side in range(2):
        rows = slice(side * pieces, (side + 1) * pieces)
        cot = cot_ref[rows, :]
        code, top = encoded(exchanged(inner_part(feat_ref[0, rows, :] * cot), member, owners))
        lines.put_block(IN_MIXED + 2 * side, code)
        tops.append(top)
        high = cot[:, :LANES].astype(BF16).astype(F32)
        both = jnp.where(lane < RIM, high, rolled(cot[:, :LANES] - high, RIM))
        rims[side] = put_lanes(rims[side], COT_LANE + 2 * RIM * side, 2 * RIM, both)
    tops.append(jnp.concatenate([filt_top] * owners, axis=0))
    rim = exchanged(rims[0] + rims[1], member, owners)
    lines.put(IN_RIM, in_lanes(tops, IN_TOP_LANE, rim))
    out_ref[...] = scratch[...].astype(BF16)
    for copy in copies[7:]:
        copy.wait()


def turned(re, im, twiddle):
    turn_re, turn_im = twiddle
    return re * turn_re - im * turn_im, re * turn_im + im * turn_re


def parted(re, im, middle):
    half = re.shape[1] // 2
    even = jnp.concatenate([re[:, :half] + re[:, half:], im[:, :half] + im[:, half:]], axis=1)
    odd = turned(re[:, :half] - re[:, half:], im[:, :half] - im[:, half:], middle)
    return jnp.concatenate([even, jnp.concatenate(odd, axis=1)], axis=0)


def joined(pair, middle):
    count, half = pair.shape[0] // 2, pair.shape[1] // 2
    re, im = pair[:count, :half], pair[:count, half:]
    turn_re, turn_im = turned(pair[count:, :half], pair[count:, half:], middle)
    whole_re = jnp.concatenate([re + turn_re, re - turn_re], axis=1)
    return whole_re, jnp.concatenate([im + turn_im, im - turn_im], axis=1)


def spectrum(columns, twiddle, middle, count):
    re, im = turned(columns[:count], columns[count:], twiddle)
    return parted(re, im, middle)


def upright(spectra, inner, twiddle, middle, count):
    inside = product3(split(spectra), inner)
    columns = []
    for start in range(0, spectra.shape[0], 2 * count):
        re, im = joined(inside[start : start + 2 * count], middle)
        columns.append(jnp.concatenate(turned(re, im, twiddle), axis=0))
    return jnp.concatenate(columns, axis=1)


def halved_lanes(value):
    high = value.astype(BF16).astype(F32)
    lane = lane_numbers(value)
    both = jnp.where(lane % (2 * RIM) < RIM, high, rolled(value - high, RIM))
    return jnp.where(lane < 12 * RIM, both, 0.0)


def forward_kernel(
    r_ref,
    w_ref,
    outer_hi,
    outer_lo,
    back_hi,
    back_lo,
    twiddle_ref,
    inner_hi,
    inner_lo,
    cross_ref,
    spec_ref,
    kept_ref,
    scratch,
    cross_scratch,
):
    scratch[...] = r_ref[...].astype(F32)
    lines = Lines(scratch, IN_ROWS, IN_FIRST)
    cross = Lines(cross_scratch, CROSS_ROWS)
    pieces = lines.count
    count = 2 * pieces
    length = 2 * LANES
    rim = lines.get(IN_RIM)
    tops = [rim[:, IN_TOP_LANE + place : IN_TOP_LANE + place + 1] for place in range(5)]
    lane = lane_numbers(rim)
    row_number = lax.broadcasted_iota(jnp.int32, rim.shape, 0)
    before = jnp.where(row_number == 0, 0.0, pltpu.roll(rim, 1, 0))
    ends = jnp.where(lane % (2 * RIM) < RIM, before, rim)
    head = jnp.zeros_like(rim)
    for offset in range(TAPS):
        head = head + w_ref[offset : offset + 1, :] * rolled(ends, offset - RIM)
    side_lanes = 2 * RIM
    head_key, head_value = rolled(head, -2 * side_lanes), rolled(head, -4 * side_lanes)
    head_cot = rolled(rim + rolled(rim, -RIM), -COT_LANE)
    head_prod, head_mixed = head_key * head_value, head_cot * head
    for place, array in enumerate((head, head_prod, head_mixed, head_key, head_value, head_cot)):
        kept_ref[place] = array

    def whole(row, top, first):
        value = decoded(lines.get_block(row), top)
        return jnp.concatenate([jnp.where(lane < RIM, first, value[:, :LANES]), value[:, LANES:]], axis=1)

    prod, mixed = [], []
    for side in range(2):
        shift = -side_lanes * side
        prod.append(whole(IN_PROD + 2 * side, tops[side], rolled(head_prod, shift)))
        mixed.append(whole(IN_MIXED + 2 * side, tops[2 + side], rolled(head_mixed, shift)))

    signals = jnp.concatenate(
        [jnp.concatenate(prod, axis=0), jnp.concatenate(mixed, axis=0)], axis=1
    )
    twiddle = (twiddle_ref[0, :count], twiddle_ref[1, :count])
    middle = tuple(twiddle_ref[place, count : count + 1, :LANES] for place in range(2))
    spread = product3((outer_hi[...], outer_lo[...]), split(signals))
    parts = [
        spectrum(spread[:, start : start + length], twiddle, middle, count) for start in (0, length)
    ]
    inner = (inner_hi[...], inner_lo[...])
    spectra = product3(split(jnp.concatenate(parts, axis=0)), inner)
    spec_ref[...] = spectra
    z_re, z_im = spectra[:length, :LANES], spectra[:length, LANES:]
    m_re, m_im = spectra[length:, :LANES], spectra[length:, LANES:]
    tail = jnp.concatenate([z_re * m_re + z_im * m_im, z_im * m_re - z_re * m_im], axis=1)
    columns = upright(tail, inner, twiddle, middle, count)
    partial = product3((back_hi[:pieces, :], back_lo[:pieces, :]), split(columns))
    code, top = encoded(partial)
    cross.put_block(CROSS_GRAD, code)
    cross.put_block(CROSS_FILT, lines.get_block(IN_FILT))
    blank = jnp.zeros((pieces, LANES), F32)
    cross.put(CROSS_TOPS, in_lanes([tops[4], top], 0, blank))
    cross_ref[...] = cross_scratch[...].astype(BF16)


def inverse_kernel(
    cross_ref,
    spec_ref,
    kept_ref,
    w_ref,
    outer_hi,
    outer_lo,
    back_hi,
    back_lo,
    twiddle_ref,
    inner_hi,
    inner_lo,
    out_ref,
    cross_scratch,
    scratch,
):
    cross_scratch[...] = cross_ref[...].astype(F32)
    cross = Lines(cross_scratch, CROSS_ROWS)
    lines = Lines(scratch, OUT_ROWS, OUT_FIRST)
    pieces = lines.count
    count = 2 * pieces
    length = 2 * LANES
    tops = cross.get(CROSS_TOPS)
    filt = decoded(cross.get_block(CROSS_FILT), tops[:, 0:1])
    inner = (inner_hi[...], inner_lo[...])
    twiddle = (twiddle_ref[0, :count], twiddle_ref[1, :count])
    middle = tuple(twiddle_ref[place, count : count + 1, :LANES] for place in range(2))
    spread = product3((outer_hi[:, :pieces], outer_lo[:, :pieces]), split(filt))
    spectra = product3(split(spectrum(spread, twiddle, middle, count)), inner)
    f_re, f_im = spectra[:, :LANES], spectra[:, LANES:]
    z_re, z_im = spec_ref[:length, :LANES], spec_ref[:length, LANES:]
    m_re, m_im = spec_ref[length:, :LANES], spec_ref[length:, LANES:]
    long_pair = jnp.concatenate(
        [z_re * f_re - z_im * f_im, -(z_re * f_im + z_im * f_re)], axis=1
    )
    grad_pair = jnp.concatenate([m_re * f_re + m_im * f_im, m_re * f_im - m_im * f_re], axis=1)
    columns = upright(
        jnp.concatenate([long_pair, grad_pair], axis=0), inner, twiddle, middle, count
    )
    restored = product3((back_hi[...], back_lo[...]), split(columns))
    side_lanes = 2 * RIM
    blank = jnp.zeros((pieces, LANES), F32)
    heads = {OUT_LONG: blank, OUT_GRAD: blank}
    out_tops = []
    for row, columns in ((OUT_LONG, slice(0, length)), (OUT_GRAD, slice(length, 2 * length))):
        for side in range(2):
            value = restored[side * pieces : (side + 1) * pieces, columns]
            code, top = encoded(value)
            lines.put_block(row + 2 * side, code)
            out_tops.append(top)
            heads[row] = put_lanes(heads[row], side_lanes * side, RIM, value[:, :LANES])
    head, prod, mixed, key, value, cot = [kept_ref[place] for place in range(6)]
    skip = w_ref[TAPS : TAPS + 1, :]
    grad_query = cot * (heads[OUT_LONG] + skip * prod)
    grad_product = heads[OUT_GRAD] + skip * mixed
    rim = put_lanes(blank, 0, 2 * side_lanes, grad_query)
    rim = put_lanes(rim, 2 * side_lanes, 2 * side_lanes, grad_product * value)
    rim = put_lanes(rim, 4 * side_lanes, 2 * side_lanes, grad_product * key)
    row_number = lax.broadcasted_iota(jnp.int32, rim.shape, 0)
    rim = jnp.where(row_number == pieces - 1, 0.0, pltpu.roll(rim, pieces - 1, 0))
    lines.put_block(OUT_FILT, cross.get_block(CROSS_GRAD))
    lines.put(OUT_RIM, in_lanes([*out_tops, tops[:, 1:2]], TOP_LANE, halved_lanes(rim)))
    lines.put(OUT_HEAD, halved_lanes(head))
    out_ref[...] = scratch[...].astype(BF16)


def local_kernel(
    owners,
    r_ref,
    feat_ref,
    w_ref,
    skip_ref,
    cot_ref,
    out_ref,
    grad_ref,
    tail_ref,
    scratch,
    out_room,
    grad_room,
    tail_room,
    sems,
):
    member = lax.axis_index("ch")
    scratch[...] = r_ref[...].astype(F32)
    lines = Lines(scratch, OUT_ROWS, OUT_FIRST)
    pieces = lines.count
    copies = []

    def send(source, target):
        copy = pltpu.make_async_copy(source, target, sems.at[len(copies)])
        copy.start()
        copies.append(copy)

    def block(row, top_place):
        return decoded(lines.get_block(row), tops[:, TOP_LANE + top_place : TOP_LANE + top_place + 1])

    tops = lines.get(OUT_RIM)
    rim = exchanged(tops, member, owners)
    rim = rim + pltpu.roll(rim, LANES - RIM, 1)
    head = exchanged(lines.get(OUT_HEAD), member, owners)
    head = head + pltpu.roll(head, LANES - RIM, 1)
    lane = lax.broadcasted_iota(jnp.int32, (pieces, LANES), 1)

    def first_lanes(array, place):
        return rolled(array, -2 * RIM * place)

    partial = block(OUT_FILT, 4)
    owned = pieces // owners
    total = partial[:owned]
    for place in range(1, owners):
        total = total + partial[place * owned : (place + 1) * owned]
    tail_room[...] = total
    send(tail_room, tail_ref)
    lane = lane[:CHUNK]
    for side in range(2):
        long_out = exchanged(block(OUT_LONG + 2 * side, side), member, owners)
        grad_long = exchanged(block(OUT_GRAD + 2 * side, 2 + side), member, owners)
        lefts = [first_lanes(head, stream * 2 + side) for stream in range(3)]
        afters = [first_lanes(rim, stream * 2 + side) for stream in range(3)]
        for start in range(0, pieces, CHUNK):
            part = slice(start, start + CHUNK)
            rows = slice(side * pieces + start, side * pieces + start + CHUNK)
            featured = []
            for stream in range(3):
                inside = feat_ref[stream, rows, :]
                left = jnp.where(lane < RIM, lefts[stream][part], inside[:, :LANES])
                featured.append(jnp.concatenate([left, inside[:, LANES:]], axis=1))
            query, key, value = featured
            cot = cot_ref[rows, :]
            skip = jnp.concatenate([skip_ref[rows, :]] * 2, axis=1)
            mixer = long_out[part] + skip * (key * value)
            out_room[rows, :] = query * mixer
            grad_product = grad_long[part] + skip * (cot * query)
            for stream, grad in enumerate((cot * mixer, grad_product * value, grad_product * key)):
                after = afters[stream][part]
                near, far = grad[:, :LANES], grad[:, LANES:]
                weight = w_ref[stream, rows, :LANES]
                total_near, total_far = weight * near, weight * far
                for offset in range(1, TAPS):
                    weight = w_ref[stream, rows, offset * LANES : (offset + 1) * LANES]
                    wrapped = lane < offset
                    moved = rolled(jnp.where(wrapped, far, near), -offset)
                    total_near = total_near + weight * moved
                    moved = rolled(jnp.where(wrapped, after, far), -offset)
                    total_far = total_far + weight * moved
                grad_room[stream, rows, :LANES] = total_near
                grad_room[stream, rows, LANES:] = total_far
        rows = slice(side * pieces, (side + 1) * pieces)
        send(out_room.at[rows, :], out_ref.at[rows, :])
        for stream in range(3):
            send(grad_room.at[stream, rows, :], grad_ref.at[stream, rows, :])
    for copy in copies:
        copy.wait()


VMEM_SPEC = pl.BlockSpec(memory_space=pltpu.VMEM)
ANY_SPEC = pl.BlockSpec(memory_space=pl.ANY)
HBM_SPEC = pl.BlockSpec(memory_space=pltpu.HBM)


def call(
    kernel, out_shape, operands, scratch=(), specs=None, flops=0, out_spec=VMEM_SPEC, room_mib=24
):
    specs = specs or {}
    return pl.pallas_call(
        kernel,
        out_shape=out_shape,
        in_specs=[specs.get(place, VMEM_SPEC) for place in range(len(operands))],
        out_specs=jax.tree.map(lambda _: out_spec, out_shape),
        scratch_shapes=list(scratch),
        compiler_params=pltpu.CompilerParams(vmem_limit_bytes=room_mib << 20),
        cost_estimate=pl.CostEstimate(flops=flops, bytes_accessed=1 << 20, transcendentals=0),
    )(*operands)


def shards(inputs, short_weight, skip, filters, cotangent):
    pieces = lax.axis_size("ctx")
    owners = lax.axis_size("ch")
    _, channels, length = inputs.shape
    owned = filters.shape[0]
    count = 2 * pieces
    scale = 1.0 / math.sqrt(pieces * length)

    def shape(*dims, dtype=F32):
        return jax.ShapeDtypeStruct(dims, dtype)

    def room(rows):
        return pltpu.VMEM((pieces * rows, LANES), F32)

    def transposed(array, first):
        rows = array.shape[0] // pieces
        order = [(place + first) % pieces for place in range(pieces)]
        array = array.reshape(pieces, rows // 2, 2, LANES)
        array = lax.all_to_all(array, "ctx", 0, 0, axis_index_groups=[order])
        return array.reshape(pieces * rows, LANES)

    taps = jnp.transpose(short_weight, (0, 2, 1))
    skip_row = skip[None]
    constants = [jnp.asarray(table) for table in tables(pieces, length, scale)]
    arguments = (inputs, cotangent, filters, taps, skip_row, *constants)
    sent, own, featured, spread, skip_wide, cot, *constants = call(
        functools.partial(pack_kernel, owners),
        (
            shape(pieces * IN_ROWS, LANES, dtype=BF16),
            shape(8, LANES),
            shape(3, channels, length),
            shape(3, channels, TAPS * LANES),
            shape(channels, LANES),
            shape(channels, length),
            *(shape(*table.shape, dtype=table.dtype) for table in constants),
        ),
        [pltpu.with_memory_space_constraint(array, pltpu.HBM) for array in arguments],
        [
            room(IN_ROWS),
            pltpu.VMEM(inputs.shape, BF16),
            pltpu.VMEM(filters.shape, F32),
            pltpu.VMEM(taps.shape, F32),
            pltpu.VMEM(skip_row.shape, F32),
            pltpu.SemaphoreType.DMA((7 + TABLES,)),
        ],
        specs={operand: HBM_SPEC for operand in range(5 + TABLES)},
    )
    received = transposed(sent, IN_FIRST)
    cross, spectra, kept = call(
        forward_kernel,
        (
            shape(pieces * CROSS_ROWS, LANES, dtype=BF16),
            shape(2 * length, length),
            shape(6, pieces, LANES),
        ),
        (received, own, *constants),
        [room(IN_ROWS), room(CROSS_ROWS)],
        flops=800000000,
    )
    partners = [
        (place * owners + shard, place * owners + (shard ^ (place // owned)))
        for place in range(pieces)
        for shard in range(owners)
    ]
    cross = lax.ppermute(cross, ("ctx", "ch"), partners)
    sent = call(
        inverse_kernel,
        shape(pieces * OUT_ROWS, LANES, dtype=BF16),
        (cross, spectra, kept, own, *constants),
        [room(CROSS_ROWS), room(OUT_ROWS)],
        flops=800000000,
    )
    received = transposed(sent, OUT_FIRST)

    return call(
        functools.partial(local_kernel, owners),
        (shape(channels, length), shape(3, channels, length), shape(owned, length)),
        (received, featured, spread, skip_wide, cot),
        [
            room(OUT_ROWS),
            pltpu.VMEM((channels, length), F32),
            pltpu.VMEM((3, channels, length), F32),
            pltpu.VMEM((owned, length), F32),
            pltpu.SemaphoreType.DMA((9,)),
        ],
        out_spec=ANY_SPEC,
    )


def solution(mesh):
    in_specs = (P(None, "ch", "ctx"), P(None, "ch", None), P("ch"), P("ch", "ctx"), P("ch", "ctx"))
    out_specs = (P("ch", "ctx"), P(None, "ch", "ctx"), P("ch", "ctx"))
    return jax.shard_map(shards, mesh=mesh, in_specs=in_specs, out_specs=out_specs, check_vma=False)
```

```python
import functools
import math

import jax
import jax.numpy as jnp
import ml_dtypes
import numpy as np
from jax import lax
from jax.experimental import pallas as pl
from jax.experimental.pallas import tpu as pltpu
from jax.sharding import PartitionSpec as P

BF16 = jnp.bfloat16
F32 = jnp.float32
LANES = 128
TAPS = 7
IN_PROD, IN_MIXED, IN_FILT, IN_RIM, IN_ROWS = 0, 4, 8, 10, 12
CROSS_FILT, CROSS_GRAD, CROSS_TOPS, CROSS_ROWS = 0, 2, 4, 5
OUT_LONG, OUT_GRAD, OUT_FILT, OUT_RIM, OUT_HEAD, OUT_ROWS = 0, 4, 8, 10, 11, 12
RIM = TAPS - 1
COT_LANE = 12 * RIM
IN_TOP_LANE = 16 * RIM
TOP_LANE = 12 * RIM
REACH = 125.0
IN_FIRST, OUT_FIRST = 44, 44
TABLES = 7
CHUNK = 16


def halves(array):
    array = np.asarray(array, np.float32)
    high = array.astype(ml_dtypes.bfloat16)
    low = (array - high.astype(np.float32)).astype(ml_dtypes.bfloat16)
    return high, low


@functools.lru_cache(maxsize=None)
def tables(pieces, length, scale):
    blocks = 2 * pieces
    total = blocks * length
    freq = np.arange(blocks)[:, None]
    angle = 2.0 * np.pi * ((freq * np.arange(pieces)[None, :]) % blocks) / blocks
    cos, sin = np.cos(angle), np.sin(angle)
    outer = np.block([[cos, sin], [-sin, cos]])
    back = np.block([[cos.T, sin.T], [sin.T, -cos.T]]) * (scale / total)
    angle = 2.0 * np.pi * ((freq * np.arange(length)[None, :]) % total) / total
    twiddle = np.stack([np.cos(angle), -np.sin(angle)]).astype(np.float32)
    angle = 2.0 * np.pi * np.arange(length // 2) / length
    middle = np.zeros((2, 8, length), np.float32)
    middle[:, 0, : length // 2] = np.stack([np.cos(angle), -np.sin(angle)])
    twiddle = np.concatenate([twiddle, middle], axis=1)
    count = np.arange(length // 2)
    angle = 2.0 * np.pi * ((count[:, None] * count[None, :]) % (length // 2)) / (length // 2)
    cos, sin = np.cos(angle), np.sin(angle)
    inner = np.block([[cos, -sin], [sin, cos]])
    return (*halves(outer), *halves(back), twiddle, *halves(inner))


def split(value):
    high = value.astype(BF16)
    return high, (value - high.astype(F32)).astype(BF16)


def product3(left, right):
    left = jnp.concatenate([left[0], left[1], left[0]], axis=1)
    right = jnp.concatenate([right[0], right[0], right[1]], axis=0)
    parts = [
        jnp.dot(left[start : start + LANES], right, preferred_element_type=F32)
        for start in range(0, left.shape[0], LANES)
    ]
    return jnp.concatenate(parts, axis=0)


def encoded(value):
    top = jnp.max(jnp.abs(value), axis=1, keepdims=True)
    top = (jnp.maximum(top, 1e-30) * 1.008).astype(BF16).astype(F32)
    square = jnp.abs(value) * (1.0 / top)
    size = square * lax.rsqrt(jnp.maximum(square, 1e-30))
    code = jnp.exp2(size * (2.0 * REACH) - REACH)
    return jnp.where(value < 0.0, -code, code), top


def decoded(code, top):
    size = (jnp.log2(jnp.abs(code)) + REACH) * (0.5 / REACH)
    value = size * size * top
    return jnp.where(code < 0.0, -value, value)


def turned_rows(value, first):
    first %= value.shape[0]
    return jnp.concatenate([value[first:], value[:first]], axis=0) if first else value


class Lines:
    def __init__(self, ref, rows, first=0):
        self.ref, self.rows = ref, rows
        self.count = ref.shape[0] // rows
        self.first = first % self.count

    def get(self, row):
        value = self.ref[pl.ds(row, self.count, stride=self.rows), :]
        return turned_rows(value, self.count - self.first)

    def put(self, row, value):
        self.ref[pl.ds(row, self.count, stride=self.rows), :] = turned_rows(value, self.first)

    def get_block(self, row):
        return jnp.concatenate([self.get(row), self.get(row + 1)], axis=1)

    def put_block(self, row, value):
        self.put(row, value[:, :LANES])
        self.put(row + 1, value[:, LANES:])


def in_lanes(columns, first, like):
    lane = lax.broadcasted_iota(jnp.int32, like.shape, 1)
    for place, column in enumerate(columns):
        like = jnp.where(lane == first + place, column, like)
    return like


def exchanged(value, member, owners):
    size = value.shape[0] // owners
    step = 1
    while step < owners:
        order = [place ^ step for place in range(owners)]
        swapped = jnp.concatenate([value[k * size : (k + 1) * size] for k in order], axis=0)
        value = jnp.where((member & step) != 0, swapped, value)
        step *= 2
    return value


def rolled(value, lanes):
    lanes %= value.shape[1]
    return pltpu.roll(value, lanes, 1) if lanes else value


def lane_numbers(like):
    return lax.broadcasted_iota(jnp.int32, like.shape, 1)


def put_lanes(target, first, count, value, start=0):
    lane = lane_numbers(target)
    inside = (lane >= first) & (lane < first + count)
    return jnp.where(inside, rolled(value, first - start), target)


def eight_rows(taps):
    return jnp.concatenate([taps, jnp.zeros((8 - TAPS, taps.shape[1]), F32)], axis=0)


def spread_taps(taps):
    rest = eight_rows(taps)
    parts = []
    for _ in range(3):
        parts.append(rest.astype(BF16).astype(F32))
        rest = rest - parts[-1]
    columns = jnp.transpose(jnp.concatenate(parts, axis=0)).astype(BF16)
    shape = (24, TAPS * LANES)
    first = lax.broadcasted_iota(jnp.int32, shape, 0) % 8 * LANES
    lane = lax.broadcasted_iota(jnp.int32, shape, 1)
    chosen = jnp.where((lane >= first) & (lane < first + LANES), 1.0, 0.0).astype(BF16)
    return jnp.dot(columns, chosen, preferred_element_type=F32)


def inner_featured(signal, spread):
    near, far = signal[:, :LANES], signal[:, LANES:]
    lane = lane_numbers(near)
    weight = spread[:, :LANES]
    total_near, total_far = weight * near, weight * far
    for offset in range(1, TAPS):
        weight = spread[:, offset * LANES : (offset + 1) * LANES]
        wrapped = jnp.where(lane >= LANES - offset, near, far)
        total_near = total_near + weight * rolled(near, offset)
        total_far = total_far + weight * rolled(wrapped, offset)
    return jnp.concatenate([total_near, total_far], axis=1)


def own_lanes(taps_ref, skip, group):
    lane = lax.broadcasted_iota(jnp.int32, (8, LANES), 1)
    row = lax.broadcasted_iota(jnp.int32, (8, LANES), 0)
    pieces = LANES // 2
    own = jnp.zeros((8, LANES), F32)
    skips = jnp.broadcast_to(skip, (8, LANES))
    for side in range(2):
        here = lane == group + side * pieces
        value = jnp.sum(jnp.where(here, skips, 0.0), axis=1, keepdims=True)
        first = 2 * RIM * side
        own = jnp.where((row == TAPS) & (lane >= first) & (lane < first + RIM), value, own)
        for stream in range(3):
            value = jnp.sum(
                jnp.where(here, eight_rows(taps_ref[stream]), 0.0), axis=1, keepdims=True
            )
            first = 2 * RIM * (stream * 2 + side)
            own = jnp.where((row < TAPS) & (lane >= first) & (lane < first + RIM), value, own)
    return own


def pack_kernel(owners, *refs):
    sources = refs[: 5 + TABLES]
    out_ref, own_ref, feat_ref, spread_ref, wide_ref, cot_ref = refs[5 + TABLES : 11 + TABLES]
    tables_here = refs[11 + TABLES : 11 + 2 * TABLES]
    scratch, x_ref, filt_ref, w_ref, skip_ref, sems = refs[11 + 2 * TABLES :]
    x_hbm, cot_hbm, filt_hbm, w_hbm, skip_hbm = sources[:5]
    pairs = [(w_hbm, w_ref), (filt_hbm, filt_ref), (skip_hbm, skip_ref)]
    pairs += [(x_hbm.at[stream], x_ref.at[stream]) for stream in (1, 2, 0)]
    pairs += [(cot_hbm, cot_ref)]
    pairs += list(zip(sources[5:], tables_here))
    copies = [
        pltpu.make_async_copy(source, target, sems.at[number])
        for number, (source, target) in enumerate(pairs)
    ]
    for copy in copies:
        copy.start()
    lines = Lines(scratch, IN_ROWS, IN_FIRST)
    pieces = lines.count
    member = lax.axis_index("ch")
    position = lax.axis_index("ctx")
    owned = pieces // owners
    group = ((position // owned) ^ member) * owned + position % owned
    blank = jnp.zeros((pieces, LANES), F32)
    lane = lane_numbers(blank)
    rims = [blank, blank]

    def inner_part(value):
        return jnp.concatenate(
            [jnp.where(lane < RIM, 0.0, value[:, :LANES]), value[:, LANES:]], axis=1
        )

    copies[0].wait()
    for stream in range(3):
        spread_ref[stream] = spread_taps(w_ref[stream])
    for copy in copies[1:7]:
        copy.wait()
    code, filt_top = encoded(filt_ref[...])
    lines.put_block(IN_FILT, jnp.concatenate([code] * owners, axis=0))
    lines.put(IN_RIM + 1, blank)
    own_ref[...] = own_lanes(w_ref, skip_ref[...], group)
    column = jnp.transpose(jnp.broadcast_to(skip_ref[...], (8, LANES)))[:, 0:1]
    wide_ref[...] = jnp.broadcast_to(column, wide_ref.shape)
    for stream in (1, 2, 0):
        for start in range(0, 2 * pieces, CHUNK):
            rows = slice(start, start + CHUNK)
            signal = x_ref[stream, rows, :].astype(F32)
            feat_ref[stream, rows, :] = inner_featured(signal, spread_ref[stream, rows, :])
        for side in range(2):
            signal = x_ref[stream, side * pieces : (side + 1) * pieces, :].astype(F32)
            ends = jnp.where(lane < RIM, signal[:, :LANES], signal[:, LANES:])
            first = 2 * RIM * (stream * 2 + side)
            rims[side] = put_lanes(rims[side], first, 2 * RIM, ends, LANES - RIM)
    tops = []
    for side in range(2):
        rows = slice(side * pieces, (side + 1) * pieces)
        product = inner_part(feat_ref[1, rows, :] * feat_ref[2, rows, :])
        code, top = encoded(exchanged(product, member, owners))
        lines.put_block(IN_PROD + 2 * side, code)
        tops.append(top)
    for side in range(2):
        rows = slice(side * pieces, (side + 1) * pieces)
        cot = cot_ref[rows, :]
        code, top = encoded(exchanged(inner_part(feat_ref[0, rows, :] * cot), member, owners))
        lines.put_block(IN_MIXED + 2 * side, code)
        tops.append(top)
        high = cot[:, :LANES].astype(BF16).astype(F32)
        both = jnp.where(lane < RIM, high, rolled(cot[:, :LANES] - high, RIM))
        rims[side] = put_lanes(rims[side], COT_LANE + 2 * RIM * side, 2 * RIM, both)
    tops.append(jnp.concatenate([filt_top] * owners, axis=0))
    rim = exchanged(rims[0] + rims[1], member, owners)
    lines.put(IN_RIM, in_lanes(tops, IN_TOP_LANE, rim))
    out_ref[...] = scratch[...].astype(BF16)
    for copy in copies[7:]:
        copy.wait()


def turned(re, im, twiddle):
    turn_re, turn_im = twiddle
    return re * turn_re - im * turn_im, re * turn_im + im * turn_re


def parted(re, im, middle):
    half = re.shape[1] // 2
    even = jnp.concatenate([re[:, :half] + re[:, half:], im[:, :half] + im[:, half:]], axis=1)
    odd = turned(re[:, :half] - re[:, half:], im[:, :half] - im[:, half:], middle)
    return jnp.concatenate([even, jnp.concatenate(odd, axis=1)], axis=0)


def joined(pair, middle):
    count, half = pair.shape[0] // 2, pair.shape[1] // 2
    re, im = pair[:count, :half], pair[:count, half:]
    turn_re, turn_im = turned(pair[count:, :half], pair[count:, half:], middle)
    whole_re = jnp.concatenate([re + turn_re, re - turn_re], axis=1)
    return whole_re, jnp.concatenate([im + turn_im, im - turn_im], axis=1)


def spectrum(columns, twiddle, middle, count):
    re, im = turned(columns[:count], columns[count:], twiddle)
    return parted(re, im, middle)


def upright(spectra, inner, twiddle, middle, count):
    inside = product3(split(spectra), inner)
    columns = []
    for start in range(0, spectra.shape[0], 2 * count):
        re, im = joined(inside[start : start + 2 * count], middle)
        columns.append(jnp.concatenate(turned(re, im, twiddle), axis=0))
    return jnp.concatenate(columns, axis=1)


def halved_lanes(value):
    high = value.astype(BF16).astype(F32)
    lane = lane_numbers(value)
    both = jnp.where(lane % (2 * RIM) < RIM, high, rolled(value - high, RIM))
    return jnp.where(lane < 12 * RIM, both, 0.0)


def forward_kernel(
    r_ref,
    w_ref,
    outer_hi,
    outer_lo,
    back_hi,
    back_lo,
    twiddle_ref,
    inner_hi,
    inner_lo,
    cross_ref,
    spec_ref,
    kept_ref,
    scratch,
    cross_scratch,
):
    scratch[...] = r_ref[...].astype(F32)
    lines = Lines(scratch, IN_ROWS, IN_FIRST)
    cross = Lines(cross_scratch, CROSS_ROWS)
    pieces = lines.count
    count = 2 * pieces
    length = 2 * LANES
    rim = lines.get(IN_RIM)
    tops = [rim[:, IN_TOP_LANE + place : IN_TOP_LANE + place + 1] for place in range(5)]
    lane = lane_numbers(rim)
    row_number = lax.broadcasted_iota(jnp.int32, rim.shape, 0)
    before = jnp.where(row_number == 0, 0.0, pltpu.roll(rim, 1, 0))
    ends = jnp.where(lane % (2 * RIM) < RIM, before, rim)
    head = jnp.zeros_like(rim)
    for offset in range(TAPS):
        head = head + w_ref[offset : offset + 1, :] * rolled(ends, offset - RIM)
    side_lanes = 2 * RIM
    head_key, head_value = rolled(head, -2 * side_lanes), rolled(head, -4 * side_lanes)
    head_cot = rolled(rim + rolled(rim, -RIM), -COT_LANE)
    head_prod, head_mixed = head_key * head_value, head_cot * head
    for place, array in enumerate((head, head_prod, head_mixed, head_key, head_value, head_cot)):
        kept_ref[place] = array

    def whole(row, top, first):
        value = decoded(lines.get_block(row), top)
        return jnp.concatenate([jnp.where(lane < RIM, first, value[:, :LANES]), value[:, LANES:]], axis=1)

    prod, mixed = [], []
    for side in range(2):
        shift = -side_lanes * side
        prod.append(whole(IN_PROD + 2 * side, tops[side], rolled(head_prod, shift)))
        mixed.append(whole(IN_MIXED + 2 * side, tops[2 + side], rolled(head_mixed, shift)))

    signals = jnp.concatenate(
        [jnp.concatenate(prod, axis=0), jnp.concatenate(mixed, axis=0)], axis=1
    )
    twiddle = (twiddle_ref[0, :count], twiddle_ref[1, :count])
    middle = tuple(twiddle_ref[place, count : count + 1, :LANES] for place in range(2))
    spread = product3((outer_hi[...], outer_lo[...]), split(signals))
    parts = [
        spectrum(spread[:, start : start + length], twiddle, middle, count) for start in (0, length)
    ]
    inner = (inner_hi[...], inner_lo[...])
    spectra = product3(split(jnp.concatenate(parts, axis=0)), inner)
    spec_ref[...] = spectra
    z_re, z_im = spectra[:length, :LANES], spectra[:length, LANES:]
    m_re, m_im = spectra[length:, :LANES], spectra[length:, LANES:]
    tail = jnp.concatenate([z_re * m_re + z_im * m_im, z_im * m_re - z_re * m_im], axis=1)
    columns = upright(tail, inner, twiddle, middle, count)
    partial = product3((back_hi[:pieces, :], back_lo[:pieces, :]), split(columns))
    code, top = encoded(partial)
    cross.put_block(CROSS_GRAD, code)
    cross.put_block(CROSS_FILT, lines.get_block(IN_FILT))
    blank = jnp.zeros((pieces, LANES), F32)
    cross.put(CROSS_TOPS, in_lanes([tops[4], top], 0, blank))
    cross_ref[...] = cross_scratch[...].astype(BF16)


def inverse_kernel(
    cross_ref,
    spec_ref,
    kept_ref,
    w_ref,
    outer_hi,
    outer_lo,
    back_hi,
    back_lo,
    twiddle_ref,
    inner_hi,
    inner_lo,
    out_ref,
    cross_scratch,
    scratch,
):
    cross_scratch[...] = cross_ref[...].astype(F32)
    cross = Lines(cross_scratch, CROSS_ROWS)
    lines = Lines(scratch, OUT_ROWS, OUT_FIRST)
    pieces = lines.count
    count = 2 * pieces
    length = 2 * LANES
    tops = cross.get(CROSS_TOPS)
    filt = decoded(cross.get_block(CROSS_FILT), tops[:, 0:1])
    inner = (inner_hi[...], inner_lo[...])
    twiddle = (twiddle_ref[0, :count], twiddle_ref[1, :count])
    middle = tuple(twiddle_ref[place, count : count + 1, :LANES] for place in range(2))
    spread = product3((outer_hi[:, :pieces], outer_lo[:, :pieces]), split(filt))
    spectra = product3(split(spectrum(spread, twiddle, middle, count)), inner)
    f_re, f_im = spectra[:, :LANES], spectra[:, LANES:]
    z_re, z_im = spec_ref[:length, :LANES], spec_ref[:length, LANES:]
    m_re, m_im = spec_ref[length:, :LANES], spec_ref[length:, LANES:]
    long_pair = jnp.concatenate(
        [z_re * f_re - z_im * f_im, -(z_re * f_im + z_im * f_re)], axis=1
    )
    grad_pair = jnp.concatenate([m_re * f_re + m_im * f_im, m_re * f_im - m_im * f_re], axis=1)
    columns = upright(
        jnp.concatenate([long_pair, grad_pair], axis=0), inner, twiddle, middle, count
    )
    restored = product3((back_hi[...], back_lo[...]), split(columns))
    side_lanes = 2 * RIM
    blank = jnp.zeros((pieces, LANES), F32)
    heads = {OUT_LONG: blank, OUT_GRAD: blank}
    out_tops = []
    for row, columns in ((OUT_LONG, slice(0, length)), (OUT_GRAD, slice(length, 2 * length))):
        for side in range(2):
            value = restored[side * pieces : (side + 1) * pieces, columns]
            code, top = encoded(value)
            lines.put_block(row + 2 * side, code)
            out_tops.append(top)
            heads[row] = put_lanes(heads[row], side_lanes * side, RIM, value[:, :LANES])
    head, prod, mixed, key, value, cot = [kept_ref[place] for place in range(6)]
    skip = w_ref[TAPS : TAPS + 1, :]
    grad_query = cot * (heads[OUT_LONG] + skip * prod)
    grad_product = heads[OUT_GRAD] + skip * mixed
    rim = put_lanes(blank, 0, 2 * side_lanes, grad_query)
    rim = put_lanes(rim, 2 * side_lanes, 2 * side_lanes, grad_product * value)
    rim = put_lanes(rim, 4 * side_lanes, 2 * side_lanes, grad_product * key)
    row_number = lax.broadcasted_iota(jnp.int32, rim.shape, 0)
    rim = jnp.where(row_number == pieces - 1, 0.0, pltpu.roll(rim, pieces - 1, 0))
    lines.put_block(OUT_FILT, cross.get_block(CROSS_GRAD))
    lines.put(OUT_RIM, in_lanes([*out_tops, tops[:, 1:2]], TOP_LANE, halved_lanes(rim)))
    lines.put(OUT_HEAD, halved_lanes(head))
    out_ref[...] = scratch[...].astype(BF16)


def local_kernel(
    owners,
    r_ref,
    feat_ref,
    w_ref,
    skip_ref,
    cot_ref,
    out_ref,
    grad_ref,
    tail_ref,
    scratch,
    out_room,
    grad_room,
    tail_room,
    sems,
):
    member = lax.axis_index("ch")
    scratch[...] = r_ref[...].astype(F32)
    lines = Lines(scratch, OUT_ROWS, OUT_FIRST)
    pieces = lines.count
    copies = []

    def send(source, target):
        copy = pltpu.make_async_copy(source, target, sems.at[len(copies)])
        copy.start()
        copies.append(copy)

    def block(row, top_place):
        return decoded(lines.get_block(row), tops[:, TOP_LANE + top_place : TOP_LANE + top_place + 1])

    tops = lines.get(OUT_RIM)
    rim = exchanged(tops, member, owners)
    rim = rim + pltpu.roll(rim, LANES - RIM, 1)
    head = exchanged(lines.get(OUT_HEAD), member, owners)
    head = head + pltpu.roll(head, LANES - RIM, 1)
    lane = lax.broadcasted_iota(jnp.int32, (pieces, LANES), 1)

    def first_lanes(array, place):
        return rolled(array, -2 * RIM * place)

    partial = block(OUT_FILT, 4)
    owned = pieces // owners
    total = partial[:owned]
    for place in range(1, owners):
        total = total + partial[place * owned : (place + 1) * owned]
    tail_room[...] = total
    send(tail_room, tail_ref)
    lane = lane[:CHUNK]
    for side in range(2):
        long_out = exchanged(block(OUT_LONG + 2 * side, side), member, owners)
        grad_long = exchanged(block(OUT_GRAD + 2 * side, 2 + side), member, owners)
        lefts = [first_lanes(head, stream * 2 + side) for stream in range(3)]
        afters = [first_lanes(rim, stream * 2 + side) for stream in range(3)]
        for start in range(0, pieces, CHUNK):
            part = slice(start, start + CHUNK)
            rows = slice(side * pieces + start, side * pieces + start + CHUNK)
            featured = []
            for stream in range(3):
                inside = feat_ref[stream, rows, :]
                left = jnp.where(lane < RIM, lefts[stream][part], inside[:, :LANES])
                featured.append(jnp.concatenate([left, inside[:, LANES:]], axis=1))
            query, key, value = featured
            cot = cot_ref[rows, :]
            skip = jnp.concatenate([skip_ref[rows, :]] * 2, axis=1)
            mixer = long_out[part] + skip * (key * value)
            out_room[rows, :] = query * mixer
            grad_product = grad_long[part] + skip * (cot * query)
            for stream, grad in enumerate((cot * mixer, grad_product * value, grad_product * key)):
                after = afters[stream][part]
                near, far = grad[:, :LANES], grad[:, LANES:]
                weight = w_ref[stream, rows, :LANES]
                total_near, total_far = weight * near, weight * far
                for offset in range(1, TAPS):
                    weight = w_ref[stream, rows, offset * LANES : (offset + 1) * LANES]
                    wrapped = lane < offset
                    moved = rolled(jnp.where(wrapped, far, near), -offset)
                    total_near = total_near + weight * moved
                    moved = rolled(jnp.where(wrapped, after, far), -offset)
                    total_far = total_far + weight * moved
                grad_room[stream, rows, :LANES] = total_near
                grad_room[stream, rows, LANES:] = total_far
        rows = slice(side * pieces, (side + 1) * pieces)
        send(out_room.at[rows, :], out_ref.at[rows, :])
        for stream in range(3):
            send(grad_room.at[stream, rows, :], grad_ref.at[stream, rows, :])
    for copy in copies:
        copy.wait()


VMEM_SPEC = pl.BlockSpec(memory_space=pltpu.VMEM)
ANY_SPEC = pl.BlockSpec(memory_space=pl.ANY)
HBM_SPEC = pl.BlockSpec(memory_space=pltpu.HBM)


def call(
    kernel, out_shape, operands, scratch=(), specs=None, flops=0, out_spec=VMEM_SPEC, room_mib=24
):
    specs = specs or {}
    return pl.pallas_call(
        kernel,
        out_shape=out_shape,
        in_specs=[specs.get(place, VMEM_SPEC) for place in range(len(operands))],
        out_specs=jax.tree.map(lambda _: out_spec, out_shape),
        scratch_shapes=list(scratch),
        compiler_params=pltpu.CompilerParams(vmem_limit_bytes=room_mib << 20),
        cost_estimate=pl.CostEstimate(flops=flops, bytes_accessed=1 << 20, transcendentals=0),
    )(*operands)


def shards(inputs, short_weight, skip, filters, cotangent):
    pieces = lax.axis_size("ctx")
    owners = lax.axis_size("ch")
    _, channels, length = inputs.shape
    owned = filters.shape[0]
    count = 2 * pieces
    scale = 1.0 / math.sqrt(pieces * length)

    def shape(*dims, dtype=F32):
        return jax.ShapeDtypeStruct(dims, dtype)

    def room(rows):
        return pltpu.VMEM((pieces * rows, LANES), F32)

    def transposed(array, first):
        rows = array.shape[0] // pieces
        order = [(place + first) % pieces for place in range(pieces)]
        array = array.reshape(pieces, rows // 2, 2, LANES)
        array = lax.all_to_all(array, "ctx", 0, 0, axis_index_groups=[order])
        return array.reshape(pieces * rows, LANES)

    taps = jnp.transpose(short_weight, (0, 2, 1))
    skip_row = skip[None]
    constants = [jnp.asarray(table) for table in tables(pieces, length, scale)]
    arguments = (inputs, cotangent, filters, taps, skip_row, *constants)
    sent, own, featured, spread, skip_wide, cot, *constants = call(
        functools.partial(pack_kernel, owners),
        (
            shape(pieces * IN_ROWS, LANES, dtype=BF16),
            shape(8, LANES),
            shape(3, channels, length),
            shape(3, channels, TAPS * LANES),
            shape(channels, LANES),
            shape(channels, length),
            *(shape(*table.shape, dtype=table.dtype) for table in constants),
        ),
        [pltpu.with_memory_space_constraint(array, pltpu.HBM) for array in arguments],
        [
            room(IN_ROWS),
            pltpu.VMEM(inputs.shape, BF16),
            pltpu.VMEM(filters.shape, F32),
            pltpu.VMEM(taps.shape, F32),
            pltpu.VMEM(skip_row.shape, F32),
            pltpu.SemaphoreType.DMA((7 + TABLES,)),
        ],
        specs={operand: HBM_SPEC for operand in range(5 + TABLES)},
    )
    received = transposed(sent, IN_FIRST)
    cross, spectra, kept = call(
        forward_kernel,
        (
            shape(pieces * CROSS_ROWS, LANES, dtype=BF16),
            shape(2 * length, length),
            shape(6, pieces, LANES),
        ),
        (received, own, *constants),
        [room(IN_ROWS), room(CROSS_ROWS)],
        flops=800000000,
    )
    partners = [
        (place * owners + shard, place * owners + (shard ^ (place // owned)))
        for place in range(pieces)
        for shard in range(owners)
    ]
    cross = lax.ppermute(cross, ("ctx", "ch"), partners)
    sent = call(
        inverse_kernel,
        shape(pieces * OUT_ROWS, LANES, dtype=BF16),
        (cross, spectra, kept, own, *constants),
        [room(CROSS_ROWS), room(OUT_ROWS)],
        flops=800000000,
    )
    received = transposed(sent, OUT_FIRST)

    return call(
        functools.partial(local_kernel, owners),
        (shape(channels, length), shape(3, channels, length), shape(owned, length)),
        (received, featured, spread, skip_wide, cot),
        [
            room(OUT_ROWS),
            pltpu.VMEM((channels, length), F32),
            pltpu.VMEM((3, channels, length), F32),
            pltpu.VMEM((owned, length), F32),
            pltpu.SemaphoreType.DMA((9,)),
        ],
        out_spec=ANY_SPEC,
    )


def solution(mesh):
    in_specs = (P(None, "ch", "ctx"), P(None, "ch", None), P("ch"), P("ch", "ctx"), P("ch", "ctx"))
    out_specs = (P("ch", "ctx"), P(None, "ch", "ctx"), P("ch", "ctx"))
    return jax.shard_map(shards, mesh=mesh, in_specs=in_specs, out_specs=out_specs, check_vma=False)
```

```python
import functools
import math

import jax
import jax.numpy as jnp
import ml_dtypes
import numpy as np
from jax import lax
from jax.experimental import pallas as pl
from jax.experimental.pallas import tpu as pltpu
from jax.sharding import PartitionSpec as P

BF16 = jnp.bfloat16
F32 = jnp.float32
LANES = 128
TAPS = 7
IN_PROD, IN_MIXED, IN_FILT, IN_RIM, IN_ROWS = 0, 4, 8, 10, 12
CROSS_FILT, CROSS_GRAD, CROSS_TOPS, CROSS_ROWS = 0, 2, 4, 5
OUT_LONG, OUT_GRAD, OUT_FILT, OUT_RIM, OUT_HEAD, OUT_ROWS = 0, 4, 8, 10, 11, 12
RIM = TAPS - 1
COT_LANE = 12 * RIM
IN_TOP_LANE = 16 * RIM
TOP_LANE = 12 * RIM
REACH = 125.0
IN_FIRST, OUT_FIRST = 45, 45
TABLES = 7
CHUNK = 16


def halves(array):
    array = np.asarray(array, np.float32)
    high = array.astype(ml_dtypes.bfloat16)
    low = (array - high.astype(np.float32)).astype(ml_dtypes.bfloat16)
    return high, low


@functools.lru_cache(maxsize=None)
def tables(pieces, length, scale):
    blocks = 2 * pieces
    total = blocks * length
    freq = np.arange(blocks)[:, None]
    angle = 2.0 * np.pi * ((freq * np.arange(pieces)[None, :]) % blocks) / blocks
    cos, sin = np.cos(angle), np.sin(angle)
    outer = np.block([[cos, sin], [-sin, cos]])
    back = np.block([[cos.T, sin.T], [sin.T, -cos.T]]) * (scale / total)
    angle = 2.0 * np.pi * ((freq * np.arange(length)[None, :]) % total) / total
    twiddle = np.stack([np.cos(angle), -np.sin(angle)]).astype(np.float32)
    angle = 2.0 * np.pi * np.arange(length // 2) / length
    middle = np.zeros((2, 8, length), np.float32)
    middle[:, 0, : length // 2] = np.stack([np.cos(angle), -np.sin(angle)])
    twiddle = np.concatenate([twiddle, middle], axis=1)
    count = np.arange(length // 2)
    angle = 2.0 * np.pi * ((count[:, None] * count[None, :]) % (length // 2)) / (length // 2)
    cos, sin = np.cos(angle), np.sin(angle)
    inner = np.block([[cos, -sin], [sin, cos]])
    return (*halves(outer), *halves(back), twiddle, *halves(inner))


def split(value):
    high = value.astype(BF16)
    return high, (value - high.astype(F32)).astype(BF16)


def product3(left, right):
    left = jnp.concatenate([left[0], left[1], left[0]], axis=1)
    right = jnp.concatenate([right[0], right[0], right[1]], axis=0)
    parts = [
        jnp.dot(left[start : start + LANES], right, preferred_element_type=F32)
        for start in range(0, left.shape[0], LANES)
    ]
    return jnp.concatenate(parts, axis=0)


def encoded(value):
    top = jnp.max(jnp.abs(value), axis=1, keepdims=True)
    top = (jnp.maximum(top, 1e-30) * 1.008).astype(BF16).astype(F32)
    square = jnp.abs(value) * (1.0 / top)
    size = square * lax.rsqrt(jnp.maximum(square, 1e-30))
    code = jnp.exp2(size * (2.0 * REACH) - REACH)
    return jnp.where(value < 0.0, -code, code), top


def decoded(code, top):
    size = (jnp.log2(jnp.abs(code)) + REACH) * (0.5 / REACH)
    value = size * size * top
    return jnp.where(code < 0.0, -value, value)


def turned_rows(value, first):
    first %= value.shape[0]
    return jnp.concatenate([value[first:], value[:first]], axis=0) if first else value


class Lines:
    def __init__(self, ref, rows, first=0):
        self.ref, self.rows = ref, rows
        self.count = ref.shape[0] // rows
        self.first = first % self.count

    def get(self, row):
        value = self.ref[pl.ds(row, self.count, stride=self.rows), :]
        return turned_rows(value, self.count - self.first)

    def put(self, row, value):
        self.ref[pl.ds(row, self.count, stride=self.rows), :] = turned_rows(value, self.first)

    def get_block(self, row):
        return jnp.concatenate([self.get(row), self.get(row + 1)], axis=1)

    def put_block(self, row, value):
        self.put(row, value[:, :LANES])
        self.put(row + 1, value[:, LANES:])


def in_lanes(columns, first, like):
    lane = lax.broadcasted_iota(jnp.int32, like.shape, 1)
    for place, column in enumerate(columns):
        like = jnp.where(lane == first + place, column, like)
    return like


def exchanged(value, member, owners):
    size = value.shape[0] // owners
    step = 1
    while step < owners:
        order = [place ^ step for place in range(owners)]
        swapped = jnp.concatenate([value[k * size : (k + 1) * size] for k in order], axis=0)
        value = jnp.where((member & step) != 0, swapped, value)
        step *= 2
    return value


def rolled(value, lanes):
    lanes %= value.shape[1]
    return pltpu.roll(value, lanes, 1) if lanes else value


def lane_numbers(like):
    return lax.broadcasted_iota(jnp.int32, like.shape, 1)


def put_lanes(target, first, count, value, start=0):
    lane = lane_numbers(target)
    inside = (lane >= first) & (lane < first + count)
    return jnp.where(inside, rolled(value, first - start), target)


def eight_rows(taps):
    return jnp.concatenate([taps, jnp.zeros((8 - TAPS, taps.shape[1]), F32)], axis=0)


def spread_taps(taps):
    rest = eight_rows(taps)
    parts = []
    for _ in range(3):
        parts.append(rest.astype(BF16).astype(F32))
        rest = rest - parts[-1]
    columns = jnp.transpose(jnp.concatenate(parts, axis=0)).astype(BF16)
    shape = (24, TAPS * LANES)
    first = lax.broadcasted_iota(jnp.int32, shape, 0) % 8 * LANES
    lane = lax.broadcasted_iota(jnp.int32, shape, 1)
    chosen = jnp.where((lane >= first) & (lane < first + LANES), 1.0, 0.0).astype(BF16)
    return jnp.dot(columns, chosen, preferred_element_type=F32)


def inner_featured(signal, spread):
    near, far = signal[:, :LANES], signal[:, LANES:]
    lane = lane_numbers(near)
    weight = spread[:, :LANES]
    total_near, total_far = weight * near, weight * far
    for offset in range(1, TAPS):
        weight = spread[:, offset * LANES : (offset + 1) * LANES]
        wrapped = jnp.where(lane >= LANES - offset, near, far)
        total_near = total_near + weight * rolled(near, offset)
        total_far = total_far + weight * rolled(wrapped, offset)
    return jnp.concatenate([total_near, total_far], axis=1)


def own_lanes(taps_ref, skip, group):
    lane = lax.broadcasted_iota(jnp.int32, (8, LANES), 1)
    row = lax.broadcasted_iota(jnp.int32, (8, LANES), 0)
    pieces = LANES // 2
    own = jnp.zeros((8, LANES), F32)
    skips = jnp.broadcast_to(skip, (8, LANES))
    for side in range(2):
        here = lane == group + side * pieces
        value = jnp.sum(jnp.where(here, skips, 0.0), axis=1, keepdims=True)
        first = 2 * RIM * side
        own = jnp.where((row == TAPS) & (lane >= first) & (lane < first + RIM), value, own)
        for stream in range(3):
            value = jnp.sum(
                jnp.where(here, eight_rows(taps_ref[stream]), 0.0), axis=1, keepdims=True
            )
            first = 2 * RIM * (stream * 2 + side)
            own = jnp.where((row < TAPS) & (lane >= first) & (lane < first + RIM), value, own)
    return own


def pack_kernel(owners, *refs):
    sources = refs[: 5 + TABLES]
    out_ref, own_ref, feat_ref, spread_ref, wide_ref, cot_ref = refs[5 + TABLES : 11 + TABLES]
    tables_here = refs[11 + TABLES : 11 + 2 * TABLES]
    scratch, x_ref, filt_ref, w_ref, skip_ref, sems = refs[11 + 2 * TABLES :]
    x_hbm, cot_hbm, filt_hbm, w_hbm, skip_hbm = sources[:5]
    pairs = [(w_hbm, w_ref), (filt_hbm, filt_ref), (skip_hbm, skip_ref)]
    pairs += [(x_hbm.at[stream], x_ref.at[stream]) for stream in (1, 2, 0)]
    pairs += [(cot_hbm, cot_ref)]
    pairs += list(zip(sources[5:], tables_here))
    copies = [
        pltpu.make_async_copy(source, target, sems.at[number])
        for number, (source, target) in enumerate(pairs)
    ]
    for copy in copies:
        copy.start()
    lines = Lines(scratch, IN_ROWS, IN_FIRST)
    pieces = lines.count
    member = lax.axis_index("ch")
    position = lax.axis_index("ctx")
    owned = pieces // owners
    group = ((position // owned) ^ member) * owned + position % owned
    blank = jnp.zeros((pieces, LANES), F32)
    lane = lane_numbers(blank)
    rims = [blank, blank]

    def inner_part(value):
        return jnp.concatenate(
            [jnp.where(lane < RIM, 0.0, value[:, :LANES]), value[:, LANES:]], axis=1
        )

    copies[0].wait()
    for stream in range(3):
        spread_ref[stream] = spread_taps(w_ref[stream])
    for copy in copies[1:7]:
        copy.wait()
    code, filt_top = encoded(filt_ref[...])
    lines.put_block(IN_FILT, jnp.concatenate([code] * owners, axis=0))
    lines.put(IN_RIM + 1, blank)
    own_ref[...] = own_lanes(w_ref, skip_ref[...], group)
    column = jnp.transpose(jnp.broadcast_to(skip_ref[...], (8, LANES)))[:, 0:1]
    wide_ref[...] = jnp.broadcast_to(column, wide_ref.shape)
    for stream in (1, 2, 0):
        for start in range(0, 2 * pieces, CHUNK):
            rows = slice(start, start + CHUNK)
            signal = x_ref[stream, rows, :].astype(F32)
            feat_ref[stream, rows, :] = inner_featured(signal, spread_ref[stream, rows, :])
        for side in range(2):
            signal = x_ref[stream, side * pieces : (side + 1) * pieces, :].astype(F32)
            ends = jnp.where(lane < RIM, signal[:, :LANES], signal[:, LANES:])
            first = 2 * RIM * (stream * 2 + side)
            rims[side] = put_lanes(rims[side], first, 2 * RIM, ends, LANES - RIM)
    tops = []
    for side in range(2):
        rows = slice(side * pieces, (side + 1) * pieces)
        product = inner_part(feat_ref[1, rows, :] * feat_ref[2, rows, :])
        code, top = encoded(exchanged(product, member, owners))
        lines.put_block(IN_PROD + 2 * side, code)
        tops.append(top)
    for side in range(2):
        rows = slice(side * pieces, (side + 1) * pieces)
        cot = cot_ref[rows, :]
        code, top = encoded(exchanged(inner_part(feat_ref[0, rows, :] * cot), member, owners))
        lines.put_block(IN_MIXED + 2 * side, code)
        tops.append(top)
        high = cot[:, :LANES].astype(BF16).astype(F32)
        both = jnp.where(lane < RIM, high, rolled(cot[:, :LANES] - high, RIM))
        rims[side] = put_lanes(rims[side], COT_LANE + 2 * RIM * side, 2 * RIM, both)
    tops.append(jnp.concatenate([filt_top] * owners, axis=0))
    rim = exchanged(rims[0] + rims[1], member, owners)
    lines.put(IN_RIM, in_lanes(tops, IN_TOP_LANE, rim))
    out_ref[...] = scratch[...].astype(BF16)
    for copy in copies[7:]:
        copy.wait()


def turned(re, im, twiddle):
    turn_re, turn_im = twiddle
    return re * turn_re - im * turn_im, re * turn_im + im * turn_re


def parted(re, im, middle):
    half = re.shape[1] // 2
    even = jnp.concatenate([re[:, :half] + re[:, half:], im[:, :half] + im[:, half:]], axis=1)
    odd = turned(re[:, :half] - re[:, half:], im[:, :half] - im[:, half:], middle)
    return jnp.concatenate([even, jnp.concatenate(odd, axis=1)], axis=0)


def joined(pair, middle):
    count, half = pair.shape[0] // 2, pair.shape[1] // 2
    re, im = pair[:count, :half], pair[:count, half:]
    turn_re, turn_im = turned(pair[count:, :half], pair[count:, half:], middle)
    whole_re = jnp.concatenate([re + turn_re, re - turn_re], axis=1)
    return whole_re, jnp.concatenate([im + turn_im, im - turn_im], axis=1)


def spectrum(columns, twiddle, middle, count):
    re, im = turned(columns[:count], columns[count:], twiddle)
    return parted(re, im, middle)


def upright(spectra, inner, twiddle, middle, count):
    inside = product3(split(spectra), inner)
    columns = []
    for start in range(0, spectra.shape[0], 2 * count):
        re, im = joined(inside[start : start + 2 * count], middle)
        columns.append(jnp.concatenate(turned(re, im, twiddle), axis=0))
    return jnp.concatenate(columns, axis=1)


def halved_lanes(value):
    high = value.astype(BF16).astype(F32)
    lane = lane_numbers(value)
    both = jnp.where(lane % (2 * RIM) < RIM, high, rolled(value - high, RIM))
    return jnp.where(lane < 12 * RIM, both, 0.0)


def forward_kernel(
    r_ref,
    w_ref,
    outer_hi,
    outer_lo,
    back_hi,
    back_lo,
    twiddle_ref,
    inner_hi,
    inner_lo,
    cross_ref,
    spec_ref,
    kept_ref,
    scratch,
    cross_scratch,
):
    scratch[...] = r_ref[...].astype(F32)
    lines = Lines(scratch, IN_ROWS, IN_FIRST)
    cross = Lines(cross_scratch, CROSS_ROWS)
    pieces = lines.count
    count = 2 * pieces
    length = 2 * LANES
    rim = lines.get(IN_RIM)
    tops = [rim[:, IN_TOP_LANE + place : IN_TOP_LANE + place + 1] for place in range(5)]
    lane = lane_numbers(rim)
    row_number = lax.broadcasted_iota(jnp.int32, rim.shape, 0)
    before = jnp.where(row_number == 0, 0.0, pltpu.roll(rim, 1, 0))
    ends = jnp.where(lane % (2 * RIM) < RIM, before, rim)
    head = jnp.zeros_like(rim)
    for offset in range(TAPS):
        head = head + w_ref[offset : offset + 1, :] * rolled(ends, offset - RIM)
    side_lanes = 2 * RIM
    head_key, head_value = rolled(head, -2 * side_lanes), rolled(head, -4 * side_lanes)
    head_cot = rolled(rim + rolled(rim, -RIM), -COT_LANE)
    head_prod, head_mixed = head_key * head_value, head_cot * head
    for place, array in enumerate((head, head_prod, head_mixed, head_key, head_value, head_cot)):
        kept_ref[place] = array

    def whole(row, top, first):
        value = decoded(lines.get_block(row), top)
        return jnp.concatenate([jnp.where(lane < RIM, first, value[:, :LANES]), value[:, LANES:]], axis=1)

    prod, mixed = [], []
    for side in range(2):
        shift = -side_lanes * side
        prod.append(whole(IN_PROD + 2 * side, tops[side], rolled(head_prod, shift)))
        mixed.append(whole(IN_MIXED + 2 * side, tops[2 + side], rolled(head_mixed, shift)))

    signals = jnp.concatenate(
        [jnp.concatenate(prod, axis=0), jnp.concatenate(mixed, axis=0)], axis=1
    )
    twiddle = (twiddle_ref[0, :count], twiddle_ref[1, :count])
    middle = tuple(twiddle_ref[place, count : count + 1, :LANES] for place in range(2))
    spread = product3((outer_hi[...], outer_lo[...]), split(signals))
    parts = [
        spectrum(spread[:, start : start + length], twiddle, middle, count) for start in (0, length)
    ]
    inner = (inner_hi[...], inner_lo[...])
    spectra = product3(split(jnp.concatenate(parts, axis=0)), inner)
    spec_ref[...] = spectra
    z_re, z_im = spectra[:length, :LANES], spectra[:length, LANES:]
    m_re, m_im = spectra[length:, :LANES], spectra[length:, LANES:]
    tail = jnp.concatenate([z_re * m_re + z_im * m_im, z_im * m_re - z_re * m_im], axis=1)
    columns = upright(tail, inner, twiddle, middle, count)
    partial = product3((back_hi[:pieces, :], back_lo[:pieces, :]), split(columns))
    code, top = encoded(partial)
    cross.put_block(CROSS_GRAD, code)
    cross.put_block(CROSS_FILT, lines.get_block(IN_FILT))
    blank = jnp.zeros((pieces, LANES), F32)
    cross.put(CROSS_TOPS, in_lanes([tops[4], top], 0, blank))
    cross_ref[...] = cross_scratch[...].astype(BF16)


def inverse_kernel(
    cross_ref,
    spec_ref,
    kept_ref,
    w_ref,
    outer_hi,
    outer_lo,
    back_hi,
    back_lo,
    twiddle_ref,
    inner_hi,
    inner_lo,
    out_ref,
    cross_scratch,
    scratch,
):
    cross_scratch[...] = cross_ref[...].astype(F32)
    cross = Lines(cross_scratch, CROSS_ROWS)
    lines = Lines(scratch, OUT_ROWS, OUT_FIRST)
    pieces = lines.count
    count = 2 * pieces
    length = 2 * LANES
    tops = cross.get(CROSS_TOPS)
    filt = decoded(cross.get_block(CROSS_FILT), tops[:, 0:1])
    inner = (inner_hi[...], inner_lo[...])
    twiddle = (twiddle_ref[0, :count], twiddle_ref[1, :count])
    middle = tuple(twiddle_ref[place, count : count + 1, :LANES] for place in range(2))
    spread = product3((outer_hi[:, :pieces], outer_lo[:, :pieces]), split(filt))
    spectra = product3(split(spectrum(spread, twiddle, middle, count)), inner)
    f_re, f_im = spectra[:, :LANES], spectra[:, LANES:]
    z_re, z_im = spec_ref[:length, :LANES], spec_ref[:length, LANES:]
    m_re, m_im = spec_ref[length:, :LANES], spec_ref[length:, LANES:]
    long_pair = jnp.concatenate(
        [z_re * f_re - z_im * f_im, -(z_re * f_im + z_im * f_re)], axis=1
    )
    grad_pair = jnp.concatenate([m_re * f_re + m_im * f_im, m_re * f_im - m_im * f_re], axis=1)
    columns = upright(
        jnp.concatenate([long_pair, grad_pair], axis=0), inner, twiddle, middle, count
    )
    restored = product3((back_hi[...], back_lo[...]), split(columns))
    side_lanes = 2 * RIM
    blank = jnp.zeros((pieces, LANES), F32)
    heads = {OUT_LONG: blank, OUT_GRAD: blank}
    out_tops = []
    for row, columns in ((OUT_LONG, slice(0, length)), (OUT_GRAD, slice(length, 2 * length))):
        for side in range(2):
            value = restored[side * pieces : (side + 1) * pieces, columns]
            code, top = encoded(value)
            lines.put_block(row + 2 * side, code)
            out_tops.append(top)
            heads[row] = put_lanes(heads[row], side_lanes * side, RIM, value[:, :LANES])
    head, prod, mixed, key, value, cot = [kept_ref[place] for place in range(6)]
    skip = w_ref[TAPS : TAPS + 1, :]
    grad_query = cot * (heads[OUT_LONG] + skip * prod)
    grad_product = heads[OUT_GRAD] + skip * mixed
    rim = put_lanes(blank, 0, 2 * side_lanes, grad_query)
    rim = put_lanes(rim, 2 * side_lanes, 2 * side_lanes, grad_product * value)
    rim = put_lanes(rim, 4 * side_lanes, 2 * side_lanes, grad_product * key)
    row_number = lax.broadcasted_iota(jnp.int32, rim.shape, 0)
    rim = jnp.where(row_number == pieces - 1, 0.0, pltpu.roll(rim, pieces - 1, 0))
    lines.put_block(OUT_FILT, cross.get_block(CROSS_GRAD))
    lines.put(OUT_RIM, in_lanes([*out_tops, tops[:, 1:2]], TOP_LANE, halved_lanes(rim)))
    lines.put(OUT_HEAD, halved_lanes(head))
    out_ref[...] = scratch[...].astype(BF16)


def local_kernel(
    owners,
    r_ref,
    feat_ref,
    w_ref,
    skip_ref,
    cot_ref,
    out_ref,
    grad_ref,
    tail_ref,
    scratch,
    out_room,
    grad_room,
    tail_room,
    sems,
):
    member = lax.axis_index("ch")
    scratch[...] = r_ref[...].astype(F32)
    lines = Lines(scratch, OUT_ROWS, OUT_FIRST)
    pieces = lines.count
    copies = []

    def send(source, target):
        copy = pltpu.make_async_copy(source, target, sems.at[len(copies)])
        copy.start()
        copies.append(copy)

    def block(row, top_place):
        return decoded(lines.get_block(row), tops[:, TOP_LANE + top_place : TOP_LANE + top_place + 1])

    tops = lines.get(OUT_RIM)
    rim = exchanged(tops, member, owners)
    rim = rim + pltpu.roll(rim, LANES - RIM, 1)
    head = exchanged(lines.get(OUT_HEAD), member, owners)
    head = head + pltpu.roll(head, LANES - RIM, 1)
    lane = lax.broadcasted_iota(jnp.int32, (pieces, LANES), 1)

    def first_lanes(array, place):
        return rolled(array, -2 * RIM * place)

    partial = block(OUT_FILT, 4)
    owned = pieces // owners
    total = partial[:owned]
    for place in range(1, owners):
        total = total + partial[place * owned : (place + 1) * owned]
    tail_room[...] = total
    send(tail_room, tail_ref)
    lane = lane[:CHUNK]
    for side in range(2):
        long_out = exchanged(block(OUT_LONG + 2 * side, side), member, owners)
        grad_long = exchanged(block(OUT_GRAD + 2 * side, 2 + side), member, owners)
        lefts = [first_lanes(head, stream * 2 + side) for stream in range(3)]
        afters = [first_lanes(rim, stream * 2 + side) for stream in range(3)]
        for start in range(0, pieces, CHUNK):
            part = slice(start, start + CHUNK)
            rows = slice(side * pieces + start, side * pieces + start + CHUNK)
            featured = []
            for stream in range(3):
                inside = feat_ref[stream, rows, :]
                left = jnp.where(lane < RIM, lefts[stream][part], inside[:, :LANES])
                featured.append(jnp.concatenate([left, inside[:, LANES:]], axis=1))
            query, key, value = featured
            cot = cot_ref[rows, :]
            skip = jnp.concatenate([skip_ref[rows, :]] * 2, axis=1)
            mixer = long_out[part] + skip * (key * value)
            out_room[rows, :] = query * mixer
            grad_product = grad_long[part] + skip * (cot * query)
            for stream, grad in enumerate((cot * mixer, grad_product * value, grad_product * key)):
                after = afters[stream][part]
                near, far = grad[:, :LANES], grad[:, LANES:]
                weight = w_ref[stream, rows, :LANES]
                total_near, total_far = weight * near, weight * far
                for offset in range(1, TAPS):
                    weight = w_ref[stream, rows, offset * LANES : (offset + 1) * LANES]
                    wrapped = lane < offset
                    moved = rolled(jnp.where(wrapped, far, near), -offset)
                    total_near = total_near + weight * moved
                    moved = rolled(jnp.where(wrapped, after, far), -offset)
                    total_far = total_far + weight * moved
                grad_room[stream, rows, :LANES] = total_near
                grad_room[stream, rows, LANES:] = total_far
        rows = slice(side * pieces, (side + 1) * pieces)
        send(out_room.at[rows, :], out_ref.at[rows, :])
        for stream in range(3):
            send(grad_room.at[stream, rows, :], grad_ref.at[stream, rows, :])
    for copy in copies:
        copy.wait()


VMEM_SPEC = pl.BlockSpec(memory_space=pltpu.VMEM)
ANY_SPEC = pl.BlockSpec(memory_space=pl.ANY)
HBM_SPEC = pl.BlockSpec(memory_space=pltpu.HBM)


def call(
    kernel, out_shape, operands, scratch=(), specs=None, flops=0, out_spec=VMEM_SPEC, room_mib=24
):
    specs = specs or {}
    return pl.pallas_call(
        kernel,
        out_shape=out_shape,
        in_specs=[specs.get(place, VMEM_SPEC) for place in range(len(operands))],
        out_specs=jax.tree.map(lambda _: out_spec, out_shape),
        scratch_shapes=list(scratch),
        compiler_params=pltpu.CompilerParams(vmem_limit_bytes=room_mib << 20),
        cost_estimate=pl.CostEstimate(flops=flops, bytes_accessed=1 << 20, transcendentals=0),
    )(*operands)


def shards(inputs, short_weight, skip, filters, cotangent):
    pieces = lax.axis_size("ctx")
    owners = lax.axis_size("ch")
    _, channels, length = inputs.shape
    owned = filters.shape[0]
    count = 2 * pieces
    scale = 1.0 / math.sqrt(pieces * length)

    def shape(*dims, dtype=F32):
        return jax.ShapeDtypeStruct(dims, dtype)

    def room(rows):
        return pltpu.VMEM((pieces * rows, LANES), F32)

    def transposed(array, first):
        rows = array.shape[0] // pieces
        order = [(place + first) % pieces for place in range(pieces)]
        array = array.reshape(pieces, rows // 2, 2, LANES)
        array = lax.all_to_all(array, "ctx", 0, 0, axis_index_groups=[order])
        return array.reshape(pieces * rows, LANES)

    taps = jnp.transpose(short_weight, (0, 2, 1))
    skip_row = skip[None]
    constants = [jnp.asarray(table) for table in tables(pieces, length, scale)]
    arguments = (inputs, cotangent, filters, taps, skip_row, *constants)
    sent, own, featured, spread, skip_wide, cot, *constants = call(
        functools.partial(pack_kernel, owners),
        (
            shape(pieces * IN_ROWS, LANES, dtype=BF16),
            shape(8, LANES),
            shape(3, channels, length),
            shape(3, channels, TAPS * LANES),
            shape(channels, LANES),
            shape(channels, length),
            *(shape(*table.shape, dtype=table.dtype) for table in constants),
        ),
        [pltpu.with_memory_space_constraint(array, pltpu.HBM) for array in arguments],
        [
            room(IN_ROWS),
            pltpu.VMEM(inputs.shape, BF16),
            pltpu.VMEM(filters.shape, F32),
            pltpu.VMEM(taps.shape, F32),
            pltpu.VMEM(skip_row.shape, F32),
            pltpu.SemaphoreType.DMA((7 + TABLES,)),
        ],
        specs={operand: HBM_SPEC for operand in range(5 + TABLES)},
    )
    received = transposed(sent, IN_FIRST)
    cross, spectra, kept = call(
        forward_kernel,
        (
            shape(pieces * CROSS_ROWS, LANES, dtype=BF16),
            shape(2 * length, length),
            shape(6, pieces, LANES),
        ),
        (received, own, *constants),
        [room(IN_ROWS), room(CROSS_ROWS)],
        flops=800000000,
    )
    partners = [
        (place * owners + shard, place * owners + (shard ^ (place // owned)))
        for place in range(pieces)
        for shard in range(owners)
    ]
    cross = lax.ppermute(cross, ("ctx", "ch"), partners)
    sent = call(
        inverse_kernel,
        shape(pieces * OUT_ROWS, LANES, dtype=BF16),
        (cross, spectra, kept, own, *constants),
        [room(CROSS_ROWS), room(OUT_ROWS)],
        flops=800000000,
    )
    received = transposed(sent, OUT_FIRST)

    return call(
        functools.partial(local_kernel, owners),
        (shape(channels, length), shape(3, channels, length), shape(owned, length)),
        (received, featured, spread, skip_wide, cot),
        [
            room(OUT_ROWS),
            pltpu.VMEM((channels, length), F32),
            pltpu.VMEM((3, channels, length), F32),
            pltpu.VMEM((owned, length), F32),
            pltpu.SemaphoreType.DMA((9,)),
        ],
        out_spec=ANY_SPEC,
    )


def solution(mesh):
    in_specs = (P(None, "ch", "ctx"), P(None, "ch", None), P("ch"), P("ch", "ctx"), P("ch", "ctx"))
    out_specs = (P("ch", "ctx"), P(None, "ch", "ctx"), P("ch", "ctx"))
    return jax.shard_map(shards, mesh=mesh, in_specs=in_specs, out_specs=out_specs, check_vma=False)
```
